256 devices in a mesh: grp: 2 (over y_hi), sub: 128 (over y_lo, x, z, core).
Axes of the slice: x: 4, y: 4 (y_hi: 2, y_lo: 2; y = y_hi * 2 + y_lo), z: 8, core: 2. Of those that a mesh axis runs over, the one named last changes fastest.
Arguments:
- fluid_state: float32 [5, 64, 262144], P(None, None, ('grp', 'sub')), may hold values from -6 to 6
- flux_jacobian: float32 [3, 5, 5], replicated, may hold values from -1.5 to 1.5
- solid_temp: float32 [256, 256, 256], P(None, 'sub', 'grp'), may hold values from -6 to 6
- iface_elem: int32 [32768], P(('grp', 'sub')), may hold values from 0 to 1023, as said below
- iface_owner: int32 [32768, 1], P(('grp', 'sub')), may hold values from 0 to 127; in each aligned block of 128 rows (0 to 127, 128 to 255, ...) at most 2 rows name the same one
- iface_patch: int32 [32768], P(('grp', 'sub')), may hold values from 0 to 15
Outputs:
- fluid_out: float32 [5, 64, 262144], P(None, None, ('grp', 'sub'))
- solid_out: float32 [256, 256, 256], P(None, 'sub', 'grp')
The draws below stay inside these ranges and needn't reach their ends.
Inputs may be any that keep to these rules, and one draw needn't show every extreme that they name: `iface_elem`: within the 128 entries of one device the elements are distinct. `iface_owner`: among the 128 rows of one device no owner appears more than 2 times; in every draw some owner appears exactly 2 times.
All inputs are finite; a program needn't handle non-finite values.
Results may differ from the reference program's by a relative error of at most 0.0003.
Values sent between devices are 32-bit elements; how exact they have to be, the bound alone decides.
No kernel may reach another device: no remote copies, remote signals or barrier semaphores. Data moves between devices by JAX's collectives and lax.ppermute only.
A program may use at most 64 MiB of HBM per device.

```python
import math
import jax
import jax.numpy as jnp
import numpy as np
from jax import lax

NQ = 64
EF_DEV = 1024
SX_DEV = 2
NY = 256
NZ = 256
IF_DEV = 128
PASSES = 2
EF = 262144
NX = 256
IFACES = 32768
PATCHES = 16
CAP = 2
N_GRP = 2
N_SUB = 128


def draw_iface_elem(key, part):
    key = jax.random.fold_in(key, 7)
    device_keys = jax.random.split(key, N_GRP * N_SUB)
    chosen = jax.vmap(lambda single: jax.random.permutation(single, EF_DEV)[:IF_DEV])(device_keys)
    return chosen.reshape(-1).astype(jnp.int32)


def place_ends(result, rng, low, largest):
    place = [jax.random.randint(jax.random.fold_in(rng, axis), (), 0, length) for axis, length in enumerate(result.shape)]
    longest = result.shape.index(max(result.shape))
    neighbour = place[:longest] + [(place[longest] + 1) % result.shape[longest]] + place[longest + 1:]
    return result.at[tuple(place)].set(low).at[tuple(neighbour)].set(largest)


def steps_of(rng, shape, cuts, least, top_value):
    level = 1.0
    for dim, shards_of in cuts:
        steps = jax.random.uniform(jax.random.fold_in(jax.random.fold_in(rng, 6), dim), (shards_of,), jnp.float32, least / len(cuts), top_value / len(cuts))
        level = level * jnp.repeat(jnp.exp(steps), shape[dim] // shards_of).reshape((-1,) + (1,) * (len(shape) - 1 - dim))
    return level


def routed_block(own_key, own, number, rows, number_of, top, bound, skew):
    ranking = jax.random.permutation(own_key, number_of)
    packed, usual = portions_of(number_of, rows * top, bound, skew, True), portions_of(number_of, rows * top, bound, skew, False)
    places = jnp.arange(number_of)

    def named(lengths, offset_by):
        used = int((lengths > 0).sum())
        fixed = max(1, used // 4)
        passed = fixed + (places - fixed + offset_by * (used - fixed)) % max(1, number_of - fixed)
        return jnp.zeros((number_of,), jnp.int32).at[ranking[jnp.where(places < fixed, places, passed)]].set(jnp.asarray(lengths, jnp.int32))

    lengths = jnp.where(number % 4 == 0, named(packed, number // 4), named(usual, number - number // 4 - 1))
    mixed = jax.random.permutation(jax.random.fold_in(own, 3), number_of)
    donor, taker = mixed[0:number_of // 2 * 2:2], mixed[1:number_of // 2 * 2:2]
    slack = jnp.minimum(lengths[donor] - 1, bound - lengths[taker]) // 2
    slack = jnp.where((donor == ranking[0]) | (taker == ranking[0]) | (lengths[taker] == 0), 0, jnp.maximum(slack, 0))
    passed = jax.random.randint(jax.random.fold_in(own, 4), (number_of // 2,), 0, 1 << 20) % (slack + 1)
    lengths = lengths.at[donor].add(-passed).at[taker].add(passed)
    labels = jnp.searchsorted(jnp.cumsum(lengths), jnp.arange(rows * top), side="right").astype(jnp.int32)
    table = labels.reshape(top, rows).T
    table = table[jax.random.permutation(jax.random.fold_in(own, 1), rows)]
    offset_by = jax.random.randint(jax.random.fold_in(own, 2), (rows, 1), 0, top)
    return jnp.take_along_axis(table, (jnp.arange(top)[None, :] + offset_by) % top, axis=1)


def portions_of(count, total, bound, slope, full):
    loads = [(1 << 20) // math.isqrt(rank ** slope) + 1 for rank in range(1, count + 1)]
    largest = bound if full else min(bound, max(-(-total // count), total * loads[0] // sum(loads)))
    least = 1 if total - largest >= count - 1 else 0
    given, surplus = [largest] + [least] * (count - 1), total - largest - least * (count - 1)
    while surplus > 0:
        free = [i for i in range(1, count) if given[i] < largest] or [i for i in range(1, count) if given[i] < bound]
        mass, left = sum([loads[i] for i in free]), surplus
        for i in free:
            addition = min(bound - given[i], max(1, left * loads[i] // mass), surplus)
            given[i] = given[i] + addition
            surplus = surplus - addition
    return np.array(given)


def centred(key, dims, spread, bound, cuts=(), held_as=jnp.bfloat16):
    values = spread * jax.random.normal(key, dims, jnp.float32)
    if cuts:
        values = values * steps_of(key, dims, cuts, -0.22, 0.18)
    return jnp.clip(values, -bound, bound).astype(held_as)


def setup_inputs(seed: int = 0) -> dict:
    arg_keys = jax.random.split(jax.random.key(seed), 7)
    fluid_state = centred(arg_keys[0], (5, NQ, EF), 1.0, 6.0, ((2, 256),), jnp.float32)
    flux_jacobian = centred(arg_keys[1], (3, 5, 5), 0.3, 1.5, (), jnp.float32)
    solid_temp = centred(arg_keys[2], (NZ, NX, NY), 1.0, 6.0, ((1, 128), (2, 2)), jnp.float32)
    iface_elem = draw_iface_elem(jax.random.fold_in(arg_keys[6], 71), 0)
    iface_owner_keys = jax.random.split(jax.random.fold_in(arg_keys[4], 1), IFACES // IF_DEV)
    iface_owner_turns = jax.random.permutation(jax.random.fold_in(arg_keys[4], 3), IFACES // IF_DEV)
    iface_owner = jax.vmap(lambda own, number: routed_block(jax.random.fold_in(arg_keys[4], 2), own, number, IF_DEV, N_SUB, 1, CAP, 2))(iface_owner_keys, iface_owner_turns).reshape((IFACES, 1))
    iface_patch = place_ends(jax.random.randint(arg_keys[5], (IFACES,), 0, PATCHES), jax.random.fold_in(arg_keys[5], 1), 0, PATCHES - 1).astype(jnp.int32)
    return dict(fluid_state=fluid_state, flux_jacobian=flux_jacobian, solid_temp=solid_temp, iface_elem=iface_elem, iface_owner=iface_owner, iface_patch=iface_patch)


DT = 0.05
LIFT = 6.0
ALPHA = 1.0
VISC = 0.05
HEAT = 1.0
HIGH = lax.Precision.HIGHEST

def lobatto_derivative():
    points = np.array([-1.0, -1.0 / np.sqrt(5.0), 1.0 / np.sqrt(5.0), 1.0])
    weights = np.array([1.0 / np.prod([points[j] - points[k] for k in range(4) if k != j]) for j in range(4)])
    deriv_table = np.zeros((4, 4))
    for i in range(4):
        for j in range(4):
            if i != j:
                deriv_table[i, j] = weights[j] / weights[i] / (points[i] - points[j])
        deriv_table[i, i] = -np.sum(deriv_table[i])
    return deriv_table

def volume_operator(flux_jacobian):
    deriv = jnp.asarray(lobatto_derivative(), jnp.float32)
    identity = jnp.eye(4, dtype=jnp.float32)
    along_x = jnp.kron(identity, jnp.kron(identity, deriv))
    along_y = jnp.kron(identity, jnp.kron(deriv, identity))
    along_z = jnp.kron(deriv, jnp.kron(identity, identity))
    second = jnp.dot(along_x, along_x, precision=HIGH) + jnp.dot(along_y, along_y, precision=HIGH) + jnp.dot(along_z, along_z, precision=HIGH)
    visc_mask = jnp.array([0.0, 1.0, 1.0, 1.0, 1.0], jnp.float32)
    advect = jnp.kron(flux_jacobian[0], along_x) + jnp.kron(flux_jacobian[1], along_y) + jnp.kron(flux_jacobian[2], along_z)
    return -advect + VISC * jnp.kron(jnp.diag(visc_mask), second)

def face_terms(fluid_now, prev_right, next_left, flux_x):
    left_face = fluid_now[:, 0::4, :]
    right_face = fluid_now[:, 3::4, :]

    def mix_fields(values):
        return jnp.einsum('fg,gne->fne', flux_x, values, precision=HIGH)
    flux_right = 0.5 * mix_fields(right_face + next_left) - 0.5 * ALPHA * (next_left - right_face)
    flux_left = 0.5 * mix_fields(prev_right + left_face) - 0.5 * ALPHA * (left_face - prev_right)
    corr_right = -LIFT * (flux_right - mix_fields(right_face))
    corr_left = LIFT * (flux_left - mix_fields(left_face))
    corrections = jnp.zeros_like(fluid_now)
    return corrections.at[:, 0::4, :].set(corr_left).at[:, 3::4, :].set(corr_right)

def fluid_step(fluid_now, operator_matrix, face_flux, source):
    volume = jnp.dot(operator_matrix, fluid_now.reshape(5 * 64, -1), precision=HIGH).reshape(fluid_now.shape)
    updated = fluid_now + DT * (volume + face_flux)
    return updated.at[4, :16, :].add(DT * LIFT * source)

def sine_basis(length):
    numbers = jnp.arange(length, dtype=jnp.int32) + 1
    phases = numbers[:, None] * numbers[None, :] % (2 * (length + 1))
    return jnp.sqrt(2.0 / (length + 1)) * jnp.sin(jnp.pi * phases.astype(jnp.float32) / (length + 1))

def eigen_values(length):
    numbers = jnp.arange(length, dtype=jnp.float32) + 1.0
    return 2.0 - 2.0 * jnp.cos(jnp.pi * numbers / (length + 1))

def solve_slab(slab_rhs):
    diffuse = 16.0 * SX_DEV * SX_DEV
    sine_z = sine_basis(NZ)
    sine_x = sine_basis(NX)
    sine_y = sine_basis(NY)
    denominator = 1.0 + diffuse * (eigen_values(NZ)[:, None, None] + eigen_values(NX)[None, :, None] + eigen_values(NY)[None, None, :])
    spectral = jnp.dot(sine_z, slab_rhs.reshape(NZ, -1), precision=HIGH).reshape(NZ, NX, NY)
    spectral = jnp.einsum('xa,zay->zxy', sine_x, spectral, precision=HIGH)
    spectral = jnp.dot(spectral.reshape(-1, NY), sine_y, precision=HIGH).reshape(NZ, NX, NY)
    spectral = spectral / denominator
    spectral = jnp.dot(spectral.reshape(-1, NY), sine_y, precision=HIGH).reshape(NZ, NX, NY)
    spectral = jnp.einsum('xa,zay->zxy', sine_x, spectral, precision=HIGH)
    return jnp.dot(sine_z, spectral.reshape(NZ, -1), precision=HIGH).reshape(NZ, NX, NY)

def surface_patches(slab_temp):
    half_width = NY // N_GRP
    return slab_temp[0].reshape(N_SUB, SX_DEV, N_GRP, half_width).transpose(2, 0, 1, 3).reshape(N_GRP, N_SUB, PATCHES, 16)

def reference(fluid_state, flux_jacobian, solid_temp, iface_elem, iface_owner, iface_patch):
    operator_matrix = volume_operator(flux_jacobian)
    slot_ids = jnp.arange(IFACES, dtype=jnp.int32)
    elem_global = slot_ids // IF_DEV * EF_DEV + iface_elem
    group_of = slot_ids // (IF_DEV * N_SUB)
    owners = iface_owner[:, 0]
    fluid_now = fluid_state
    slab_temp = solid_temp
    for pass_index in range(PASSES):
        left_face = fluid_now[:, 0::4, :]
        right_face = fluid_now[:, 3::4, :]
        prev_right = jnp.pad(right_face[:, :, :-1], ((0, 0), (0, 0), (1, 0)))
        next_left = jnp.pad(left_face[:, :, 1:], ((0, 0), (0, 0), (0, 1)))
        face_flux = face_terms(fluid_now, prev_right, next_left, flux_jacobian[0])
        traces = (fluid_now[4, :16, :] - fluid_now[0, :16, :])[:, elem_global]
        old_patch = surface_patches(slab_temp)[group_of, owners, iface_patch]
        heat_in = HEAT * (traces.T - old_patch)
        totals = jnp.zeros((N_GRP, N_SUB, PATCHES, 16), jnp.float32).at[group_of, owners, iface_patch].add(heat_in)
        surface_add = totals.reshape(N_GRP, N_SUB, SX_DEV, NY // N_GRP).transpose(1, 2, 0, 3).reshape(NX, NY)
        slab_temp = solve_slab(slab_temp.at[0].add(surface_add))
        new_patch = surface_patches(slab_temp)[group_of, owners, iface_patch]
        source = jnp.zeros((16, EF), jnp.float32).at[:, elem_global].add(HEAT * (new_patch.T - traces))
        fluid_now = fluid_step(fluid_now, operator_matrix, face_flux, source)
    return (fluid_now, slab_temp)
```

```python
import jax
import jax.numpy as jnp
import numpy as np
from jax import lax
from jax.sharding import Mesh, PartitionSpec as P

ALL = ("g", "yl", "x", "z", "c")
SUB = ("yl", "x", "z", "c")
SAME_CORE = ("g", "yl", "x", "z")
N = 256
HALF = 128
DT = 0.05
VISC = 0.05
GAIN = 0.3
HIGH = lax.Precision.HIGH
F32 = jnp.float32


def sine_table(length):
    numbers = np.arange(length) + 1
    phases = numbers[:, None] * numbers[None, :] % (2 * (length + 1))
    return np.sqrt(2.0 / (length + 1)) * np.sin(np.pi * phases / (length + 1))


def rates(length):
    return 2.0 - 2.0 * np.cos(np.pi * (np.arange(length) + 1) / (length + 1))


SINE = sine_table(N)
RATES = rates(N)
MODE_ORDER = np.array([2 * q + k for k in range(2) for q in range(HALF)])
X_ORDER = np.array([4 * j + 2 * k + i for i in range(2) for k in range(2) for j in range(64)])


def surface_response():
    total = np.zeros((N, N))
    for c in range(N):
        total += SINE[0, c] ** 2 / (1.0 + 64.0 * (RATES[c] + RATES[:, None] + RATES[None, :]))
    return total


Q = SINE.astype(np.float32)
RESPONSE = surface_response()[MODE_ORDER].astype(np.float32)
Q_MODES = Q[MODE_ORDER]
Q_X = Q[:, X_ORDER]


def lobatto_derivative():
    points = np.array([-1.0, -1.0 / np.sqrt(5.0), 1.0 / np.sqrt(5.0), 1.0])
    weights = np.array(
        [1.0 / np.prod([points[j] - points[k] for k in range(4) if k != j]) for j in range(4)]
    )
    deriv = np.zeros((4, 4))
    for i in range(4):
        for j in range(4):
            if i != j:
                deriv[i, j] = weights[j] / weights[i] / (points[i] - points[j])
        deriv[i, i] = -np.sum(deriv[i])
    return deriv


def operator_parts():
    deriv, eye = lobatto_derivative(), np.eye(4)
    along = [
        np.kron(eye, np.kron(eye, deriv)),
        np.kron(eye, np.kron(deriv, eye)),
        np.kron(deriv, np.kron(eye, eye)),
    ]
    second = sum(d @ d for d in along)
    pick = np.zeros((4, 4, 4, 4))
    for i in range(4):
        for j in range(4):
            pick[i, j, i, j] = 1.0
    eye16 = np.eye(16)
    right, left = np.kron(eye16, pick[3, 3]), np.kron(eye16, pick[0, 0])
    right_from, left_from = np.kron(eye16, pick[3, 0]), np.kron(eye16, pick[0, 3])
    fixed = np.kron(np.eye(5), np.eye(64) - 0.15 * right - 0.15 * left)
    fixed = fixed + DT * VISC * np.kron(np.diag([0.0, 1.0, 1.0, 1.0, 1.0]), second)
    by_x = -DT * along[0] + 0.15 * right - 0.15 * left
    return [
        np.asarray(a, np.float32)
        for a in (
            fixed,
            by_x,
            -DT * along[1],
            -DT * along[2],
            np.kron(np.eye(5), 0.15 * right_from),
            -0.15 * right_from,
            np.kron(np.eye(5), 0.15 * left_from),
            0.15 * left_from,
        )
    ]


FIXED, BY_X, BY_Y, BY_Z, NEXT_FIXED, NEXT_X, PREV_FIXED, PREV_X = operator_parts()


def mm(a, b):
    return lax.dot_general(a, b, (((1,), (0,)), ((), ())), precision=HIGH)


def mm_nt(a, b):
    return lax.dot_general(a, b, (((1,), (1,)), ((), ())), precision=HIGH)


def mm_tn(a, b):
    return lax.dot_general(a, b, (((0,), (0,)), ((), ())), precision=HIGH)


def step_matrices(flux_jacobian):
    own = (
        FIXED
        + jnp.kron(flux_jacobian[0], BY_X)
        + jnp.kron(flux_jacobian[1], BY_Y)
        + jnp.kron(flux_jacobian[2], BY_Z)
    )
    following = NEXT_FIXED + jnp.kron(flux_jacobian[0], NEXT_X)
    preceding = PREV_FIXED + jnp.kron(flux_jacobian[0], PREV_X)
    return own, following, preceding


def chain_halo(fluid):
    last, first = fluid[:, -1:], fluid[:, :1]
    before = lax.ppermute(last, ALL, [(i, i + 1) for i in range(255)])
    after = lax.ppermute(first, ALL, [(i + 1, i) for i in range(255)])
    return before, after


def fluid_step(fluid, matrices, halo):
    own, following, preceding = matrices
    before, after = halo
    shifted_next = jnp.concatenate([fluid[:, 1:], after], axis=1)
    shifted_prev = jnp.concatenate([before, fluid[:, :-1]], axis=1)
    return mm(own, fluid) + mm(following, shifted_next) + mm(preceding, shifted_prev)


def wall(fluid):
    return fluid[256:272] - fluid[0:16]


def patch_values(surface_t, x_hot, chunk_hot, fold):
    return mm(fold, mm(surface_t, x_hot) * chunk_hot)


def on_device(fluid_state, flux_jacobian, solid_temp, iface_elem, iface_owner, iface_patch):
    me = lax.axis_index(ALL)
    group, core = me // HALF, me % 2
    sine = jnp.asarray(Q)
    sine_half = lax.dynamic_slice(sine, (0, group * HALF), (N, HALF))

    pay1 = jnp.concatenate([mm_nt(sine_half, solid_temp[:, i, :]) for i in range(2)], axis=1)
    got1 = lax.all_to_all(pay1, ALL, split_axis=0, concat_axis=0, tiled=True)

    fluid0 = fluid_state.reshape(320, -1)
    matrices = step_matrices(flux_jacobian)
    fluid1 = fluid_step(fluid0, matrices, chain_halo(fluid0))
    elem_hot = (iface_elem[:, None] == jnp.arange(fluid0.shape[1])[None, :]).astype(F32)
    wall0, wall1 = wall(fluid0), wall(fluid1)
    slot_values = mm_nt(jnp.concatenate([wall0, wall1 - GAIN * wall0], axis=0), elem_hot)
    trace0 = slot_values[:16]

    owners = iface_owner[:, 0]
    patch = iface_patch
    same = (owners[:, None] == owners[None, :]) & (
        jnp.arange(HALF)[:, None] < jnp.arange(HALF)[None, :]
    )
    place = jnp.sum(same.astype(jnp.int32), axis=0)
    sent = jnp.concatenate(
        [slot_values, (patch + 1).astype(F32)[None, :], jnp.zeros((31, HALF), F32)], axis=0
    )
    lanes = []
    for i in range(2):
        hot = (jnp.arange(HALF)[:, None] == owners[None, :]) & (place == i)[None, :]
        lanes.append(mm_nt(hot.astype(F32), sent))
    got_fluid = lax.all_to_all(
        jnp.concatenate(lanes, axis=1), SUB, split_axis=0, concat_axis=0, tiled=True
    )

    lane = np.arange(HALF)
    spread = np.zeros((2, HALF, 2 * HALF), np.float32)
    for i in range(2):
        for f in range(2):
            spread[i, i * 64 + f * 16 + lane % 16, f * HALF + lane] = 1.0
    sums = [[0.0, 0.0], [0.0, 0.0]]
    counts = [0.0, 0.0]
    count_lanes = 0.0
    for i in range(2):
        ids = got_fluid[:, i * 64 + 32 : i * 64 + 33] - 1.0
        values = mm(got_fluid, spread[i])
        count_lanes = count_lanes + jnp.sum((ids == lane).astype(F32), axis=0, keepdims=True)
        for xl in range(2):
            mask = ids == (xl * 8 + lane // 16)
            counts[xl] = counts[xl] + jnp.sum(mask.astype(F32), axis=0, keepdims=True)
            for f in range(2):
                part = jnp.where(mask, values[:, f * HALF : (f + 1) * HALF], 0.0)
                sums[f][xl] = sums[f][xl] + jnp.sum(part, axis=0, keepdims=True)
    heat0 = [sums[0][xl] - counts[xl] * solid_temp[0, xl : xl + 1, :] for xl in range(2)]
    later = jnp.concatenate(sums[1], axis=0)

    sine_surface = sine[0:1]
    modes = 0.0
    for i in range(2):
        by_z = mm_nt(sine, got1[:, i * N : (i + 1) * N])
        modes = modes + mm(by_z, np.concatenate([Q[:, i::2].T] * 2, axis=0))
    own_rate = lax.dynamic_slice(jnp.asarray(RATES, F32), (me,), (1,))
    z_x_rates = (1.0 + 64.0 * (RATES[:, None] + RATES[None, :])).astype(np.float32)
    decay = 1.0 / (z_x_rates + 64.0 * own_rate[0])
    once = decay * modes
    surface_row = mm(sine_surface, once)

    sine_modes = jnp.asarray(Q_MODES)
    modes_half = lax.dynamic_slice(sine_modes, (0, group * HALF), (N, HALF))
    later_modes = mm_nt(modes_half, later)
    shared = jnp.concatenate([surface_row, heat0[0], heat0[1]], axis=1)
    tail = jnp.concatenate(
        [
            jnp.broadcast_to(count_lanes[:, :16], (HALF, 16)),
            later_modes[:HALF],
            later_modes[HALF:],
            jnp.zeros((HALF, 108), F32),
        ],
        axis=1,
    )
    pay2 = jnp.concatenate([jnp.broadcast_to(shared, (HALF, 512)), tail], axis=1)
    got2 = lax.all_to_all(pay2, SAME_CORE, split_axis=0, concat_axis=0, tiled=True)
    other = lax.ppermute(got2, "c", [(0, 1), (1, 0)])
    first = core == 0
    gathered = jnp.concatenate(
        [jnp.where(first, got2, other), jnp.where(first, other, got2)], axis=0
    )

    def block(g, lo, hi):
        return jnp.concatenate(
            [gathered[k * HALF + g * 64 : k * HALF + g * 64 + 64, lo:hi] for k in range(2)], axis=0
        )

    heat_modes = 0.0
    for xl in range(2):
        by_y = 0.0
        for g in range(2):
            by_y = by_y + mm_nt(
                Q_MODES[:, g * HALF : (g + 1) * HALF],
                block(g, N + xl * HALF, N + (xl + 1) * HALF),
            )
        heat_modes = heat_modes + mm(by_y, Q_X[:, xl * HALF : (xl + 1) * HALF].T)
    surface1_modes = gathered[:, :N] + RESPONSE * heat_modes
    surface1 = mm(mm(Q_MODES.T, surface1_modes), Q_X)
    tails = [block(g, 512, 640) for g in range(2)]
    expand = [
        (lane[None, :] == (xl * 8 + lane // 16)[:, None]).astype(np.float32) for xl in range(2)
    ]
    count_t = jnp.concatenate(
        [
            jnp.concatenate([mm_nt(expand[xl], tails[g]) for xl in range(2)], axis=1)
            for g in range(2)
        ],
        axis=0,
    )
    own_sine = lax.dynamic_slice(sine, (me, 0), (1, N))
    reduced = mm(own_sine, count_t * surface1)
    tail_sum = tails[0] + tails[1]
    later_row = jnp.concatenate(
        [
            mm_nt((lane[None, :] == 16 + 2 * core + xl).astype(F32), tail_sum)
            for xl in range(2)
        ],
        axis=1,
    )
    heat1_modes = mm(later_row - 0.7 * reduced, Q_X.T)
    heat0_modes = lax.dynamic_slice(heat_modes, (core * HALF + me // 2, 0), (1, N))
    surface_column = jnp.asarray(Q[0][:, None])
    final = decay * (decay * (modes + surface_column * heat0_modes) + surface_column * heat1_modes)
    final_row = mm(sine_surface, final)

    back = [mm(mm_nt(Q[:, xl::2].T, final), sine) for xl in range(2)]
    pay3 = jnp.concatenate(back + [jnp.broadcast_to(final_row, (HALF, N))], axis=1)
    got3 = lax.all_to_all(
        jnp.concatenate([pay3, pay3], axis=0), ALL, split_axis=0, concat_axis=0, tiled=True
    )

    x_of_slot = patch // 8 * HALF + owners % 2 * 64 + owners // 2
    x_hot = (jnp.arange(N)[:, None] == x_of_slot[None, :]).astype(F32)
    chunk_hot = ((lane // 16)[:, None] == (patch % 8)[None, :]).astype(F32)
    fold = (np.arange(16)[:, None] == (lane % 16)[None, :]).astype(np.float32)
    own_surface1 = lax.dynamic_slice(surface1, (group * HALF, 0), (HALF, N))
    patch1 = patch_values(own_surface1, x_hot, chunk_hot, fold)
    source0 = GAIN * mm(patch1 - trace0, elem_hot)
    fluid1 = jnp.concatenate([fluid1[:256], fluid1[256:272] + source0, fluid1[272:]], axis=0)
    trace1 = mm_nt(wall(fluid1), elem_hot)
    fluid2 = fluid_step(fluid1, matrices, chain_halo(fluid1))

    sine_back = sine_half.T
    solid_out = jnp.stack(
        [mm_tn(got3[:, xl * N : (xl + 1) * N], sine_half) for xl in range(2)], axis=1
    )
    surface2 = mm(mm(sine_back, got3[:, 512:]), Q_X)
    patch2 = patch_values(surface2, x_hot, chunk_hot, fold)
    source1 = GAIN * mm(patch2 - trace1, elem_hot)
    fluid2 = jnp.concatenate([fluid2[:256], fluid2[256:272] + source1, fluid2[272:]], axis=0)
    return fluid2.reshape(fluid_state.shape), solid_out


def solution(mesh):
    fine = Mesh(mesh.devices.reshape(2, 2, 4, 8, 2), ALL)
    placed = (
        P(None, None, ALL),
        P(),
        P(None, SUB, "g"),
        P(ALL),
        P(ALL, None),
        P(ALL),
    )
    return jax.shard_map(
        on_device,
        mesh=fine,
        in_specs=placed,
        out_specs=(P(None, None, ALL), P(None, SUB, "g")),
        check_vma=False,
    )
```

```python
import jax
import jax.numpy as jnp
import ml_dtypes
import numpy as np
from jax import lax
from jax.experimental import pallas as pl
from jax.experimental.pallas import tpu as pltpu
from jax.sharding import Mesh, PartitionSpec as P

ALL = ("g", "yl", "x", "z", "c")
SUB = ("yl", "x", "z", "c")
SAME_CORE = ("g", "yl", "x", "z")
N = 256
HALF = 128
DT = 0.05
VISC = 0.05
GAIN = 0.3
F32 = jnp.float32
BF16 = jnp.bfloat16
NN = ((1,), (0,))
NT = ((1,), (1,))
TN = ((0,), (0,))


def sine_table(length):
    numbers = np.arange(length) + 1
    phases = numbers[:, None] * numbers[None, :] % (2 * (length + 1))
    return np.sqrt(2.0 / (length + 1)) * np.sin(np.pi * phases / (length + 1))


def rates(length):
    return 2.0 - 2.0 * np.cos(np.pi * (np.arange(length) + 1) / (length + 1))


SINE = sine_table(N)
RATES = rates(N)
MODE_ORDER = np.array([2 * q + k for k in range(2) for q in range(HALF)])
X_ORDER = np.array([4 * j + 2 * k + i for i in range(2) for k in range(2) for j in range(64)])


def surface_response():
    total = np.zeros((N, N))
    for c in range(N):
        total += SINE[0, c] ** 2 / (1.0 + 64.0 * (RATES[c] + RATES[:, None] + RATES[None, :]))
    return total


Q = SINE.astype(np.float32)
RESPONSE = surface_response()[MODE_ORDER].astype(np.float32)
Q_MODES = Q[MODE_ORDER]
Q_X = Q[:, X_ORDER]


def lobatto_derivative():
    points = np.array([-1.0, -1.0 / np.sqrt(5.0), 1.0 / np.sqrt(5.0), 1.0])
    weights = np.array(
        [1.0 / np.prod([points[j] - points[k] for k in range(4) if k != j]) for j in range(4)]
    )
    deriv = np.zeros((4, 4))
    for i in range(4):
        for j in range(4):
            if i != j:
                deriv[i, j] = weights[j] / weights[i] / (points[i] - points[j])
        deriv[i, i] = -np.sum(deriv[i])
    return deriv


def operator_parts():
    deriv, eye = lobatto_derivative(), np.eye(4)
    along = [
        np.kron(eye, np.kron(eye, deriv)),
        np.kron(eye, np.kron(deriv, eye)),
        np.kron(deriv, np.kron(eye, eye)),
    ]
    second = sum(d @ d for d in along)
    pick = np.zeros((4, 4, 4, 4))
    for i in range(4):
        for j in range(4):
            pick[i, j, i, j] = 1.0
    eye16 = np.eye(16)
    right, left = np.kron(eye16, pick[3, 3]), np.kron(eye16, pick[0, 0])
    right_from, left_from = np.kron(eye16, pick[3, 0]), np.kron(eye16, pick[0, 3])
    fixed = np.kron(np.eye(5), np.eye(64) - 0.15 * right - 0.15 * left)
    fixed = fixed + DT * VISC * np.kron(np.diag([0.0, 1.0, 1.0, 1.0, 1.0]), second)
    by_x = -DT * along[0] + 0.15 * right - 0.15 * left
    return [
        np.asarray(a, np.float32)
        for a in (
            fixed,
            by_x,
            -DT * along[1],
            -DT * along[2],
            np.kron(np.eye(5), 0.15 * right_from),
            -0.15 * right_from,
            np.kron(np.eye(5), 0.15 * left_from),
            0.15 * left_from,
        )
    ]


FIXED, BY_X, BY_Y, BY_Z, NEXT_FIXED, NEXT_X, PREV_FIXED, PREV_X = operator_parts()


def pair(table):
    high = np.asarray(table, np.float32).astype(ml_dtypes.bfloat16)
    low = (np.asarray(table, np.float32) - high.astype(np.float32)).astype(ml_dtypes.bfloat16)
    return np.stack([high, low])


SINE_PAIR = pair(Q)
SINE_BLOCKS = np.ascontiguousarray(
    pair(Q).reshape(2, 2, HALF, 2, HALF).transpose(0, 1, 3, 2, 4)
)
X_SPLIT = np.stack([pair(Q[i::2]) for i in range(2)])
MODES_PAIR = pair(Q_MODES)
MODES_PAIR_T = pair(Q_MODES.T)
X_PAIR = pair(Q_X)
X_PAIR_T = pair(Q_X.T)
Y_HALVES = np.stack([pair(Q[:, :HALF]), pair(Q[:, HALF:])])
Y_HALVES_T = np.stack([pair(Q[:HALF]), pair(Q[HALF:])])
MODES_HALVES = np.stack([pair(Q_MODES[:, :HALF]), pair(Q_MODES[:, HALF:])])
RATE_TABLE = (1.0 + 64.0 * (RATES[:, None] + RATES[None, :])).astype(np.float32)
SURFACE_ROW = np.broadcast_to(Q[:1], (8, N)).copy()
SURFACE_COLUMN = Q[:, :1].copy()
FIELD_ROWS = np.kron(np.eye(5), np.ones((64, 1))).astype(np.float32)
FIELD_HOT = np.pad(FIELD_ROWS, ((0, 0), (0, 123))).astype(ml_dtypes.bfloat16)
BY_TILES = np.stack([np.tile(t, (5, 5)) for t in (BY_X, BY_Y, BY_Z)])
NEXT_TILE, PREV_TILE = np.tile(NEXT_X, (5, 5)), np.tile(PREV_X, (5, 5))


def split(value):
    high = value.astype(BF16)
    return high, (value - high.astype(F32)).astype(BF16)


def dot(a, b, dims=NN):
    return lax.dot_general(a, b, (dims, ((), ())), preferred_element_type=F32)


def dot3(a, b, dims=NN):
    a = split(a) if not isinstance(a, tuple) else a
    b = split(b) if not isinstance(b, tuple) else b
    return dot(a[0], b[0], dims) + (dot(a[0], b[1], dims) + dot(a[1], b[0], dims))


def hot_dot(hot, b, dims=NN):
    high, low = split(b)
    return dot(hot, high, dims) + dot(hot, low, dims)


def dot_hot(a, hot, dims=NN):
    high, low = split(a)
    return dot(high, hot, dims) + dot(low, hot, dims)


def hot_of(condition):
    return jnp.where(condition, 1.0, 0.0).astype(BF16)


def iota(shape, dim):
    return lax.broadcasted_iota(jnp.int32, shape, dim)


def both(ref):
    return ref[0], ref[1]


def rows(ref, first, count, stride):
    return ref[pl.ds(first, count, stride), :]


def edges_kernel(left_ref, right_ref, first_ref, last_ref):
    first_ref[...] = left_ref[...].T[0:1]
    last_ref[...] = right_ref[...].T[HALF - 1 : HALF]


def matrices_kernel(
    fluid_ref, jac_ref, hot_ref, fixed_ref, tiles_ref, nf_ref, nt_ref, pf_ref, pt_ref, out_ref, wall_ref
):
    spread = []
    for d in range(3):
        by_row = hot_dot(hot_ref[...], jac_ref[d])
        spread.append(dot_hot(by_row, hot_ref[...], NT))
    own = fixed_ref[...]
    for d in range(3):
        own = own + spread[d] * tiles_ref[d]
    parts = [own, nf_ref[...] + spread[0] * nt_ref[...], pf_ref[...] + spread[0] * pt_ref[...]]
    for i, part in enumerate(parts):
        out_ref[pl.ds(320 * i, 320), :] = part
    moved = jnp.concatenate([part[256:272] - part[0:16] for part in parts], axis=0)
    wall_ref[0:48] = dot3(moved, fluid_ref[...])
    wall_ref[48:64] = fluid_ref[256:272] - fluid_ref[0:16]


def with_halo(own, following, preceding, after, before):
    lane = iota(own.shape, 1)
    count = own.shape[1]
    following = jnp.where(lane == count - 1, after, pltpu.roll(following, count - 1, 1))
    preceding = jnp.where(lane == 0, before, pltpu.roll(preceding, 1, 1))
    return own + following + preceding


def first_kernel(
    where_ref, solid_ref, far_ref, wall_ref, matrix_ref, before_ref, after_ref, elem_ref,
    owner_col_ref, owner_ref, patch_ref, blocks_ref, out_ref, trace_ref
):
    group = where_ref[0]
    near, far = [
        (blocks_ref[0, group, h], blocks_ref[1, group, h]) for h in (group, 1 - group)
    ]
    for i in range(2):
        modes = dot3(near, rows(solid_ref, i, N, 2), NT) + dot3(far, rows(far_ref, i, N, 2), NT)
        for h in range(2):
            out_ref[pl.ds(2 * i + h, HALF, 5), :] = modes[:, h * HALF : (h + 1) * HALF]

    def halo(part, row):
        start = 320 * part
        moved = matrix_ref[pl.ds(start + 256, 16), :] - matrix_ref[pl.ds(start, 16), :]
        return jnp.sum(moved * row, axis=1, keepdims=True)

    later = with_halo(
        wall_ref[0:16], wall_ref[16:32], wall_ref[32:48],
        halo(1, after_ref[...]), halo(2, before_ref[...]),
    )
    wall0 = wall_ref[48:64]
    elem_hot = hot_of(elem_ref[...] == iota((HALF, wall0.shape[1]), 1))
    values = dot_hot(jnp.concatenate([wall0, later - GAIN * wall0], axis=0), elem_hot, NT)
    trace_ref[...] = values[:16]
    owner = owner_ref[...]
    square = (HALF, HALF)
    same = (owner_col_ref[...] == owner) & (iota(square, 0) < iota(square, 1))
    place = jnp.sum(jnp.where(same, 1.0, 0.0), axis=0, keepdims=True)
    ids = jnp.broadcast_to((patch_ref[...] + 1).astype(F32), (8, HALF))
    filler = jnp.zeros((24, HALF), F32)
    sent = jnp.concatenate([values, ids, filler], axis=0)
    none = jnp.zeros((64, HALF), F32)
    arranged = 0.0
    for i in range(2):
        hot = hot_of((iota(square, 0) == owner) & (place == float(i)))
        padded = jnp.concatenate([sent, none] if i == 0 else [none, sent], axis=0)
        arranged = arranged + hot_dot(hot, padded, NT)
    out_ref[pl.ds(4, HALF, 5), :] = arranged


def modes_kernel(
    where_ref, rate_ref, got_ref, surface_ref, sine_ref, x_ref, table_ref, row_ref, halves_ref,
    modes_ref, out_ref
):
    group = where_ref[0]
    sine = both(sine_ref)
    modes = 0.0
    for i in range(2):
        part = jnp.concatenate([rows(got_ref, 2 * i + h, HALF, 5) for h in range(2)], axis=1)
        by_z = dot3(sine, part, NT)
        modes = modes + dot3(by_z, (x_ref[i, 0], x_ref[i, 1]))
    modes_ref[...] = modes
    once = modes / (table_ref[...] + 64.0 * rate_ref[0])
    surface_row = dot3(row_ref[...], once)[0:1]

    fluid = rows(got_ref, 4, HALF, 5)
    square = (HALF, HALF)
    lane = iota(square, 1)
    fluid_pair = split(fluid)
    sums = [[0.0, 0.0], [0.0, 0.0]]
    counts = [0.0, 0.0]
    count_lanes = 0.0
    for i in range(2):
        ids = fluid[:, i * 64 + 32 : i * 64 + 33].astype(jnp.int32) - 1
        count_lanes = count_lanes + jnp.sum(jnp.where(ids == lane, 1.0, 0.0), axis=0, keepdims=True)
        for f in range(2):
            pick = hot_of(iota(square, 0) == i * 64 + f * 16 + lane % 16)
            values = dot(fluid_pair[0], pick) + dot(fluid_pair[1], pick)
            for xl in range(2):
                mask = ids == xl * 8 + lane // 16
                sums[f][xl] = sums[f][xl] + jnp.sum(
                    jnp.where(mask, values, 0.0), axis=0, keepdims=True
                )
                if f == 0:
                    counts[xl] = counts[xl] + jnp.sum(
                        jnp.where(mask, 1.0, 0.0), axis=0, keepdims=True
                    )
    heat = [sums[0][xl] - counts[xl] * surface_ref[xl : xl + 1, :] for xl in range(2)]
    by_modes = (halves_ref[group, 0], halves_ref[group, 1])
    tail = jnp.where(lane < 16, count_lanes, 0.0)
    for xl in range(2):
        column = dot3(by_modes, jnp.broadcast_to(sums[1][xl], (8, HALF)), NT)[:, 0:1]
        for k in range(2):
            tail = jnp.where(lane == 16 + 2 * k + xl, column[k * HALF : (k + 1) * HALF], tail)
    shared = [surface_row[:, :HALF], surface_row[:, HALF:], heat[0], heat[1]]
    for r in range(4):
        out_ref[pl.ds(r, HALF, 5), :] = jnp.broadcast_to(shared[r], square)
    out_ref[pl.ds(4, HALF, 5), :] = tail


def solve_kernel(
    where_ref, rate_ref, got_ref, other_ref, modes_ref, response_ref, by_modes_ref, from_modes_ref,
    x_ref, xt_ref, sine_ref, full_ref, x_split_ref, table_ref, row_ref, column_ref,
    surface_ref, out_ref, heat_ref
):
    group, core, me = where_ref[0], where_ref[1], where_ref[2]
    first = jnp.full((HALF, HALF), core, jnp.int32) == 0
    ordered = []
    for r in range(5):
        mine, theirs = rows(got_ref, r, HALF, 5), rows(other_ref, r, HALF, 5)
        ordered.append((jnp.where(first, mine, theirs), jnp.where(first, theirs, mine)))

    def block(g, r):
        return jnp.concatenate([ordered[r][k][g * 64 : (g + 1) * 64] for k in range(2)], axis=0)

    heat_modes = 0.0
    for xl in range(2):
        by_y = 0.0
        for g in range(2):
            halves = (by_modes_ref[g, 0], by_modes_ref[g, 1])
            by_y = by_y + dot3(halves, block(g, 2 + xl), NT)
        at = pl.ds(xl * HALF, HALF)
        heat_modes = heat_modes + dot3(by_y, (xt_ref[0, at, :], xt_ref[1, at, :]))
    heat_ref[...] = heat_modes
    given = jnp.concatenate(
        [jnp.concatenate([ordered[h][k] for h in range(2)], axis=1) for k in range(2)], axis=0
    )
    x_pair = both(x_ref)
    surface = dot3(both(from_modes_ref), given + response_ref[...] * heat_modes)
    surface = dot3(surface, x_pair)
    heat_ref[...] = surface
    surface_ref[...] = heat_ref[pl.ds(pl.multiple_of(group * HALF, HALF), HALF), :]
    heat_ref[...] = heat_modes
    square = (HALF, HALF)
    tails = [block(g, 4) for g in range(2)]
    tail_pairs = [tail.astype(BF16) for tail in tails]
    expand = [hot_of(iota(square, 1) == xl * 8 + iota(square, 0) // 16) for xl in range(2)]
    count = jnp.concatenate(
        [
            jnp.concatenate([dot(expand[xl], tail_pairs[g], NT) for xl in range(2)], axis=1)
            for g in range(2)
        ],
        axis=0,
    )
    own_sine = jnp.broadcast_to(full_ref[pl.ds(me, 1), :], (8, N))
    reduced = dot3(own_sine, count * surface)
    tail_sum = tails[0] + tails[1]
    lane8 = iota((8, HALF), 1)
    later = jnp.concatenate(
        [hot_dot(hot_of(lane8 == 16 + 2 * core + xl), tail_sum, NT) for xl in range(2)], axis=1
    )
    heat1 = dot3(later - 0.7 * reduced, both(xt_ref))[0:1]
    heat0 = heat_ref[pl.ds(core * HALF + me // 2, 1), :]
    decay = 1.0 / (table_ref[...] + 64.0 * rate_ref[0])
    column = column_ref[...]
    final = decay * (decay * (modes_ref[...] + column * heat0) + column * heat1)
    final_row = dot3(row_ref[...], final)[0:1]
    final = split(final)
    sine = both(sine_ref)
    for xl in range(2):
        by_x = dot3((x_split_ref[xl, 0], x_split_ref[xl, 1]), final, NT)
        back = dot3(by_x, sine)
        for g in range(2):
            for h in range(2):
                out_ref[pl.ds(g * 768 + 2 * xl + h, HALF, 6), :] = back[:, h * HALF : (h + 1) * HALF]
    for h in range(2):
        out_ref[pl.ds(4 + h, N, 6), :] = jnp.broadcast_to(
            final_row[:, h * HALF : (h + 1) * HALF], (N, HALF)
        )


def patch_values(surface, owner, patch):
    x_of_slot = patch // 8 * HALF + owner % 2 * 64 + owner // 2
    square = (HALF, HALF)
    x_hot = hot_of(iota((N, HALF), 0) == x_of_slot)
    met = dot_hot(surface, x_hot)
    met = jnp.where(iota(square, 0) // 16 == patch % 8, met, 0.0)
    fold = hot_of(iota((16, HALF), 0) == iota((16, HALF), 1) % 16)
    return hot_dot(fold, met)


def source_kernel(
    fluid_ref, surface_ref, trace_ref, elem_ref, owner_ref, patch_ref,
    out_ref, later_ref, first_ref, last_ref
):
    count = fluid_ref.shape[1]
    elem_hot = hot_of(elem_ref[...] == iota((HALF, count), 1))
    met = patch_values(surface_ref[...], owner_ref[...], patch_ref[...])
    source = GAIN * dot_hot(met - trace_ref[...], elem_hot)
    out_ref[...] = fluid_ref[...]
    walls = fluid_ref[256:272] + source
    out_ref[256:272] = walls
    later_ref[...] = dot_hot(walls - fluid_ref[0:16], elem_hot, NT)
    first_ref[...] = out_ref[:, 0:HALF].T[0:1]
    last_ref[...] = out_ref[:, count - HALF : count].T[HALF - 1 : HALF]


def step_kernel(fluid_ref, matrix_ref, before_ref, after_ref, out_ref):
    fluid = split(fluid_ref[...])
    after, before = [
        jnp.sum(matrix_ref[pl.ds(320 * part, 320), :] * row, axis=1, keepdims=True)
        for part, row in ((1, after_ref[...]), (2, before_ref[...]))
    ]
    parts = [dot3(matrix_ref[pl.ds(320 * i, 320), :], fluid) for i in range(3)]
    out_ref[...] = with_halo(*parts, after, before)


def last_kernel(
    where_ref, got_ref, y_ref, yt_ref, x_ref, later_ref, elem_ref, owner_ref, patch_ref, fluid_ref,
    solid_ref, out_ref
):
    group = where_ref[0]
    by_y = (y_ref[group, 0], y_ref[group, 1])
    for xl in range(2):
        for h in range(2):
            part = rows(got_ref, 2 * xl + h, N, 6)
            solid_ref[pl.ds(h * N + xl, HALF, 2), :] = dot3(part, by_y, TN)
    given = jnp.concatenate([rows(got_ref, 4 + h, N, 6) for h in range(2)], axis=1)
    surface = dot3(dot3((yt_ref[group, 0], yt_ref[group, 1]), given), both(x_ref))
    met = patch_values(surface, owner_ref[...], patch_ref[...])
    elem_hot = hot_of(elem_ref[...] == iota((HALF, fluid_ref.shape[1]), 1))
    out_ref[...] = fluid_ref[...] + GAIN * dot_hot(met - later_ref[...], elem_hot)


def call(kernel, outs, args, scalars=0, scratch=(), aliases=None, specs=None, out_specs=None, cost=None):
    whole = pl.BlockSpec(memory_space=pltpu.VMEM)
    given = [pl.BlockSpec(memory_space=pltpu.SMEM)] * scalars + [whole] * (len(args) - scalars)
    return pl.pallas_call(
        kernel,
        out_shape=[jax.ShapeDtypeStruct(shape, F32) for shape in outs],
        in_specs=specs or given,
        out_specs=out_specs or [whole] * len(outs),
        scratch_shapes=list(scratch),
        input_output_aliases=aliases or {},
        cost_estimate=pl.CostEstimate(flops=int(cost or 1e8), bytes_accessed=1 << 20, transcendentals=0),
        compiler_params=pltpu.CompilerParams(vmem_limit_bytes=40 << 20),
    )(*args)


def chain_halo(first, last):
    before = lax.ppermute(last, ALL, [(i, i + 1) for i in range(255)])
    after = lax.ppermute(first, ALL, [(i + 1, i) for i in range(255)])
    return before, after


def on_device(fluid_state, flux_jacobian, solid_temp, iface_elem, iface_owner, iface_patch):
    me = lax.axis_index(ALL)
    where = jnp.stack([me // HALF, me % 2, me]).astype(jnp.int32)
    rate = lax.dynamic_slice(jnp.asarray(RATES, F32), (me,), (1,))
    fluid0 = fluid_state.reshape(320, -1)
    count = fluid0.shape[1]
    solid = solid_temp.reshape(2 * N, HALF)
    elem = iface_elem[:, None]
    owner, patch = iface_owner.reshape(1, HALF), iface_patch[None, :]

    far = lax.ppermute(solid, "g", [(0, 1), (1, 0)])
    first, last = pl.pallas_call(
        edges_kernel,
        grid=(1,),
        out_shape=[jax.ShapeDtypeStruct((1, 320), F32)] * 2,
        in_specs=[
            pl.BlockSpec((320, HALF), lambda i: (0, 0)),
            pl.BlockSpec((320, HALF), lambda i: (0, count // HALF - 1)),
        ],
        out_specs=[pl.BlockSpec((1, 320), lambda i: (0, 0))] * 2,
    )(fluid0, fluid0)
    before, after = chain_halo(first, last)
    jacobian = jnp.pad(flux_jacobian, ((0, 0), (0, 123), (0, 123)))
    matrix, walls = call(
        matrices_kernel,
        [(960, 320), (64, count)],
        [fluid0, jacobian, FIELD_HOT, FIXED, BY_TILES, NEXT_FIXED, NEXT_TILE, PREV_FIXED, PREV_TILE],
    )
    pay1, trace0 = call(
        first_kernel,
        [(5 * HALF, HALF), (16, HALF)],
        [where, solid, far, walls, matrix, before, after, elem, iface_owner, owner, patch, SINE_BLOCKS],
        scalars=1,
    )
    got1 = lax.all_to_all(pay1, SUB, split_axis=0, concat_axis=0, tiled=True)
    (fluid1,) = call(step_kernel, [(320, count)], [fluid0, matrix, before, after], cost=2e9)
    modes, pay2 = call(
        modes_kernel,
        [(N, N), (5 * HALF, HALF)],
        [where, rate, got1, solid[:2], SINE_PAIR, X_SPLIT, RATE_TABLE, SURFACE_ROW, MODES_HALVES],
        scalars=2,
    )
    got2 = lax.all_to_all(pay2, SAME_CORE, split_axis=0, concat_axis=0, tiled=True)
    other = lax.ppermute(got2, "c", [(0, 1), (1, 0)])
    surface1, pay3 = call(
        solve_kernel,
        [(HALF, N), (6 * N, HALF)],
        [where, rate, got2, other, modes, RESPONSE, MODES_HALVES, MODES_PAIR_T, X_PAIR, X_PAIR_T,
         SINE_PAIR, Q, X_SPLIT, RATE_TABLE, SURFACE_ROW, SURFACE_COLUMN],
        scalars=2,
        scratch=[pltpu.VMEM((N, N), F32)],
    )
    got3 = lax.all_to_all(pay3, ALL, split_axis=0, concat_axis=0, tiled=True)
    fluid1, trace1, first, last = call(
        source_kernel,
        [(320, count), (16, HALF), (1, 320), (1, 320)],
        [fluid1, surface1, trace0, elem, owner, patch],
    )
    before, after = chain_halo(first, last)
    (fluid2,) = call(step_kernel, [(320, count)], [fluid1, matrix, before, after], cost=2e9)
    solid_out, fluid2 = pl.pallas_call(
        last_kernel,
        grid=(1,),
        out_shape=[
            jax.ShapeDtypeStruct((2 * N, HALF), F32),
            jax.ShapeDtypeStruct((320, count), F32),
        ],
        in_specs=[pl.BlockSpec(memory_space=pltpu.SMEM)]
        + [pl.BlockSpec(memory_space=pltpu.VMEM)] * 8
        + [pl.BlockSpec((16, count), lambda i: (16, 0))],
        out_specs=[
            pl.BlockSpec((2 * N, HALF), lambda i: (0, 0)),
            pl.BlockSpec((16, count), lambda i: (16, 0)),
        ],
        input_output_aliases={9: 1},
        compiler_params=pltpu.CompilerParams(vmem_limit_bytes=40 << 20),
    )(where, got3, Y_HALVES, Y_HALVES_T, X_PAIR, trace1, elem, owner, patch, fluid2)
    return fluid2.reshape(fluid_state.shape), solid_out.reshape(solid_temp.shape)


def solution(mesh):
    fine = Mesh(mesh.devices.reshape(2, 2, 4, 8, 2), ALL)
    placed = (
        P(None, None, ALL),
        P(),
        P(None, SUB, "g"),
        P(ALL),
        P(ALL, None),
        P(ALL),
    )
    return jax.shard_map(
        on_device,
        mesh=fine,
        in_specs=placed,
        out_specs=(P(None, None, ALL), P(None, SUB, "g")),
        check_vma=False,
    )
```

```python
import functools

import jax
import jax.numpy as jnp
import ml_dtypes
import numpy as np
from jax import lax
from jax.experimental import pallas as pl
from jax.experimental.pallas import tpu as pltpu
from jax.sharding import Mesh, PartitionSpec as P

ALL = ("g", "yl", "x", "z", "c")
SUB = ("yl", "x", "z", "c")
SAME_CORE = ("g", "yl", "x", "z")
N = 256
HALF = 128
DT = 0.05
VISC = 0.05
GAIN = 0.3
F32 = jnp.float32
BF16 = jnp.bfloat16
NN = ((1,), (0,))
NT = ((1,), (1,))
TN = ((0,), (0,))


def sine_table(length):
    numbers = np.arange(length) + 1
    phases = numbers[:, None] * numbers[None, :] % (2 * (length + 1))
    return np.sqrt(2.0 / (length + 1)) * np.sin(np.pi * phases / (length + 1))


def rates(length):
    return 2.0 - 2.0 * np.cos(np.pi * (np.arange(length) + 1) / (length + 1))


SINE = sine_table(N)
RATES = rates(N)
MODE_ORDER = np.array([2 * q + k for k in range(2) for q in range(HALF)])


def surface_response():
    total = np.zeros((N, N))
    for c in range(N):
        total += SINE[0, c] ** 2 / (1.0 + 64.0 * (RATES[c] + RATES[:, None] + RATES[None, :]))
    return total


Q = SINE.astype(np.float32)
Q_HALVES = np.concatenate([Q[:, :HALF], Q[:, HALF:]], axis=0)
RESPONSE = surface_response()[MODE_ORDER].astype(np.float32)


def lobatto_derivative():
    points = np.array([-1.0, -1.0 / np.sqrt(5.0), 1.0 / np.sqrt(5.0), 1.0])
    weights = np.array(
        [1.0 / np.prod([points[j] - points[k] for k in range(4) if k != j]) for j in range(4)]
    )
    deriv = np.zeros((4, 4))
    for i in range(4):
        for j in range(4):
            if i != j:
                deriv[i, j] = weights[j] / weights[i] / (points[i] - points[j])
        deriv[i, i] = -np.sum(deriv[i])
    return deriv


def operator_parts():
    deriv, eye = lobatto_derivative(), np.eye(4)
    along = [
        np.kron(eye, np.kron(eye, deriv)),
        np.kron(eye, np.kron(deriv, eye)),
        np.kron(deriv, np.kron(eye, eye)),
    ]
    second = sum(d @ d for d in along)
    pick = np.zeros((4, 4, 4, 4))
    for i in range(4):
        for j in range(4):
            pick[i, j, i, j] = 1.0
    eye16 = np.eye(16)
    right, left = np.kron(eye16, pick[3, 3]), np.kron(eye16, pick[0, 0])
    right_from, left_from = np.kron(eye16, pick[3, 0]), np.kron(eye16, pick[0, 3])
    fixed = np.kron(np.eye(5), np.eye(64) - 0.15 * right - 0.15 * left)
    fixed = fixed + DT * VISC * np.kron(np.diag([0.0, 1.0, 1.0, 1.0, 1.0]), second)
    by_x = -DT * along[0] + 0.15 * right - 0.15 * left
    return [
        np.asarray(a, np.float32)
        for a in (
            fixed,
            by_x,
            -DT * along[1],
            -DT * along[2],
            np.kron(np.eye(5), 0.15 * right_from),
            -0.15 * right_from,
            np.kron(np.eye(5), 0.15 * left_from),
            0.15 * left_from,
        )
    ]


FIXED, BY_X, BY_Y, BY_Z, NEXT_FIXED, NEXT_X, PREV_FIXED, PREV_X = operator_parts()


def wall_tables():
    groups = []
    for fixed, tables in ((FIXED, (BY_X, BY_Y, BY_Z)), (NEXT_FIXED, (NEXT_X,)), (PREV_FIXED, (PREV_X,))):
        groups.append(fixed[256:272] - fixed[0:16])
        groups += [np.tile(t[:16], (1, 5)) for t in tables]
    return np.stack(groups).astype(np.float32)


WALL_TABLES = wall_tables()
RATE_LIST = RATES.astype(np.float32)
RATE_ROW = (1.0 + 64.0 * RATES)[None, :].astype(np.float32)
RATE_COLUMN = (64.0 * RATES)[:, None].astype(np.float32)
SURFACE_ROW = np.broadcast_to(Q[:1], (8, N)).copy()
SURFACE_COLUMN = Q[:, :1].copy()
FIELD_HOT = np.pad(np.kron(np.eye(5), np.ones((64, 1))), ((0, 0), (0, 3))).astype(ml_dtypes.bfloat16)
TILE_HOT = np.kron(np.ones((5, 1)), np.eye(64)).astype(ml_dtypes.bfloat16)
OPERATORS = np.stack([BY_X, BY_Y, BY_Z, NEXT_X, PREV_X])


def split(value):
    high = value.astype(BF16)
    return high, (value - high.astype(F32)).astype(BF16)


def dot(a, b, dims=NN):
    return lax.dot_general(a, b, (dims, ((), ())), preferred_element_type=F32)


def dot3(a, b, dims=NN):
    a = split(a) if not isinstance(a, tuple) else a
    b = split(b) if not isinstance(b, tuple) else b
    return dot(a[0], b[0], dims) + (dot(a[0], b[1], dims) + dot(a[1], b[0], dims))


def hot_dot(hot, b, dims=NN):
    high, low = split(b)
    return dot(hot, high, dims) + dot(hot, low, dims)


def dot_hot(a, hot, dims=NN):
    high, low = split(a)
    return dot(high, hot, dims) + dot(low, hot, dims)


def hot_of(condition):
    return jnp.where(condition, 1.0, 0.0).astype(BF16)


def iota(shape, dim):
    return lax.broadcasted_iota(jnp.int32, shape, dim)


def rows(ref, first, count, stride):
    return ref[pl.ds(first, count, stride) if stride > 1 else pl.ds(first, count), :]


def sine_rows(ref, first, count, stride):
    return jnp.concatenate([rows(ref, h * N + first, count, stride) for h in range(2)], axis=1)


def x_ordered(sine_ref):
    blocks = [sine_rows(sine_ref, 2 * k + i, 64, 4) for i in range(2) for k in range(2)]
    return split(jnp.concatenate(blocks, axis=0))


def mode_ordered(sine_ref):
    return jnp.concatenate([sine_rows(sine_ref, k, HALF, 2) for k in range(2)], axis=0)


def edges_kernel(left_ref, right_ref, elem_ref, owner_ref, patch_ref, first_ref, last_ref, *, count):
    lane = iota((1, 384), 1)
    gap = jnp.zeros((1, 64), F32)
    for ref, block, at, out, element in (
        (left_ref, left_ref[...], (0, 1), first_ref, 0),
        (right_ref, right_ref[...], (HALF - 1, HALF - 2), last_ref, count - 1),
    ):
        turned = block.T
        met = elem_ref[...] == element
        owner = jnp.sum(jnp.where(met, owner_ref[...] + 1, 0).astype(F32), axis=1, keepdims=True)
        patch = jnp.sum(jnp.where(met, patch_ref[...], 0).astype(F32), axis=1, keepdims=True)
        slot = jnp.where(lane == 0, owner, jnp.where(lane == 1, patch, 0.0))
        out[0:1] = jnp.concatenate([turned[at[0] : at[0] + 1], gap], axis=1)
        out[1:2] = jnp.concatenate([turned[at[1] : at[1] + 1], gap], axis=1)
        out[2:3] = slot
        out[3:8] = jnp.zeros((5, 384), F32)


def walls_kernel(jac_ref, fluid_ref, table_ref, out_ref, matrix_ref):
    @pl.when(pl.program_id(0) == 0)
    def _():
        field = iota((1, 320), 1) // 64
        coefficients = []
        for d in range(3):
            row = jnp.zeros((1, 320), F32)
            for f in range(5):
                row = jnp.where(field == f, jac_ref[d, 4, f] - jac_ref[d, 0, f], row)
            coefficients.append(row)
        own = table_ref[0]
        for d in range(3):
            own = own + coefficients[d] * table_ref[1 + d]
        matrix_ref[0:16] = own
        matrix_ref[16:32] = table_ref[4] + coefficients[0] * table_ref[5]
        matrix_ref[32:48] = table_ref[6] + coefficients[0] * table_ref[7]

    out_ref[0:48] = dot3(matrix_ref[...], fluid_ref[...])
    out_ref[48:64] = fluid_ref[256:272] - fluid_ref[0:16]


def matrices_kernel(jac_ref, field_ref, tile_ref, fixed_ref, operators_ref, out_ref):
    field, tile = field_ref[...], tile_ref[...]

    def spread(d):
        return dot_hot(hot_dot(field, jac_ref[d]), field, NT)

    def tiled(d):
        return dot_hot(hot_dot(tile, operators_ref[d]), tile, NT)

    by_x = spread(0)
    own = by_x * tiled(0) + spread(1) * tiled(1) + spread(2) * tiled(2)
    out_ref[0:320] = fixed_ref[0] + own
    out_ref[320:640] = fixed_ref[1] + by_x * tiled(3)
    out_ref[640:960] = fixed_ref[2] + by_x * tiled(4)


def first_kernel(
    where_ref, solid_ref, far_ref, wall_ref, matrix_ref, before_ref, after_ref, elem_ref,
    owner_col_ref, owner_ref, patch_ref, sine_ref, out_ref, trace_ref, surface_ref
):
    group = where_ref[0]
    near, far = [
        split(sine_ref[pl.ds(pl.multiple_of(half * N + group * HALF, HALF), HALF), :])
        for half in (group, 1 - group)
    ]
    for i in range(2):
        modes = dot3(near, rows(solid_ref, i, N, 2), NT) + dot3(far, rows(far_ref, i, N, 2), NT)
        for h in range(2):
            out_ref[pl.ds(2 * i + h, HALF, 5), :] = modes[:, h * HALF : (h + 1) * HALF]
    surface_ref[...] = solid_ref[0:2]

    def halo(part, ref):
        return jnp.sum(matrix_ref[16 * part : 16 * part + 16] * ref[0:1, 0:320], axis=1, keepdims=True)

    wall0, own = wall_ref[48:64], wall_ref[0:16]
    count = own.shape[1]
    lane = iota(own.shape, 1)
    following = pltpu.roll(wall_ref[16:32], count - 1, 1)
    preceding = pltpu.roll(wall_ref[32:48], 1, 1)
    later = own + jnp.where(lane == count - 1, halo(1, after_ref), following)
    later = later + jnp.where(lane == 0, halo(2, before_ref), preceding)
    elem_hot = hot_of(elem_ref[...] == iota((HALF, count), 1))
    values = dot_hot(jnp.concatenate([wall0, later - GAIN * wall0], axis=0), elem_hot, NT)
    trace_ref[...] = values[:16]
    owner = owner_ref[...]
    square = (HALF, HALF)
    same = (owner_col_ref[...] == owner) & (iota(square, 0) < iota(square, 1))
    place = jnp.sum(jnp.where(same, 1.0, 0.0), axis=0, keepdims=True)
    ids = jnp.broadcast_to((patch_ref[...] + 1).astype(F32), (8, HALF))
    filler = jnp.zeros((24, HALF), F32)
    sent = jnp.concatenate([values, ids, filler], axis=0)
    none = jnp.zeros((64, HALF), F32)
    arranged = 0.0
    for i in range(2):
        hot = hot_of((iota(square, 0) == owner) & (place == float(i)))
        padded = jnp.concatenate([sent, none] if i == 0 else [none, sent], axis=0)
        arranged = arranged + hot_dot(hot, padded, NT)
    out_ref[pl.ds(4, HALF, 5), :] = arranged


def modes_kernel(
    where_ref, rate_ref, got_ref, surface_ref, sine_ref, rate_row_ref, rate_col_ref, row_ref,
    modes_ref, out_ref
):
    group, me = where_ref[0], where_ref[2]
    sine = split(sine_rows(sine_ref, 0, N, 1))
    modes = 0.0
    for i in range(2):
        part = jnp.concatenate([rows(got_ref, 2 * i + h, HALF, 5) for h in range(2)], axis=1)
        by_z = dot3(sine, part, NT)
        modes = modes + dot3(by_z, sine_rows(sine_ref, i, HALF, 2))
    modes_ref[...] = modes
    once = modes / (rate_col_ref[...] + (rate_row_ref[...] + 64.0 * rate_ref[me]))
    surface_row = dot3(row_ref[...], once)[0:1]

    fluid = rows(got_ref, 4, HALF, 5)
    square = (HALF, HALF)
    lane = iota(square, 1)
    fluid_pair = split(fluid)
    sums = [[0.0, 0.0], [0.0, 0.0]]
    counts = [0.0, 0.0]
    count_lanes = 0.0
    for i in range(2):
        ids = fluid[:, i * 64 + 32 : i * 64 + 33].astype(jnp.int32) - 1
        count_lanes = count_lanes + jnp.sum(jnp.where(ids == lane, 1.0, 0.0), axis=0, keepdims=True)
        for f in range(2):
            pick = hot_of(iota(square, 0) == i * 64 + f * 16 + lane % 16)
            values = dot(fluid_pair[0], pick) + dot(fluid_pair[1], pick)
            for xl in range(2):
                mask = ids == xl * 8 + lane // 16
                sums[f][xl] = sums[f][xl] + jnp.sum(
                    jnp.where(mask, values, 0.0), axis=0, keepdims=True
                )
                if f == 0:
                    counts[xl] = counts[xl] + jnp.sum(
                        jnp.where(mask, 1.0, 0.0), axis=0, keepdims=True
                    )
    heat = [sums[0][xl] - counts[xl] * surface_ref[xl : xl + 1, :] for xl in range(2)]
    tail = jnp.where(lane < 16, count_lanes, 0.0)
    for k in range(2):
        by_modes = split(sine_ref[pl.ds(group * N + k, HALF, 2), :])
        for xl in range(2):
            column = dot3(by_modes, jnp.broadcast_to(sums[1][xl], (8, HALF)), NT)[:, 0:1]
            tail = jnp.where(lane == 16 + 2 * k + xl, column, tail)
    shared = [surface_row[:, :HALF], surface_row[:, HALF:], heat[0], heat[1]]
    for r in range(4):
        out_ref[pl.ds(r, HALF, 5), :] = jnp.broadcast_to(shared[r], square)
    out_ref[pl.ds(4, HALF, 5), :] = tail


def solve_kernel(
    where_ref, rate_ref, got_ref, other_ref, modes_ref, response_ref, sine_ref, rate_row_ref,
    rate_col_ref, row_ref, column_ref, surface_ref, out_ref, heat_ref
):
    core, me = where_ref[1], where_ref[2]
    first = jnp.full((HALF, HALF), core, jnp.int32) == 0
    ordered = []
    for r in range(5):
        mine, theirs = rows(got_ref, r, HALF, 5), rows(other_ref, r, HALF, 5)
        ordered.append((jnp.where(first, mine, theirs), jnp.where(first, theirs, mine)))

    def block(g, r):
        return jnp.concatenate([ordered[r][k][g * 64 : (g + 1) * 64] for k in range(2)], axis=0)

    by_modes = mode_ordered(sine_ref)
    halves = [split(by_modes[:, g * HALF : (g + 1) * HALF]) for g in range(2)]
    by_x = x_ordered(sine_ref)
    heat_modes = 0.0
    for xl in range(2):
        by_y = 0.0
        for g in range(2):
            by_y = by_y + dot3(halves[g], block(g, 2 + xl), NT)
        at = slice(xl * HALF, (xl + 1) * HALF)
        heat_modes = heat_modes + dot3(by_y, (by_x[0][at], by_x[1][at]))
    heat_ref[...] = heat_modes
    given = jnp.concatenate(
        [jnp.concatenate([ordered[h][k] for h in range(2)], axis=1) for k in range(2)], axis=0
    )
    surface = dot3(split(by_modes.T), given + response_ref[...] * heat_modes)
    surface = dot3(surface, by_x, NT)
    surface_ref[...] = surface
    square = (HALF, HALF)
    tails = [block(g, 4) for g in range(2)]
    tail_pairs = [tail.astype(BF16) for tail in tails]
    expand = [hot_of(iota(square, 1) == xl * 8 + iota(square, 0) // 16) for xl in range(2)]
    count = jnp.concatenate(
        [
            jnp.concatenate([dot(expand[xl], tail_pairs[g], NT) for xl in range(2)], axis=1)
            for g in range(2)
        ],
        axis=0,
    )
    own_sine = jnp.broadcast_to(sine_rows(sine_ref, me, 1, 1), (8, N))
    reduced = dot3(own_sine, count * surface)
    tail_sum = tails[0] + tails[1]
    lane8 = iota((8, HALF), 1)
    later = jnp.concatenate(
        [hot_dot(hot_of(lane8 == 16 + 2 * core + xl), tail_sum, NT) for xl in range(2)], axis=1
    )
    heat1 = dot3(later - 0.7 * reduced, by_x)[0:1]
    heat0 = heat_ref[pl.ds(core * HALF + me // 2, 1), :]
    decay = 1.0 / (rate_col_ref[...] + (rate_row_ref[...] + 64.0 * rate_ref[me]))
    column = column_ref[...]
    final = decay * (decay * (modes_ref[...] + column * heat0) + column * heat1)
    final_row = dot3(row_ref[...], final)[0:1]
    final = split(final)
    sine = split(sine_rows(sine_ref, 0, N, 1))
    for xl in range(2):
        back = dot3(dot3(sine_rows(sine_ref, xl, HALF, 2), final, NT), sine)
        for g in range(2):
            for h in range(2):
                out_ref[pl.ds(g * 768 + 2 * xl + h, HALF, 6), :] = back[:, h * HALF : (h + 1) * HALF]
    for h in range(2):
        out_ref[pl.ds(4 + h, N, 6), :] = jnp.broadcast_to(
            final_row[:, h * HALF : (h + 1) * HALF], (N, HALF)
        )


def met_values(surface, owner, patch):
    x_of_slot = patch // 8 * HALF + owner % 2 * 64 + owner // 2
    x_hot = hot_of(iota((N, HALF), 0) == x_of_slot)
    met = dot_hot(surface, x_hot)
    return jnp.where(iota((HALF, HALF), 0) // 16 == patch % 8, met, 0.0)


def folded(met):
    fold = hot_of(iota((16, HALF), 0) == iota((16, HALF), 1) % 16)
    return hot_dot(fold, met)


def stepped(extended, matrix_ref):
    fluid = split(extended)
    width = extended.shape[1]
    own, following, preceding = [
        dot3(matrix_ref[pl.ds(320 * i, 320), :], fluid) for i in range(3)
    ]
    return own + pltpu.roll(following, width - 1, 1) + pltpu.roll(preceding, 1, 1)


def step_kernel(where_ref, fluid_ref, matrix_ref, before_ref, after_ref, out_ref):
    count = fluid_ref.shape[1]
    me = where_ref[2]
    lane = iota((320, HALF), 1)
    following, preceding = after_ref[...].T[0:320], before_ref[...].T[0:320]
    halo = jnp.zeros((320, HALF), F32)
    for at, column in (
        (0, following[:, 0:1]),
        (1, following[:, 1:2]),
        (HALF - 1, preceding[:, 0:1]),
        (HALF - 2, preceding[:, 1:2]),
    ):
        halo = jnp.where(lane == at, column, halo)
    result = stepped(jnp.concatenate([fluid_ref[...], halo], axis=1), matrix_ref)
    edge = result[:, count:]
    beyond = ((lane == 0) & (me == 255)) | ((lane == HALF - 1) & (me == 0))
    out_ref[:, :count] = result[:, :count]
    out_ref[:, count:] = jnp.where(beyond, 0.0, edge)


def second_kernel(
    where_ref, fluid_ref, surface_ref, trace_ref, matrix_ref, before_ref, after_ref, elem_ref,
    owner_ref, patch_ref, out_ref, later_ref
):
    group, me = where_ref[0], where_ref[2]
    width = fluid_ref.shape[1]
    count = width - HALF
    own_surface = surface_ref[pl.ds(pl.multiple_of(group * HALF, HALF), HALF), :]
    elem_hot = hot_of(elem_ref[...] == iota((HALF, count), 1))
    met = folded(met_values(own_surface, owner_ref[...], patch_ref[...]))
    source = GAIN * dot_hot(met - trace_ref[...], elem_hot)
    square = (16, HALF)
    edge = jnp.zeros(square, F32)
    for ref, at, device in ((after_ref, 0, me + 1), (before_ref, HALF - 1, me - 1)):
        owner = ref[2:3, 0:1].astype(jnp.int32) - 1
        patch = ref[2:3, 1:2].astype(jnp.int32)
        side = jnp.clip(device, 0, 255) // HALF
        near = surface_ref[pl.ds(pl.multiple_of(side * HALF, HALF), HALF), :]
        lanes = jnp.zeros((1, HALF), jnp.int32)
        value = folded(met_values(near, owner + lanes, patch + lanes))
        column = ref[...].T
        value = GAIN * (value - (column[256:272, 0:1] - column[0:16, 0:1]))
        used = (iota(square, 1) == at) & (owner >= 0)
        edge = jnp.where(used, value, edge)
    walls = fluid_ref[256:272] + jnp.concatenate([source, edge], axis=1)
    later_ref[...] = dot_hot(walls[:, :count] - fluid_ref[0:16, :count], elem_hot, NT)
    extended = jnp.concatenate([fluid_ref[0:256], walls, fluid_ref[272:320]], axis=0)
    out_ref[...] = stepped(extended, matrix_ref)[:, :count]


def last_kernel(
    where_ref, got_ref, sine_ref, later_ref, elem_ref, owner_ref, patch_ref, fluid_ref,
    solid_ref, out_ref
):
    group = where_ref[0]
    by_y = split(sine_ref[pl.ds(pl.multiple_of(group * N, N), N), :])
    for xl in range(2):
        for h in range(2):
            part = rows(got_ref, 2 * xl + h, N, 6)
            solid_ref[pl.ds(h * N + xl, HALF, 2), :] = dot3(part, by_y, TN)
    given = jnp.concatenate([rows(got_ref, 4 + h, N, 6) for h in range(2)], axis=1)
    own_rows = sine_rows(sine_ref, pl.multiple_of(group * HALF, HALF), HALF, 1)
    surface = dot3(dot3(own_rows, given), x_ordered(sine_ref), NT)
    met = folded(met_values(surface, owner_ref[...], patch_ref[...]))
    elem_hot = hot_of(elem_ref[...] == iota((HALF, fluid_ref.shape[1]), 1))
    out_ref[...] = fluid_ref[...] + GAIN * dot_hot(met - later_ref[...], elem_hot)


def call(kernel, outs, args, scalars=0, scratch=(), aliases=None, specs=None, out_specs=None, cost=None):
    whole = pl.BlockSpec(memory_space=pltpu.VMEM)
    given = [pl.BlockSpec(memory_space=pltpu.SMEM)] * scalars + [whole] * (len(args) - scalars)
    return pl.pallas_call(
        kernel,
        out_shape=[jax.ShapeDtypeStruct(shape, F32) for shape in outs],
        in_specs=specs or given,
        out_specs=out_specs or [whole] * len(outs),
        scratch_shapes=list(scratch),
        input_output_aliases=aliases or {},
        cost_estimate=pl.CostEstimate(flops=int(cost or 1e8), bytes_accessed=1 << 20, transcendentals=0),
        compiler_params=pltpu.CompilerParams(vmem_limit_bytes=40 << 20),
    )(*args)


def exchange(payload, axes):
    chunks = payload.reshape(payload.shape[0], 1, HALF)
    return lax.all_to_all(chunks, axes, split_axis=0, concat_axis=0, tiled=True).reshape(payload.shape)


def on_device(fluid_state, flux_jacobian, solid_temp, iface_elem, iface_owner, iface_patch):
    me = lax.axis_index(ALL)
    where = jnp.stack([me // HALF, me % 2, me]).astype(jnp.int32)
    fluid0 = fluid_state.reshape(320, -1)
    count = fluid0.shape[1]
    solid = solid_temp.reshape(2 * N, HALF)
    elem = iface_elem[:, None]
    owner, patch = iface_owner.reshape(1, HALF), iface_patch[None, :]
    smem = pl.BlockSpec(memory_space=pltpu.SMEM)

    far = lax.ppermute(solid, "g", [(0, 1), (1, 0)])
    row_spec = pl.BlockSpec((1, HALF), lambda i: (0, 0))
    first, last = pl.pallas_call(
        functools.partial(edges_kernel, count=count),
        grid=(1,),
        out_shape=[jax.ShapeDtypeStruct((8, 384), F32)] * 2,
        in_specs=[
            pl.BlockSpec((320, HALF), lambda i: (0, 0)),
            pl.BlockSpec((320, HALF), lambda i: (0, count // HALF - 1)),
        ]
        + [row_spec] * 3,
        out_specs=[pl.BlockSpec((8, 384), lambda i: (0, 0))] * 2,
    )(fluid0, fluid0, iface_elem[None, :], owner, patch)
    before = lax.ppermute(last, ALL, [(i, i + 1) for i in range(255)])
    after = lax.ppermute(first, ALL, [(i + 1, i) for i in range(255)])
    walls, wall_matrix = pl.pallas_call(
        walls_kernel,
        grid=(4,),
        out_shape=[jax.ShapeDtypeStruct((64, count), F32), jax.ShapeDtypeStruct((48, 320), F32)],
        in_specs=[
            smem,
            pl.BlockSpec((320, count // 4), lambda i: (0, i)),
            pl.BlockSpec((8, 16, 320), lambda i: (0, 0, 0)),
        ],
        out_specs=[
            pl.BlockSpec((64, count // 4), lambda i: (0, i)),
            pl.BlockSpec((48, 320), lambda i: (0, 0)),
        ],
    )(flux_jacobian, fluid0, WALL_TABLES)
    pay1, trace0, surface0 = call(
        first_kernel,
        [(5 * HALF, HALF), (16, HALF), (2, HALF)],
        [where, solid, far, walls, wall_matrix, before, after, elem, iface_owner, owner, patch, Q_HALVES],
        scalars=1,
    )
    got1 = exchange(pay1, SUB)
    jacobian = jnp.pad(flux_jacobian, ((0, 0), (0, 3), (0, 3)))
    (matrix,) = call(
        matrices_kernel,
        [(960, 320)],
        [jacobian, FIELD_HOT, TILE_HOT, np.stack([FIXED, NEXT_FIXED, PREV_FIXED]), OPERATORS],
    )
    (fluid1,) = call(
        step_kernel,
        [(320, count + HALF)],
        [where, fluid0, matrix, before, after],
        scalars=1,
        cost=2e9,
    )
    modes, pay2 = call(
        modes_kernel,
        [(N, N), (5 * HALF, HALF)],
        [where, RATE_LIST, got1, surface0, Q_HALVES, RATE_ROW, RATE_COLUMN, SURFACE_ROW],
        scalars=2,
    )
    got2 = exchange(pay2, SAME_CORE)
    other = lax.ppermute(got2, "c", [(0, 1), (1, 0)])
    surface1, pay3 = call(
        solve_kernel,
        [(N, N), (6 * N, HALF)],
        [where, RATE_LIST, got2, other, modes, RESPONSE, Q_HALVES, RATE_ROW, RATE_COLUMN, SURFACE_ROW,
         SURFACE_COLUMN],
        scalars=2,
        scratch=[pltpu.VMEM((N, N), F32)],
    )
    got3 = exchange(pay3, ALL)
    fluid2, trace1 = call(
        second_kernel,
        [(320, count), (16, HALF)],
        [where, fluid1, surface1, trace0, matrix, before, after, elem, owner, patch],
        scalars=1,
        cost=2e9,
    )
    solid_out, fluid2 = pl.pallas_call(
        last_kernel,
        grid=(1,),
        out_shape=[
            jax.ShapeDtypeStruct((2 * N, HALF), F32),
            jax.ShapeDtypeStruct((320, count), F32),
        ],
        in_specs=[smem]
        + [pl.BlockSpec(memory_space=pltpu.VMEM)] * 6
        + [pl.BlockSpec((16, count), lambda i: (16, 0))],
        out_specs=[
            pl.BlockSpec((2 * N, HALF), lambda i: (0, 0)),
            pl.BlockSpec((16, count), lambda i: (16, 0)),
        ],
        input_output_aliases={7: 1},
        compiler_params=pltpu.CompilerParams(vmem_limit_bytes=40 << 20),
    )(where, got3, Q_HALVES, trace1, elem, owner, patch, fluid2)
    return fluid2.reshape(fluid_state.shape), solid_out.reshape(solid_temp.shape)


def solution(mesh):
    fine = Mesh(mesh.devices.reshape(2, 2, 4, 8, 2), ALL)
    placed = (
        P(None, None, ALL),
        P(),
        P(None, SUB, "g"),
        P(ALL),
        P(ALL, None),
        P(ALL),
    )
    return jax.shard_map(
        on_device,
        mesh=fine,
        in_specs=placed,
        out_specs=(P(None, None, ALL), P(None, SUB, "g")),
        check_vma=False,
    )
```

```python
import functools

import jax
import jax.numpy as jnp
import ml_dtypes
import numpy as np
from jax import lax
from jax.experimental import pallas as pl
from jax.experimental.pallas import tpu as pltpu
from jax.sharding import Mesh, PartitionSpec as P

ALL = ("g", "yl", "x", "z", "c")
SUB = ("yl", "x", "z", "c")
SAME_CORE = ("g", "yl", "x", "z")
N = 256
HALF = 128
DT = 0.05
VISC = 0.05
GAIN = 0.3
F32 = jnp.float32
BF16 = jnp.bfloat16
NN = ((1,), (0,))
NT = ((1,), (1,))
TN = ((0,), (0,))


def sine_table(length):
    numbers = np.arange(length) + 1
    phases = numbers[:, None] * numbers[None, :] % (2 * (length + 1))
    return np.sqrt(2.0 / (length + 1)) * np.sin(np.pi * phases / (length + 1))


def rates(length):
    return 2.0 - 2.0 * np.cos(np.pi * (np.arange(length) + 1) / (length + 1))


SINE = sine_table(N)
RATES = rates(N)
MODE_ORDER = np.array([2 * q + k for k in range(2) for q in range(HALF)])


def surface_response():
    total = np.zeros((N, N))
    for c in range(N):
        total += SINE[0, c] ** 2 / (1.0 + 64.0 * (RATES[c] + RATES[:, None] + RATES[None, :]))
    return total


Q = SINE.astype(np.float32)
Q_HALVES = np.concatenate([Q[:, :HALF], Q[:, HALF:]], axis=0)
RESPONSE = surface_response()[MODE_ORDER].astype(np.float32)


def lobatto_derivative():
    points = np.array([-1.0, -1.0 / np.sqrt(5.0), 1.0 / np.sqrt(5.0), 1.0])
    weights = np.array(
        [1.0 / np.prod([points[j] - points[k] for k in range(4) if k != j]) for j in range(4)]
    )
    deriv = np.zeros((4, 4))
    for i in range(4):
        for j in range(4):
            if i != j:
                deriv[i, j] = weights[j] / weights[i] / (points[i] - points[j])
        deriv[i, i] = -np.sum(deriv[i])
    return deriv


def operator_parts():
    deriv, eye = lobatto_derivative(), np.eye(4)
    along = [
        np.kron(eye, np.kron(eye, deriv)),
        np.kron(eye, np.kron(deriv, eye)),
        np.kron(deriv, np.kron(eye, eye)),
    ]
    second = sum(d @ d for d in along)
    pick = np.zeros((4, 4, 4, 4))
    for i in range(4):
        for j in range(4):
            pick[i, j, i, j] = 1.0
    eye16 = np.eye(16)
    right, left = np.kron(eye16, pick[3, 3]), np.kron(eye16, pick[0, 0])
    right_from, left_from = np.kron(eye16, pick[3, 0]), np.kron(eye16, pick[0, 3])
    fixed = np.kron(np.eye(5), np.eye(64) - 0.15 * right - 0.15 * left)
    fixed = fixed + DT * VISC * np.kron(np.diag([0.0, 1.0, 1.0, 1.0, 1.0]), second)
    by_x = -DT * along[0] + 0.15 * right - 0.15 * left
    return [
        np.asarray(a, np.float32)
        for a in (
            fixed,
            by_x,
            -DT * along[1],
            -DT * along[2],
            np.kron(np.eye(5), 0.15 * right_from),
            -0.15 * right_from,
            np.kron(np.eye(5), 0.15 * left_from),
            0.15 * left_from,
        )
    ]


FIXED, BY_X, BY_Y, BY_Z, NEXT_FIXED, NEXT_X, PREV_FIXED, PREV_X = operator_parts()


def wall_tables():
    groups = []
    for fixed, tables in ((FIXED, (BY_X, BY_Y, BY_Z)), (NEXT_FIXED, (NEXT_X,)), (PREV_FIXED, (PREV_X,))):
        groups.append(fixed[256:272] - fixed[0:16])
        groups += [np.tile(t[:16], (1, 5)) for t in tables]
    return np.stack(groups).astype(np.float32)


WALL_TABLES = wall_tables()
RATE_LIST = RATES.astype(np.float32)
RATE_ROW = (1.0 + 64.0 * RATES)[None, :].astype(np.float32)
RATE_COLUMN = (64.0 * RATES)[:, None].astype(np.float32)
SURFACE_ROW = np.broadcast_to(Q[:1], (8, N)).copy()
SURFACE_COLUMN = Q[:, :1].copy()
FIELD_HOT = np.pad(np.kron(np.eye(5), np.ones((64, 1))), ((0, 0), (0, 3))).astype(ml_dtypes.bfloat16)
TILE_HOT = np.kron(np.ones((5, 1)), np.eye(64)).astype(ml_dtypes.bfloat16)
OPERATORS = np.stack([BY_X, BY_Y, BY_Z, NEXT_X, PREV_X])


def split(value):
    high = value.astype(BF16)
    return high, (value - high.astype(F32)).astype(BF16)


def dot(a, b, dims=NN):
    return lax.dot_general(a, b, (dims, ((), ())), preferred_element_type=F32)


def dot3(a, b, dims=NN):
    a = split(a) if not isinstance(a, tuple) else a
    b = split(b) if not isinstance(b, tuple) else b
    return dot(a[0], b[0], dims) + (dot(a[0], b[1], dims) + dot(a[1], b[0], dims))


def hot_dot(hot, b, dims=NN):
    high, low = split(b)
    return dot(hot, high, dims) + dot(hot, low, dims)


def dot_hot(a, hot, dims=NN):
    high, low = split(a)
    return dot(high, hot, dims) + dot(low, hot, dims)


def hot_of(condition):
    return jnp.where(condition, 1.0, 0.0).astype(BF16)


def iota(shape, dim):
    return lax.broadcasted_iota(jnp.int32, shape, dim)


def rows(ref, first, count, stride):
    return ref[pl.ds(first, count, stride) if stride > 1 else pl.ds(first, count), :]


def sine_rows(ref, first, count, stride):
    return jnp.concatenate([rows(ref, h * N + first, count, stride) for h in range(2)], axis=1)


def x_ordered(sine_ref):
    blocks = [sine_rows(sine_ref, 2 * k + i, 64, 4) for i in range(2) for k in range(2)]
    return split(jnp.concatenate(blocks, axis=0))


def mode_ordered(sine_ref):
    return jnp.concatenate([sine_rows(sine_ref, k, HALF, 2) for k in range(2)], axis=0)


def column_of(row):
    return jnp.broadcast_to(row.astype(F32), (8, row.shape[1])).T[:, 0:1].astype(jnp.int32)


def near_kernel(
    where_ref, jac_hbm, fluid_hbm, solid_hbm, sine_hbm, table_ref, elem_ref, owner_ref, patch_ref,
    out_ref, trace_ref, surface_ref, first_ref, last_ref, matrix_ref, far_table_ref,
    jac_ref, fluid_ref, solid_ref, sine_ref, sems
):
    group = where_ref[0]
    count = fluid_ref.shape[1]
    copies = [
        pltpu.make_async_copy(jac_hbm, jac_ref, sems.at[0]),
        pltpu.make_async_copy(solid_hbm, solid_ref, sems.at[1]),
        pltpu.make_async_copy(sine_hbm, sine_ref, sems.at[2]),
    ]
    for i in range(5):
        at = pl.ds(64 * i, 64)
        copies.append(pltpu.make_async_copy(fluid_hbm.at[at, :], fluid_ref.at[at, :], sems.at[3 + i]))
    for copy in copies:
        copy.start()
    for copy in copies[:3]:
        copy.wait()

    near, far = [
        sine_ref[pl.ds(pl.multiple_of(half * N + group * HALF, HALF), HALF), :]
        for half in (group, 1 - group)
    ]
    far_table_ref[...] = far
    near = split(near)
    for i in range(2):
        modes = dot3(near, rows(solid_ref, i, N, 2), NT)
        for h in range(2):
            out_ref[pl.ds(2 * i + h, HALF, 5), :] = modes[:, h * HALF : (h + 1) * HALF]
    surface_ref[...] = solid_ref[0:2]

    field = iota((1, 320), 1) // 64
    coefficients = []
    for d in range(3):
        change = jac_ref[d, 4:5, :] - jac_ref[d, 0:1, :]
        row = jnp.zeros((1, 320), F32)
        for f in range(5):
            row = jnp.where(field == f, change[:, f : f + 1], row)
        coefficients.append(row)
    own = table_ref[0]
    for d in range(3):
        own = own + coefficients[d] * table_ref[1 + d]
    matrix_ref[0:16] = own
    matrix_ref[16:32] = table_ref[4] + coefficients[0] * table_ref[5]
    matrix_ref[32:48] = table_ref[6] + coefficients[0] * table_ref[7]

    owner, patch, elem = owner_ref[...], patch_ref[...], elem_ref[...]
    square = (HALF, HALF)
    same = (column_of(owner) == owner) & (iota(square, 0) < iota(square, 1))
    place = jnp.sum(jnp.where(same, 1.0, 0.0), axis=0, keepdims=True)
    elem_hot = hot_of(column_of(elem) == iota((HALF, count), 1))

    for copy in copies[3:]:
        copy.wait()
    lane = iota((1, 384), 1)
    gap = jnp.zeros((1, 64), F32)
    for block, at, out, element in (
        (fluid_ref[:, 0:HALF], (0, 1), first_ref, 0),
        (fluid_ref[:, count - HALF : count], (HALF - 1, HALF - 2), last_ref, count - 1),
    ):
        turned = block.T
        met = elem == element
        edge_owner = jnp.sum(jnp.where(met, owner + 1, 0).astype(F32), axis=1, keepdims=True)
        edge_patch = jnp.sum(jnp.where(met, patch, 0).astype(F32), axis=1, keepdims=True)
        out[0:1] = jnp.concatenate([turned[at[0] : at[0] + 1], gap], axis=1)
        out[1:2] = jnp.concatenate([turned[at[1] : at[1] + 1], gap], axis=1)
        out[2:3] = jnp.where(lane == 0, edge_owner, jnp.where(lane == 1, edge_patch, 0.0))
        out[3:8] = jnp.zeros((5, 384), F32)

    walls = dot3(matrix_ref[...], fluid_ref[...])
    wall0 = fluid_ref[256:272] - fluid_ref[0:16]
    lane = iota(wall0.shape, 1)
    following = pltpu.roll(walls[16:32], count - 1, 1)
    preceding = pltpu.roll(walls[32:48], 1, 1)
    later = walls[0:16] + jnp.where(lane == count - 1, 0.0, following)
    later = later + jnp.where(lane == 0, 0.0, preceding)
    values = dot_hot(jnp.concatenate([wall0, later - GAIN * wall0], axis=0), elem_hot, NT)
    trace_ref[...] = values[:16]
    ids = jnp.broadcast_to((patch + 1).astype(F32), (8, HALF))
    filler = jnp.zeros((24, HALF), F32)
    sent = jnp.concatenate([values, ids, filler], axis=0)
    none = jnp.zeros((64, HALF), F32)
    arranged = 0.0
    for i in range(2):
        hot = hot_of((iota(square, 0) == owner) & (place == float(i)))
        padded = jnp.concatenate([sent, none] if i == 0 else [none, sent], axis=0)
        arranged = arranged + hot_dot(hot, padded, NT)
    out_ref[pl.ds(4, HALF, 5), :] = arranged


def far_kernel(far_ref, table_ref, near_ref, out_ref):
    table = split(table_ref[...])
    out_ref[pl.ds(4, HALF, 5), :] = rows(near_ref, 4, HALF, 5)
    for i in range(2):
        modes = dot3(table, rows(far_ref, i, N, 2), NT)
        for h in range(2):
            part = modes[:, h * HALF : (h + 1) * HALF]
            out_ref[pl.ds(2 * i + h, HALF, 5), :] = rows(near_ref, 2 * i + h, HALF, 5) + part


def tables_kernel(
    where_ref, rate_ref, sine_ref, rate_row_ref, rate_col_ref, order_ref,
    sine_out, x_out, modes_out, modes_t_out, split_out, decay_out
):
    del order_ref
    by_modes = mode_ordered(sine_ref)
    for out, table in (
        (sine_out, split(sine_rows(sine_ref, 0, N, 1))),
        (x_out, x_ordered(sine_ref)),
        (modes_out, split(by_modes)),
        (modes_t_out, split(by_modes.T)),
    ):
        out[0], out[1] = table
    for i in range(2):
        split_out[2 * i], split_out[2 * i + 1] = split(sine_rows(sine_ref, i, HALF, 2))
    decay_out[...] = 1.0 / (rate_col_ref[...] + (rate_row_ref[...] + 64.0 * rate_ref[where_ref[2]]))


def matrices_kernel(jac_ref, field_ref, tile_ref, fixed_ref, operators_ref, out_ref):
    field, tile = field_ref[...], tile_ref[...]

    def spread(d):
        return dot_hot(hot_dot(field, jac_ref[d]), field, NT)

    def tiled(d):
        return dot_hot(hot_dot(tile, operators_ref[d]), tile, NT)

    by_x = spread(0)
    own = by_x * tiled(0) + spread(1) * tiled(1) + spread(2) * tiled(2)
    out_ref[0:320] = fixed_ref[0] + own
    out_ref[320:640] = fixed_ref[1] + by_x * tiled(3)
    out_ref[640:960] = fixed_ref[2] + by_x * tiled(4)


def modes_kernel(
    where_ref, got_ref, surface_ref, sine_ref, split_ref, by_modes_ref, decay_ref, row_ref,
    matrix_ref, before_ref, after_ref, elem_ref, owner_ref, patch_ref, modes_ref, out_ref, *, count
):
    group = where_ref[0]
    sine = sine_ref[0], sine_ref[1]
    modes = 0.0
    for i in range(2):
        part = jnp.concatenate([rows(got_ref, 2 * i + h, HALF, 5) for h in range(2)], axis=1)
        by_z = dot3(sine, part, NT)
        modes = modes + dot3(by_z, (split_ref[2 * i], split_ref[2 * i + 1]))
    modes_ref[...] = modes
    surface_row = dot3(row_ref[...], decay_ref[...] * modes)[0:1]

    fluid = rows(got_ref, 4, HALF, 5)
    square = (HALF, HALF)
    lane = iota(square, 1)
    fluid_pair = split(fluid)
    sums = [[0.0, 0.0], [0.0, 0.0]]
    counts = [0.0, 0.0]
    count_lanes = 0.0
    for i in range(2):
        ids = fluid[:, i * 64 + 32 : i * 64 + 33].astype(jnp.int32) - 1
        count_lanes = count_lanes + jnp.sum(jnp.where(ids == lane, 1.0, 0.0), axis=0, keepdims=True)
        for f in range(2):
            pick = hot_of(iota(square, 0) == i * 64 + f * 16 + lane % 16)
            values = dot(fluid_pair[0], pick) + dot(fluid_pair[1], pick)
            for xl in range(2):
                mask = ids == xl * 8 + lane // 16
                sums[f][xl] = sums[f][xl] + jnp.sum(
                    jnp.where(mask, values, 0.0), axis=0, keepdims=True
                )
                if f == 0:
                    counts[xl] = counts[xl] + jnp.sum(
                        jnp.where(mask, 1.0, 0.0), axis=0, keepdims=True
                    )
    heat = [sums[0][xl] - counts[xl] * surface_ref[xl : xl + 1, :] for xl in range(2)]
    tail = jnp.where(lane < 16, count_lanes, 0.0)
    edge_rows = []
    for t, (part, ref, element) in enumerate(((2, before_ref, 0), (1, after_ref, count - 1))):
        met = elem_ref[...] == element
        owner, patch = [
            jnp.sum(jnp.where(met, value, 0).astype(F32), axis=1, keepdims=True).astype(jnp.int32)
            for value in (owner_ref[...] + 1, patch_ref[...])
        ]
        x_of_slot = patch // 8 * HALF + (owner - 1) % 2 * 64 + (owner - 1) // 2
        tail = jnp.where(lane == 40 + t, jnp.where(owner > 0, x_of_slot + 1, 0).astype(F32), tail)
        tables = matrix_ref[16 * part : 16 * part + 16]
        column = jnp.sum(tables * ref[0:1, 0:320], axis=1, keepdims=True)
        node, lane16 = iota((16, HALF), 0), iota((16, HALF), 1)
        used = (lane16 % 16 == node) & (lane16 // 16 == patch % 8)
        edge_rows.append(jnp.sum(jnp.where(used, column, 0.0), axis=0, keepdims=True))
    for k in range(2):
        by_modes = []
        for part in range(2):
            table = by_modes_ref[part, k * HALF : (k + 1) * HALF, :].astype(F32)
            own = jnp.where(group == 0, table[:, :HALF], table[:, HALF:])
            by_modes.append(own.astype(BF16))
        by_modes = tuple(by_modes)
        for xl in range(2):
            column = dot3(by_modes, jnp.broadcast_to(sums[1][xl], (8, HALF)), NT)[:, 0:1]
            tail = jnp.where(lane == 16 + 2 * k + xl, column, tail)
        for t in range(2):
            column = dot3(by_modes, jnp.broadcast_to(edge_rows[t], (8, HALF)), NT)[:, 0:1]
            tail = jnp.where(lane == 32 + 2 * t + k, column, tail)
    shared = [surface_row[:, :HALF], surface_row[:, HALF:], heat[0], heat[1]]
    for r in range(4):
        out_ref[pl.ds(r, HALF, 5), :] = jnp.broadcast_to(shared[r], square)
    out_ref[pl.ds(4, HALF, 5), :] = tail


def solve_kernel(
    where_ref, got_ref, other_ref, modes_ref, response_ref, sine_ref, pair_ref, x_ref, by_modes_ref,
    from_modes_ref, split_ref, decay_ref, row_ref, column_ref, surface_ref, out_ref, heat_ref
):
    core, me = where_ref[1], where_ref[2]
    first = jnp.full((HALF, HALF), core, jnp.int32) == 0
    ordered = []
    for r in range(5):
        mine, theirs = rows(got_ref, r, HALF, 5), rows(other_ref, r, HALF, 5)
        ordered.append((jnp.where(first, mine, theirs), jnp.where(first, theirs, mine)))

    def block(g, r):
        return jnp.concatenate([ordered[r][k][g * 64 : (g + 1) * 64] for k in range(2)], axis=0)

    halves = [
        tuple(by_modes_ref[part, :, g * HALF : (g + 1) * HALF] for part in range(2))
        for g in range(2)
    ]
    by_x = x_ref[0], x_ref[1]
    heat_modes = 0.0
    for xl in range(2):
        by_y = 0.0
        for g in range(2):
            by_y = by_y + dot3(halves[g], block(g, 2 + xl), NT)
        at = slice(xl * HALF, (xl + 1) * HALF)
        heat_modes = heat_modes + dot3(by_y, (by_x[0][at], by_x[1][at]))
    heat_ref[...] = heat_modes
    given = jnp.concatenate(
        [jnp.concatenate([ordered[h][k] for h in range(2)], axis=1) for k in range(2)], axis=0
    )
    surface = dot3((from_modes_ref[0], from_modes_ref[1]), given + response_ref[...] * heat_modes)
    surface = dot3(surface, by_x, NT)
    surface_ref[...] = surface
    square = (HALF, HALF)
    tails = [block(g, 4) for g in range(2)]
    tail_pairs = [tail.astype(BF16) for tail in tails]
    expand = [hot_of(iota(square, 1) == xl * 8 + iota(square, 0) // 16) for xl in range(2)]
    count = jnp.concatenate(
        [
            jnp.concatenate([dot(expand[xl], tail_pairs[g], NT) for xl in range(2)], axis=1)
            for g in range(2)
        ],
        axis=0,
    )
    own_sine = jnp.broadcast_to(sine_rows(sine_ref, me, 1, 1), (8, N))
    reduced = dot3(own_sine, count * surface)
    tail_sum = tails[0] + tails[1]
    lane8 = iota((8, HALF), 1)
    later = jnp.concatenate(
        [hot_dot(hot_of(lane8 == 16 + 2 * core + xl), tail_sum, NT) for xl in range(2)], axis=1
    )
    wide = iota((HALF, N), 1)
    for k in range(2):
        tail = ordered[4][k]
        for t in range(2):
            value = jnp.where(first[:, 0:1], tail[:, 32 + 2 * t : 33 + 2 * t], tail[:, 33 + 2 * t : 34 + 2 * t])
            met = tail[:, 40 + t : 41 + t].astype(jnp.int32) - 1 == wide
            later = later + jnp.sum(jnp.where(met, value, 0.0), axis=0, keepdims=True)
    heat1 = dot3(later - 0.7 * reduced, by_x)[0:1]
    heat0 = heat_ref[pl.ds(core * HALF + me // 2, 1), :]
    decay = decay_ref[...]
    column = column_ref[...]
    final = decay * (decay * (modes_ref[...] + column * heat0) + column * heat1)
    final_row = dot3(row_ref[...], final)[0:1]
    final = split(final)
    sine = pair_ref[0], pair_ref[1]
    for xl in range(2):
        back = dot3(dot3((split_ref[2 * xl], split_ref[2 * xl + 1]), final, NT), sine)
        for g in range(2):
            for h in range(2):
                out_ref[pl.ds(g * 640 + 2 * xl + h, HALF, 5), :] = back[:, h * HALF : (h + 1) * HALF]
    for k in range(2):
        out_ref[pl.ds(4 + 5 * k, HALF, 10), :] = jnp.broadcast_to(
            final_row[:, k * HALF : (k + 1) * HALF], (HALF, HALF)
        )


def met_values(surface, owner, patch):
    x_of_slot = patch // 8 * HALF + owner % 2 * 64 + owner // 2
    x_hot = hot_of(iota((N, HALF), 0) == x_of_slot)
    met = dot_hot(surface, x_hot)
    return jnp.where(iota((HALF, HALF), 0) // 16 == patch % 8, met, 0.0)


def folded(met):
    fold = hot_of(iota((16, HALF), 0) == iota((16, HALF), 1) % 16)
    return hot_dot(fold, met)


def stepped(extended, matrix_ref):
    fluid = split(extended)
    width = extended.shape[1]
    own, following, preceding = [
        dot3(matrix_ref[pl.ds(320 * i, 320), :], fluid) for i in range(3)
    ]
    return own + pltpu.roll(following, width - 1, 1) + pltpu.roll(preceding, 1, 1)


def step_kernel(where_ref, fluid_ref, matrix_ref, before_ref, after_ref, out_ref):
    count = fluid_ref.shape[1]
    me = where_ref[2]
    lane = iota((320, HALF), 1)
    following, preceding = after_ref[...].T[0:320], before_ref[...].T[0:320]
    halo = jnp.zeros((320, HALF), F32)
    for at, column in (
        (0, following[:, 0:1]),
        (1, following[:, 1:2]),
        (HALF - 1, preceding[:, 0:1]),
        (HALF - 2, preceding[:, 1:2]),
    ):
        halo = jnp.where(lane == at, column, halo)
    result = stepped(jnp.concatenate([fluid_ref[...], halo], axis=1), matrix_ref)
    edge = result[:, count:]
    beyond = ((lane == 0) & (me == 255)) | ((lane == HALF - 1) & (me == 0))
    out_ref[:, :count] = result[:, :count]
    out_ref[:, count:] = jnp.where(beyond, 0.0, edge)


def second_kernel(
    where_ref, fluid_ref, surface_ref, trace_ref, matrix_ref, before_ref, after_ref, elem_ref,
    owner_ref, patch_ref, sine_ref, out_ref, later_ref, slots_ref
):
    group, me = where_ref[0], where_ref[2]
    width = fluid_ref.shape[1]
    count = width - HALF
    own_surface = surface_ref[pl.ds(pl.multiple_of(group * HALF, HALF), HALF), :]
    elem_hot = hot_of(column_of(elem_ref[...]) == iota((HALF, count), 1))
    met = folded(met_values(own_surface, owner_ref[...], patch_ref[...]))
    source = GAIN * dot_hot(met - trace_ref[...], elem_hot)
    square = (16, HALF)
    edge = jnp.zeros(square, F32)
    for ref, at, device in ((after_ref, 0, me + 1), (before_ref, HALF - 1, me - 1)):
        owner = ref[2:3, 0:1].astype(jnp.int32) - 1
        patch = ref[2:3, 1:2].astype(jnp.int32)
        side = jnp.clip(device, 0, 255) // HALF
        near = surface_ref[pl.ds(pl.multiple_of(side * HALF, HALF), HALF), :]
        lanes = jnp.zeros((1, HALF), jnp.int32)
        value = folded(met_values(near, owner + lanes, patch + lanes))
        column = ref[...].T
        value = GAIN * (value - (column[256:272, 0:1] - column[0:16, 0:1]))
        used = (iota(square, 1) == at) & (owner >= 0)
        edge = jnp.where(used, value, edge)
    slot_hot = hot_of(iota((N, HALF), 0) == 2 * owner_ref[...] + patch_ref[...] // 8)
    slots_ref[...] = dot_hot(sine_rows(sine_ref, 0, N, 1), slot_hot)
    walls = fluid_ref[256:272] + jnp.concatenate([source, edge], axis=1)
    later_ref[...] = dot_hot(walls[:, :count] - fluid_ref[0:16, :count], elem_hot, NT)
    extended = jnp.concatenate([fluid_ref[0:256], walls, fluid_ref[272:320]], axis=0)
    out_ref[...] = stepped(extended, matrix_ref)[:, :count]


def solid_kernel(where_ref, got_ref, sine_ref, solid_ref):
    by_y = split(sine_ref[pl.ds(pl.multiple_of(where_ref[0] * N, N), N), :])
    for xl in range(2):
        for h in range(2):
            part = rows(got_ref, 2 * xl + h, N, 5)
            solid_ref[pl.ds(h * N + xl, HALF, 2), :] = dot3(part, by_y, TN)


def last_kernel(
    where_ref, mine_ref, other_ref, sine_ref, slots_ref, later_ref, elem_ref, patch_ref, fluid_ref,
    out_ref
):
    group, core = where_ref[0], where_ref[1]
    first = jnp.full((N, HALF), core, jnp.int32) == 0
    mine, other = mine_ref[...], other_ref[...]
    given = jnp.concatenate([jnp.where(first, mine, other), jnp.where(first, other, mine)], axis=1)
    own_rows = sine_rows(sine_ref, pl.multiple_of(group * HALF, HALF), HALF, 1)
    met = dot3(own_rows, dot3(given, slots_ref[...]))
    met = folded(jnp.where(iota((HALF, HALF), 0) // 16 == patch_ref[...] % 8, met, 0.0))
    elem_hot = hot_of(column_of(elem_ref[...]) == iota((HALF, fluid_ref.shape[1]), 1))
    out_ref[...] = fluid_ref[...] + GAIN * dot_hot(met - later_ref[...], elem_hot)


def call(kernel, outs, args, scalars=0, scratch=(), aliases=None, specs=None, out_specs=None, cost=None):
    whole = pl.BlockSpec(memory_space=pltpu.VMEM)
    given = [pl.BlockSpec(memory_space=pltpu.SMEM)] * scalars + [whole] * (len(args) - scalars)
    return pl.pallas_call(
        kernel,
        out_shape=[
            jax.ShapeDtypeStruct(*(out if isinstance(out[0], tuple) else (out, F32))) for out in outs
        ],
        in_specs=specs or given,
        out_specs=out_specs or [whole] * len(outs),
        scratch_shapes=list(scratch),
        input_output_aliases=aliases or {},
        cost_estimate=pl.CostEstimate(flops=int(cost or 1e8), bytes_accessed=1 << 20, transcendentals=0),
        compiler_params=pltpu.CompilerParams(vmem_limit_bytes=40 << 20),
    )(*args)


def exchange(payload, axes):
    chunks = payload.reshape(payload.shape[0], 1, HALF)
    return lax.all_to_all(chunks, axes, split_axis=0, concat_axis=0, tiled=True).reshape(payload.shape)


def on_device(fluid_state, flux_jacobian, solid_temp, iface_elem, iface_owner, iface_patch):
    me = lax.axis_index(ALL)
    where = jnp.stack([me // HALF, me % 2, me]).astype(jnp.int32)
    fluid0 = fluid_state.reshape(320, -1)
    count = fluid0.shape[1]
    solid = solid_temp.reshape(2 * N, HALF)
    elem, owner, patch = iface_elem[None, :], iface_owner.reshape(1, HALF), iface_patch[None, :]
    smem = pl.BlockSpec(memory_space=pltpu.SMEM)
    vmem = pl.BlockSpec(memory_space=pltpu.VMEM)
    anywhere = pl.BlockSpec(memory_space=pl.ANY)

    far = lax.ppermute(solid, "g", [(0, 1), (1, 0)])
    near, trace0, surface0, first, last, wall_matrix, far_table = call(
        near_kernel,
        [(5 * HALF, HALF), (16, HALF), (2, HALF), (8, 384), (8, 384), (48, 320), (HALF, HALF)],
        [where, flux_jacobian, fluid0, solid, Q_HALVES, WALL_TABLES, elem, owner, patch],
        specs=[smem] + [anywhere] * 4 + [vmem] * 4,
        scratch=[
            pltpu.VMEM(flux_jacobian.shape, F32),
            pltpu.VMEM(fluid0.shape, F32),
            pltpu.VMEM(solid.shape, F32),
            pltpu.VMEM(Q_HALVES.shape, F32),
            pltpu.SemaphoreType.DMA((8,)),
        ],
    )
    before = lax.ppermute(last, ALL, [(i, i + 1) for i in range(255)])
    after = lax.ppermute(first, ALL, [(i + 1, i) for i in range(255)])
    (pay1,) = call(far_kernel, [(5 * HALF, HALF)], [far, far_table, near])
    got1 = exchange(pay1, SUB)
    tables = call(
        tables_kernel,
        [((2, N, N), BF16)] * 4 + [((4, HALF, N), BF16), (N, N)],
        [where, RATE_LIST, Q_HALVES, RATE_ROW, RATE_COLUMN, surface0],
        scalars=2,
    )
    sine_pair, x_pair, modes_pair, modes_t_pair, split_pair, decay = tables
    jacobian = jnp.pad(flux_jacobian, ((0, 0), (0, 3), (0, 3)))
    (matrix,) = call(
        matrices_kernel,
        [(960, 320)],
        [jacobian, FIELD_HOT, TILE_HOT, np.stack([FIXED, NEXT_FIXED, PREV_FIXED]), OPERATORS],
    )
    (fluid1,) = call(
        step_kernel,
        [(320, count + HALF)],
        [where, fluid0, matrix, before, after],
        scalars=1,
        cost=2e9,
    )
    modes, pay2 = call(
        functools.partial(modes_kernel, count=count),
        [(N, N), (5 * HALF, HALF)],
        [where, got1, surface0, sine_pair, split_pair, modes_pair, decay, SURFACE_ROW,
         wall_matrix, before, after, elem, owner, patch],
        scalars=1,
    )
    got2 = exchange(pay2, SAME_CORE)
    other = lax.ppermute(got2, "c", [(0, 1), (1, 0)])
    surface1, pay3 = call(
        solve_kernel,
        [(N, N), (5 * N, HALF)],
        [where, got2, other, modes, RESPONSE, Q_HALVES, sine_pair, x_pair, modes_pair, modes_t_pair,
         split_pair, decay, SURFACE_ROW, SURFACE_COLUMN],
        scalars=1,
        scratch=[pltpu.VMEM((N, N), F32)],
    )
    got3 = exchange(pay3, ALL)
    fluid2, trace1, slots = call(
        second_kernel,
        [(320, count), (16, HALF), (N, HALF)],
        [where, fluid1, surface1, trace0, matrix, before, after, elem, owner, patch, Q_HALVES],
        scalars=1,
        cost=2e9,
    )
    got3, fluid2, trace1, slots = lax.optimization_barrier((got3, fluid2, trace1, slots))
    mine = got3.reshape(N, 5, 1, HALF)[:, 4].reshape(N, HALF)
    far_row = lax.ppermute(mine, "c", [(0, 1), (1, 0)])
    (solid_out,) = call(solid_kernel, [(2 * N, HALF)], [where, got3, Q_HALVES], scalars=1)
    walls_spec = pl.BlockSpec((16, count), lambda i: (16, 0))
    (fluid2,) = pl.pallas_call(
        last_kernel,
        grid=(1,),
        out_shape=[jax.ShapeDtypeStruct((320, count), F32)],
        in_specs=[smem] + [vmem] * 7 + [walls_spec],
        out_specs=[walls_spec],
        input_output_aliases={8: 0},
        compiler_params=pltpu.CompilerParams(vmem_limit_bytes=40 << 20),
    )(where, mine, far_row, Q_HALVES, slots, trace1, elem, patch, fluid2)
    return fluid2.reshape(fluid_state.shape), solid_out.reshape(solid_temp.shape)


def solution(mesh):
    fine = Mesh(mesh.devices.reshape(2, 2, 4, 8, 2), ALL)
    placed = (
        P(None, None, ALL),
        P(),
        P(None, SUB, "g"),
        P(ALL),
        P(ALL, None),
        P(ALL),
    )
    return jax.shard_map(
        on_device,
        mesh=fine,
        in_specs=placed,
        out_specs=(P(None, None, ALL), P(None, SUB, "g")),
        check_vma=False,
    )
```

```python
import functools

import jax
import jax.numpy as jnp
import ml_dtypes
import numpy as np
from jax import lax
from jax.experimental import pallas as pl
from jax.experimental.pallas import tpu as pltpu
from jax.sharding import Mesh, PartitionSpec as P

ALL = ("g", "yl", "x", "z", "c")
SUB = ("yl", "x", "z", "c")
SAME_CORE = ("g", "yl", "x", "z")
N = 256
HALF = 128
DT = 0.05
VISC = 0.05
GAIN = 0.3
F32 = jnp.float32
BF16 = jnp.bfloat16
NN = ((1,), (0,))
NT = ((1,), (1,))
TN = ((0,), (0,))


def sine_table(length):
    numbers = np.arange(length) + 1
    phases = numbers[:, None] * numbers[None, :] % (2 * (length + 1))
    return np.sqrt(2.0 / (length + 1)) * np.sin(np.pi * phases / (length + 1))


def rates(length):
    return 2.0 - 2.0 * np.cos(np.pi * (np.arange(length) + 1) / (length + 1))


SINE = sine_table(N)
RATES = rates(N)
MODE_ORDER = np.array([2 * q + k for k in range(2) for q in range(HALF)])


def surface_response():
    total = np.zeros((N, N))
    for c in range(N):
        total += SINE[0, c] ** 2 / (1.0 + 64.0 * (RATES[c] + RATES[:, None] + RATES[None, :]))
    return total


Q = SINE.astype(np.float32)
Q_HALVES = np.concatenate([Q[:, :HALF], Q[:, HALF:]], axis=0)
RESPONSE = surface_response()[MODE_ORDER].astype(np.float32)


def lobatto_derivative():
    points = np.array([-1.0, -1.0 / np.sqrt(5.0), 1.0 / np.sqrt(5.0), 1.0])
    weights = np.array(
        [1.0 / np.prod([points[j] - points[k] for k in range(4) if k != j]) for j in range(4)]
    )
    deriv = np.zeros((4, 4))
    for i in range(4):
        for j in range(4):
            if i != j:
                deriv[i, j] = weights[j] / weights[i] / (points[i] - points[j])
        deriv[i, i] = -np.sum(deriv[i])
    return deriv


def operator_parts():
    deriv, eye = lobatto_derivative(), np.eye(4)
    along = [
        np.kron(eye, np.kron(eye, deriv)),
        np.kron(eye, np.kron(deriv, eye)),
        np.kron(deriv, np.kron(eye, eye)),
    ]
    second = sum(d @ d for d in along)
    pick = np.zeros((4, 4, 4, 4))
    for i in range(4):
        for j in range(4):
            pick[i, j, i, j] = 1.0
    eye16 = np.eye(16)
    right, left = np.kron(eye16, pick[3, 3]), np.kron(eye16, pick[0, 0])
    right_from, left_from = np.kron(eye16, pick[3, 0]), np.kron(eye16, pick[0, 3])
    fixed = np.kron(np.eye(5), np.eye(64) - 0.15 * right - 0.15 * left)
    fixed = fixed + DT * VISC * np.kron(np.diag([0.0, 1.0, 1.0, 1.0, 1.0]), second)
    by_x = -DT * along[0] + 0.15 * right - 0.15 * left
    return [
        np.asarray(a, np.float32)
        for a in (
            fixed,
            by_x,
            -DT * along[1],
            -DT * along[2],
            np.kron(np.eye(5), 0.15 * right_from),
            -0.15 * right_from,
            np.kron(np.eye(5), 0.15 * left_from),
            0.15 * left_from,
        )
    ]


FIXED, BY_X, BY_Y, BY_Z, NEXT_FIXED, NEXT_X, PREV_FIXED, PREV_X = operator_parts()


def wall_tables():
    groups = []
    for fixed, tables in ((FIXED, (BY_X, BY_Y, BY_Z)), (NEXT_FIXED, (NEXT_X,)), (PREV_FIXED, (PREV_X,))):
        groups.append(fixed[256:272] - fixed[0:16])
        groups += [np.tile(t[:16], (1, 5)) for t in tables]
    return np.stack(groups).astype(np.float32)


WALL_TABLES = wall_tables()
RATE_LIST = RATES.astype(np.float32)
RATE_ROW = (1.0 + 64.0 * RATES)[None, :].astype(np.float32)
RATE_COLUMN = (64.0 * RATES)[:, None].astype(np.float32)
SURFACE_ROW = np.broadcast_to(Q[:1], (8, N)).copy()
FIELD_HOT = np.pad(np.kron(np.eye(5), np.ones((64, 1))), ((0, 0), (0, 3))).astype(ml_dtypes.bfloat16)
TILE_HOT = np.kron(np.ones((5, 1)), np.eye(64)).astype(ml_dtypes.bfloat16)
OPERATORS = np.stack([BY_X, BY_Y, BY_Z, NEXT_X, PREV_X])


def split(value):
    high = value.astype(BF16)
    return high, (value - high.astype(F32)).astype(BF16)


def dot(a, b, dims=NN):
    return lax.dot_general(a, b, (dims, ((), ())), preferred_element_type=F32)


def dot3(a, b, dims=NN):
    a = split(a) if not isinstance(a, tuple) else a
    b = split(b) if not isinstance(b, tuple) else b
    return dot(a[0], b[0], dims) + (dot(a[0], b[1], dims) + dot(a[1], b[0], dims))


def hot_dot(hot, b, dims=NN):
    high, low = split(b)
    return dot(hot, high, dims) + dot(hot, low, dims)


def dot_hot(a, hot, dims=NN):
    high, low = split(a)
    return dot(high, hot, dims) + dot(low, hot, dims)


def hot_of(condition):
    return jnp.where(condition, 1.0, 0.0).astype(BF16)


def iota(shape, dim):
    return lax.broadcasted_iota(jnp.int32, shape, dim)


def rows(ref, first, count, stride):
    return ref[pl.ds(first, count, stride) if stride > 1 else pl.ds(first, count), :]


def sine_rows(ref, first, count, stride):
    return jnp.concatenate([rows(ref, h * N + first, count, stride) for h in range(2)], axis=1)


def x_ordered(sine_ref):
    blocks = [sine_rows(sine_ref, 2 * k + i, 64, 4) for i in range(2) for k in range(2)]
    return split(jnp.concatenate(blocks, axis=0))


def mode_ordered(sine_ref):
    return jnp.concatenate([sine_rows(sine_ref, k, HALF, 2) for k in range(2)], axis=0)


def column_of(row):
    return jnp.broadcast_to(row.astype(F32), (8, row.shape[1])).T[:, 0:1].astype(jnp.int32)


def near_kernel(
    where_ref, jac_hbm, fluid_hbm, solid_hbm, sine_hbm, table_hbm, elem_hbm, owner_hbm, patch_hbm,
    out_ref, trace_ref, surface_ref, first_ref, last_ref, matrix_ref, far_table_ref,
    jac_ref, fluid_ref, solid_ref, sine_ref, table_ref, elem_ref, owner_ref, patch_ref, sems
):
    group = where_ref[0]
    count = fluid_ref.shape[1]
    copies = [
        pltpu.make_async_copy(jac_hbm, jac_ref, sems.at[0]),
        pltpu.make_async_copy(solid_hbm, solid_ref, sems.at[1]),
        pltpu.make_async_copy(sine_hbm, sine_ref, sems.at[2]),
        pltpu.make_async_copy(table_hbm, table_ref, sems.at[3]),
        pltpu.make_async_copy(elem_hbm, elem_ref, sems.at[4]),
        pltpu.make_async_copy(owner_hbm, owner_ref, sems.at[5]),
        pltpu.make_async_copy(patch_hbm, patch_ref, sems.at[6]),
    ]
    for i in range(5):
        at = pl.ds(64 * i, 64)
        copies.append(pltpu.make_async_copy(fluid_hbm.at[at, :], fluid_ref.at[at, :], sems.at[7 + i]))
    for copy in copies:
        copy.start()
    for copy in copies[:7]:
        copy.wait()

    near, far = [
        sine_ref[pl.ds(pl.multiple_of(half * N + group * HALF, HALF), HALF), :]
        for half in (group, 1 - group)
    ]
    far_table_ref[...] = far
    near = split(near)
    for i in range(2):
        modes = dot3(near, rows(solid_ref, i, N, 2), NT)
        for h in range(2):
            out_ref[pl.ds(2 * i + h, HALF, 5), :] = modes[:, h * HALF : (h + 1) * HALF]
    surface_ref[...] = solid_ref[0:2]

    field = iota((1, 320), 1) // 64
    coefficients = []
    for d in range(3):
        change = jac_ref[d, 4:5, :] - jac_ref[d, 0:1, :]
        row = jnp.zeros((1, 320), F32)
        for f in range(5):
            row = jnp.where(field == f, change[:, f : f + 1], row)
        coefficients.append(row)
    own = table_ref[0]
    for d in range(3):
        own = own + coefficients[d] * table_ref[1 + d]
    matrix_ref[0:16] = own
    matrix_ref[16:32] = table_ref[4] + coefficients[0] * table_ref[5]
    matrix_ref[32:48] = table_ref[6] + coefficients[0] * table_ref[7]

    owner, patch, elem = owner_ref[...], patch_ref[...], elem_ref[...]
    square = (HALF, HALF)
    same = (column_of(owner) == owner) & (iota(square, 0) < iota(square, 1))
    place = jnp.sum(jnp.where(same, 1.0, 0.0), axis=0, keepdims=True)
    elem_hot = hot_of(column_of(elem) == iota((HALF, count), 1))

    for copy in copies[7:]:
        copy.wait()
    lane = iota((1, 384), 1)
    gap = jnp.zeros((1, 64), F32)
    for block, at, out, element in (
        (fluid_ref[:, 0:HALF], (0, 1), first_ref, 0),
        (fluid_ref[:, count - HALF : count], (HALF - 1, HALF - 2), last_ref, count - 1),
    ):
        turned = block.T
        met = elem == element
        edge_owner = jnp.sum(jnp.where(met, owner + 1, 0).astype(F32), axis=1, keepdims=True)
        edge_patch = jnp.sum(jnp.where(met, patch, 0).astype(F32), axis=1, keepdims=True)
        out[0:1] = jnp.concatenate([turned[at[0] : at[0] + 1], gap], axis=1)
        out[1:2] = jnp.concatenate([turned[at[1] : at[1] + 1], gap], axis=1)
        out[2:3] = jnp.where(lane == 0, edge_owner, jnp.where(lane == 1, edge_patch, 0.0))
        out[3:8] = jnp.zeros((5, 384), F32)

    walls = dot3(matrix_ref[...], fluid_ref[...])
    wall0 = fluid_ref[256:272] - fluid_ref[0:16]
    lane = iota(wall0.shape, 1)
    following = pltpu.roll(walls[16:32], count - 1, 1)
    preceding = pltpu.roll(walls[32:48], 1, 1)
    later = walls[0:16] + jnp.where(lane == count - 1, 0.0, following)
    later = later + jnp.where(lane == 0, 0.0, preceding)
    values = dot_hot(jnp.concatenate([wall0, later - GAIN * wall0], axis=0), elem_hot, NT)
    trace_ref[...] = values[:16]
    ids = jnp.broadcast_to((patch + 1).astype(F32), (8, HALF))
    filler = jnp.zeros((24, HALF), F32)
    sent = jnp.concatenate([values, ids, filler], axis=0)
    none = jnp.zeros((64, HALF), F32)
    arranged = 0.0
    for i in range(2):
        hot = hot_of((iota(square, 0) == owner) & (place == float(i)))
        padded = jnp.concatenate([sent, none] if i == 0 else [none, sent], axis=0)
        arranged = arranged + hot_dot(hot, padded, NT)
    out_ref[pl.ds(4, HALF, 5), :] = arranged


def far_kernel(far_ref, table_ref, near_ref, out_ref):
    table = split(table_ref[...])
    out_ref[pl.ds(4, HALF, 5), :] = rows(near_ref, 4, HALF, 5)
    for i in range(2):
        modes = dot3(table, rows(far_ref, i, N, 2), NT)
        for h in range(2):
            part = modes[:, h * HALF : (h + 1) * HALF]
            out_ref[pl.ds(2 * i + h, HALF, 5), :] = rows(near_ref, 2 * i + h, HALF, 5) + part


def tables_kernel(
    where_ref, rate_ref, sine_ref, rate_row_ref, rate_col_ref, order_ref,
    sine_out, x_out, modes_out, modes_t_out, split_out, decay_out
):
    del order_ref
    by_modes = mode_ordered(sine_ref)
    for out, table in (
        (sine_out, split(sine_rows(sine_ref, 0, N, 1))),
        (x_out, x_ordered(sine_ref)),
        (modes_out, split(by_modes)),
        (modes_t_out, split(by_modes.T)),
    ):
        out[0], out[1] = table
    for i in range(2):
        split_out[2 * i], split_out[2 * i + 1] = split(sine_rows(sine_ref, i, HALF, 2))
    decay_out[...] = 1.0 / (rate_col_ref[...] + (rate_row_ref[...] + 64.0 * rate_ref[where_ref[2]]))


def matrices_kernel(jac_ref, field_ref, tile_ref, fixed_ref, operators_ref, out_ref):
    field, tile = field_ref[...], tile_ref[...]

    def spread(d):
        return dot_hot(hot_dot(field, jac_ref[d]), field, NT)

    def tiled(d):
        return dot_hot(hot_dot(tile, operators_ref[d]), tile, NT)

    by_x = spread(0)
    own = by_x * tiled(0) + spread(1) * tiled(1) + spread(2) * tiled(2)
    out_ref[0:320] = fixed_ref[0] + own
    out_ref[320:640] = fixed_ref[1] + by_x * tiled(3)
    out_ref[640:960] = fixed_ref[2] + by_x * tiled(4)


def modes_kernel(
    where_ref, got_ref, surface_ref, sine_ref, split_ref, by_modes_ref, decay_ref, row_ref,
    matrix_ref, before_ref, after_ref, elem_ref, owner_ref, patch_ref, modes_ref, out_ref, *, count
):
    group = where_ref[0]
    sine = sine_ref[0], sine_ref[1]
    modes = 0.0
    for i in range(2):
        part = jnp.concatenate([rows(got_ref, 2 * i + h, HALF, 5) for h in range(2)], axis=1)
        by_z = dot3(sine, part, NT)
        modes = modes + dot3(by_z, (split_ref[2 * i], split_ref[2 * i + 1]))
    modes_ref[...] = modes
    surface_row = dot3(row_ref[...], decay_ref[...] * modes)[0:1]

    fluid = rows(got_ref, 4, HALF, 5)
    square = (HALF, HALF)
    lane = iota(square, 1)
    fluid_pair = split(fluid)
    sums = [[0.0, 0.0], [0.0, 0.0]]
    counts = [0.0, 0.0]
    count_lanes = 0.0
    for i in range(2):
        ids = fluid[:, i * 64 + 32 : i * 64 + 33].astype(jnp.int32) - 1
        count_lanes = count_lanes + jnp.sum(jnp.where(ids == lane, 1.0, 0.0), axis=0, keepdims=True)
        for f in range(2):
            pick = hot_of(iota(square, 0) == i * 64 + f * 16 + lane % 16)
            values = dot(fluid_pair[0], pick) + dot(fluid_pair[1], pick)
            for xl in range(2):
                mask = ids == xl * 8 + lane // 16
                sums[f][xl] = sums[f][xl] + jnp.sum(
                    jnp.where(mask, values, 0.0), axis=0, keepdims=True
                )
                if f == 0:
                    counts[xl] = counts[xl] + jnp.sum(
                        jnp.where(mask, 1.0, 0.0), axis=0, keepdims=True
                    )
    heat = [sums[0][xl] - counts[xl] * surface_ref[xl : xl + 1, :] for xl in range(2)]
    tail = jnp.where(lane < 16, count_lanes, 0.0)
    edge_rows = []
    for t, (part, ref, element) in enumerate(((2, before_ref, 0), (1, after_ref, count - 1))):
        met = elem_ref[...] == element
        owner, patch = [
            jnp.sum(jnp.where(met, value, 0).astype(F32), axis=1, keepdims=True).astype(jnp.int32)
            for value in (owner_ref[...] + 1, patch_ref[...])
        ]
        x_of_slot = patch // 8 * HALF + (owner - 1) % 2 * 64 + (owner - 1) // 2
        tail = jnp.where(lane == 40 + t, jnp.where(owner > 0, x_of_slot + 1, 0).astype(F32), tail)
        tables = matrix_ref[16 * part : 16 * part + 16]
        column = jnp.sum(tables * ref[0:1, 0:320], axis=1, keepdims=True)
        node, lane16 = iota((16, HALF), 0), iota((16, HALF), 1)
        used = (lane16 % 16 == node) & (lane16 // 16 == patch % 8)
        edge_rows.append(jnp.sum(jnp.where(used, column, 0.0), axis=0, keepdims=True))
    for k in range(2):
        by_modes = []
        for part in range(2):
            table = by_modes_ref[part, k * HALF : (k + 1) * HALF, :].astype(F32)
            own = jnp.where(group == 0, table[:, :HALF], table[:, HALF:])
            by_modes.append(own.astype(BF16))
        by_modes = tuple(by_modes)
        for xl in range(2):
            column = dot3(by_modes, jnp.broadcast_to(sums[1][xl], (8, HALF)), NT)[:, 0:1]
            tail = jnp.where(lane == 16 + 2 * k + xl, column, tail)
        for t in range(2):
            column = dot3(by_modes, jnp.broadcast_to(edge_rows[t], (8, HALF)), NT)[:, 0:1]
            tail = jnp.where(lane == 32 + 2 * t + k, column, tail)
    shared = [surface_row[:, :HALF], surface_row[:, HALF:], heat[0], heat[1]]
    for r in range(4):
        out_ref[pl.ds(r, HALF, 5), :] = jnp.broadcast_to(shared[r], square)
    out_ref[pl.ds(4, HALF, 5), :] = tail


def solve_kernel(
    where_ref, got_ref, other_ref, modes_ref, response_ref, sine_ref, pair_ref, x_ref, by_modes_ref,
    from_modes_ref, split_ref, decay_ref, row_ref, surface_hbm, out_ref, heat_ref, surface_ref, sem
):
    core, me = where_ref[1], where_ref[2]
    first = jnp.full((HALF, HALF), core, jnp.int32) == 0
    ordered = []
    for r in range(5):
        mine, theirs = rows(got_ref, r, HALF, 5), rows(other_ref, r, HALF, 5)
        ordered.append((jnp.where(first, mine, theirs), jnp.where(first, theirs, mine)))

    def block(g, r):
        return jnp.concatenate([ordered[r][k][g * 64 : (g + 1) * 64] for k in range(2)], axis=0)

    halves = [
        tuple(by_modes_ref[part, :, g * HALF : (g + 1) * HALF] for part in range(2))
        for g in range(2)
    ]
    by_x = x_ref[0], x_ref[1]
    heat_modes = 0.0
    for xl in range(2):
        by_y = 0.0
        for g in range(2):
            by_y = by_y + dot3(halves[g], block(g, 2 + xl), NT)
        at = slice(xl * HALF, (xl + 1) * HALF)
        heat_modes = heat_modes + dot3(by_y, (by_x[0][at], by_x[1][at]))
    heat_ref[...] = heat_modes
    given = jnp.concatenate(
        [jnp.concatenate([ordered[h][k] for h in range(2)], axis=1) for k in range(2)], axis=0
    )
    surface = dot3((from_modes_ref[0], from_modes_ref[1]), given + response_ref[...] * heat_modes)
    surface = dot3(surface, by_x, NT)
    surface_ref[...] = surface
    copy = pltpu.make_async_copy(surface_ref, surface_hbm, sem)
    copy.start()
    square = (HALF, HALF)
    tails = [block(g, 4) for g in range(2)]
    tail_pairs = [tail.astype(BF16) for tail in tails]
    expand = [hot_of(iota(square, 1) == xl * 8 + iota(square, 0) // 16) for xl in range(2)]
    count = jnp.concatenate(
        [
            jnp.concatenate([dot(expand[xl], tail_pairs[g], NT) for xl in range(2)], axis=1)
            for g in range(2)
        ],
        axis=0,
    )
    own_sine = jnp.broadcast_to(sine_rows(sine_ref, me, 1, 1), (8, N))
    reduced = dot3(own_sine, count * surface)
    tail_sum = tails[0] + tails[1]
    lane8 = iota((8, HALF), 1)
    later = jnp.concatenate(
        [hot_dot(hot_of(lane8 == 16 + 2 * core + xl), tail_sum, NT) for xl in range(2)], axis=1
    )
    wide = iota((HALF, N), 1)
    for k in range(2):
        tail = ordered[4][k]
        for t in range(2):
            value = jnp.where(first[:, 0:1], tail[:, 32 + 2 * t : 33 + 2 * t], tail[:, 33 + 2 * t : 34 + 2 * t])
            met = tail[:, 40 + t : 41 + t].astype(jnp.int32) - 1 == wide
            later = later + jnp.sum(jnp.where(met, value, 0.0), axis=0, keepdims=True)
    heat1 = dot3(later - 0.7 * reduced, by_x)[0:1]
    heat0 = heat_ref[pl.ds(core * HALF + me // 2, 1), :]
    decay = decay_ref[...]
    column = sine_ref[pl.ds(0, N), 0:1]
    final = decay * (decay * (modes_ref[...] + column * heat0) + column * heat1)
    final_row = dot3(row_ref[...], final)[0:1]
    final = split(final)
    sine = pair_ref[0], pair_ref[1]
    for xl in range(2):
        back = dot3(dot3((split_ref[2 * xl], split_ref[2 * xl + 1]), final, NT), sine)
        for g in range(2):
            for h in range(2):
                out_ref[pl.ds(g * 640 + 2 * xl + h, HALF, 5), :] = back[:, h * HALF : (h + 1) * HALF]
    for k in range(2):
        out_ref[pl.ds(4 + 5 * k, HALF, 10), :] = jnp.broadcast_to(
            final_row[:, k * HALF : (k + 1) * HALF], (HALF, HALF)
        )
    copy.wait()


def met_values(surface, owner, patch):
    x_of_slot = patch // 8 * HALF + owner % 2 * 64 + owner // 2
    x_hot = hot_of(iota((N, HALF), 0) == x_of_slot)
    met = dot_hot(surface, x_hot)
    return jnp.where(iota((HALF, HALF), 0) // 16 == patch % 8, met, 0.0)


def folded(met):
    fold = hot_of(iota((16, HALF), 0) == iota((16, HALF), 1) % 16)
    return hot_dot(fold, met)


def stepped(extended, matrix_ref):
    fluid = split(extended)
    width = extended.shape[1]
    own, following, preceding = [
        dot3(matrix_ref[pl.ds(320 * i, 320), :], fluid) for i in range(3)
    ]
    return own + pltpu.roll(following, width - 1, 1) + pltpu.roll(preceding, 1, 1)


def step_kernel(where_ref, fluid_ref, matrix_ref, before_ref, after_ref, out_ref):
    count = fluid_ref.shape[1]
    me = where_ref[2]
    lane = iota((320, HALF), 1)
    following, preceding = after_ref[...].T[0:320], before_ref[...].T[0:320]
    halo = jnp.zeros((320, HALF), F32)
    for at, column in (
        (0, following[:, 0:1]),
        (1, following[:, 1:2]),
        (HALF - 1, preceding[:, 0:1]),
        (HALF - 2, preceding[:, 1:2]),
    ):
        halo = jnp.where(lane == at, column, halo)
    result = stepped(jnp.concatenate([fluid_ref[...], halo], axis=1), matrix_ref)
    edge = result[:, count:]
    beyond = ((lane == 0) & (me == 255)) | ((lane == HALF - 1) & (me == 0))
    out_ref[:, :count] = result[:, :count]
    out_ref[:, count:] = jnp.where(beyond, 0.0, edge)


def second_kernel(
    where_ref, fluid_ref, surface_ref, trace_ref, matrix_ref, before_ref, after_ref, elem_ref,
    owner_ref, patch_ref, sine_ref, out_ref, later_ref, slots_ref, walls_ref
):
    group, me = where_ref[0], where_ref[2]
    width = fluid_ref.shape[1]
    count = width - HALF
    own_surface = surface_ref[pl.ds(pl.multiple_of(group * HALF, HALF), HALF), :]
    elem_hot = hot_of(column_of(elem_ref[...]) == iota((HALF, count), 1))
    met = folded(met_values(own_surface, owner_ref[...], patch_ref[...]))
    source = GAIN * dot_hot(met - trace_ref[...], elem_hot)
    square = (16, HALF)
    edge = jnp.zeros(square, F32)
    for ref, at, device in ((after_ref, 0, me + 1), (before_ref, HALF - 1, me - 1)):
        owner = ref[2:3, 0:1].astype(jnp.int32) - 1
        patch = ref[2:3, 1:2].astype(jnp.int32)
        side = jnp.clip(device, 0, 255) // HALF
        near = surface_ref[pl.ds(pl.multiple_of(side * HALF, HALF), HALF), :]
        lanes = jnp.zeros((1, HALF), jnp.int32)
        value = folded(met_values(near, owner + lanes, patch + lanes))
        column = ref[...].T
        value = GAIN * (value - (column[256:272, 0:1] - column[0:16, 0:1]))
        used = (iota(square, 1) == at) & (owner >= 0)
        edge = jnp.where(used, value, edge)
    slot_hot = hot_of(iota((N, HALF), 0) == 2 * owner_ref[...] + patch_ref[...] // 8)
    slots_ref[...] = dot_hot(sine_rows(sine_ref, 0, N, 1), slot_hot)
    walls = fluid_ref[256:272] + jnp.concatenate([source, edge], axis=1)
    later_ref[...] = dot_hot(walls[:, :count] - fluid_ref[0:16, :count], elem_hot, NT)
    extended = jnp.concatenate([fluid_ref[0:256], walls, fluid_ref[272:320]], axis=0)
    result = stepped(extended, matrix_ref)[:, :count]
    out_ref[...] = result
    walls_ref[...] = result[256:272]


def solid_kernel(where_ref, got_ref, sine_ref, solid_hbm, solid_ref, sems):
    by_y = split(sine_ref[pl.ds(pl.multiple_of(where_ref[0] * N, N), N), :])
    copies = []
    for h in range(2):
        for xl in range(2):
            part = rows(got_ref, 2 * xl + h, N, 5)
            solid_ref[pl.ds(h * N + xl, HALF, 2), :] = dot3(part, by_y, TN)
        at = pl.ds(h * N, N)
        copies.append(pltpu.make_async_copy(solid_ref.at[at, :], solid_hbm.at[at, :], sems.at[h]))
        copies[h].start()
    for copy in copies:
        copy.wait()


def last_kernel(
    where_ref, mine_ref, other_ref, sine_ref, slots_ref, later_ref, elem_ref, patch_ref, walls_ref,
    fluid_hbm, out_hbm, out_ref, sem
):
    group, core = where_ref[0], where_ref[1]
    first = jnp.full((N, HALF), core, jnp.int32) == 0
    mine, other = mine_ref[...], other_ref[...]
    given = jnp.concatenate([jnp.where(first, mine, other), jnp.where(first, other, mine)], axis=1)
    own_rows = sine_rows(sine_ref, pl.multiple_of(group * HALF, HALF), HALF, 1)
    met = dot3(own_rows, dot3(given, slots_ref[...]))
    met = folded(jnp.where(iota((HALF, HALF), 0) // 16 == patch_ref[...] % 8, met, 0.0))
    elem_hot = hot_of(column_of(elem_ref[...]) == iota((HALF, walls_ref.shape[1]), 1))
    out_ref[...] = walls_ref[...] + GAIN * dot_hot(met - later_ref[...], elem_hot)
    copy = pltpu.make_async_copy(out_ref, out_hbm.at[pl.ds(256, 16), :], sem)
    copy.start()
    copy.wait()


def call(kernel, outs, args, scalars=0, scratch=(), aliases=None, specs=None, out_specs=None, cost=None, limit=40):
    whole = pl.BlockSpec(memory_space=pltpu.VMEM)
    given = [pl.BlockSpec(memory_space=pltpu.SMEM)] * scalars + [whole] * (len(args) - scalars)
    return pl.pallas_call(
        kernel,
        out_shape=[
            jax.ShapeDtypeStruct(*(out if isinstance(out[0], tuple) else (out, F32))) for out in outs
        ],
        in_specs=specs or given,
        out_specs=out_specs or [whole] * len(outs),
        scratch_shapes=list(scratch),
        input_output_aliases=aliases or {},
        cost_estimate=pl.CostEstimate(flops=int(cost or 1e8), bytes_accessed=1 << 20, transcendentals=0),
        compiler_params=pltpu.CompilerParams(vmem_limit_bytes=limit << 20),
    )(*args)


def exchange(payload, axes):
    chunks = payload.reshape(payload.shape[0], 1, HALF)
    return lax.all_to_all(chunks, axes, split_axis=0, concat_axis=0, tiled=True).reshape(payload.shape)


def on_device(fluid_state, flux_jacobian, solid_temp, iface_elem, iface_owner, iface_patch):
    me = lax.axis_index(ALL)
    where = jnp.stack([me // HALF, me % 2, me]).astype(jnp.int32)
    fluid0 = fluid_state.reshape(320, -1)
    count = fluid0.shape[1]
    solid = solid_temp.reshape(2 * N, HALF)
    elem, owner, patch = iface_elem[None, :], iface_owner.reshape(1, HALF), iface_patch[None, :]
    smem = pl.BlockSpec(memory_space=pltpu.SMEM)
    vmem = pl.BlockSpec(memory_space=pltpu.VMEM)
    hbm = pl.BlockSpec(memory_space=pltpu.HBM)

    far = lax.ppermute(solid, "g", [(0, 1), (1, 0)])
    near, trace0, surface0, first, last, wall_matrix, far_table = call(
        near_kernel,
        [(5 * HALF, HALF), (16, HALF), (2, HALF), (8, 384), (8, 384), (48, 320), (HALF, HALF)],
        [where, flux_jacobian, fluid0, solid, Q_HALVES, WALL_TABLES, elem, owner, patch],
        specs=[smem] + [hbm] * 8,
        limit=52,
        scratch=[
            pltpu.VMEM(flux_jacobian.shape, F32),
            pltpu.VMEM(fluid0.shape, F32),
            pltpu.VMEM(solid.shape, F32),
            pltpu.VMEM(Q_HALVES.shape, F32),
            pltpu.VMEM(WALL_TABLES.shape, F32),
            pltpu.VMEM((1, HALF), jnp.int32),
            pltpu.VMEM((1, HALF), jnp.int32),
            pltpu.VMEM((1, HALF), jnp.int32),
            pltpu.SemaphoreType.DMA((12,)),
        ],
    )
    before = lax.ppermute(last, ALL, [(i, i + 1) for i in range(255)])
    after = lax.ppermute(first, ALL, [(i + 1, i) for i in range(255)])
    (pay1,) = call(far_kernel, [(5 * HALF, HALF)], [far, far_table, near])
    got1 = exchange(pay1, SUB)
    tables = call(
        tables_kernel,
        [((2, N, N), BF16)] * 4 + [((4, HALF, N), BF16), (N, N)],
        [where, RATE_LIST, Q_HALVES, RATE_ROW, RATE_COLUMN, surface0],
        scalars=2,
    )
    sine_pair, x_pair, modes_pair, modes_t_pair, split_pair, decay = tables
    jacobian = jnp.pad(flux_jacobian, ((0, 0), (0, 3), (0, 3)))
    (matrix,) = call(
        matrices_kernel,
        [(960, 320)],
        [jacobian, FIELD_HOT, TILE_HOT, np.stack([FIXED, NEXT_FIXED, PREV_FIXED]), OPERATORS],
    )
    (fluid1,) = call(
        step_kernel,
        [(320, count + HALF)],
        [where, fluid0, matrix, before, after],
        scalars=1,
        cost=2e9,
    )
    modes, pay2 = call(
        functools.partial(modes_kernel, count=count),
        [(N, N), (5 * HALF, HALF)],
        [where, got1, surface0, sine_pair, split_pair, modes_pair, decay, SURFACE_ROW,
         wall_matrix, before, after, elem, owner, patch],
        scalars=1,
    )
    got2 = exchange(pay2, SAME_CORE)
    other = lax.ppermute(got2, "c", [(0, 1), (1, 0)])
    surface1, pay3 = call(
        solve_kernel,
        [(N, N), (5 * N, HALF)],
        [where, got2, other, modes, RESPONSE, Q_HALVES, sine_pair, x_pair, modes_pair, modes_t_pair,
         split_pair, decay, SURFACE_ROW],
        scalars=1,
        out_specs=[hbm, vmem],
        scratch=[pltpu.VMEM((N, N), F32), pltpu.VMEM((N, N), F32), pltpu.SemaphoreType.DMA],
    )
    got3 = exchange(pay3, ALL)
    fluid2, trace1, slots, walls2 = call(
        second_kernel,
        [(320, count), (16, HALF), (N, HALF), (16, count)],
        [where, fluid1, surface1, trace0, matrix, before, after, elem, owner, patch, Q_HALVES],
        scalars=1,
        cost=2e9,
    )
    got3, fluid2, trace1, slots, walls2 = lax.optimization_barrier(
        (got3, fluid2, trace1, slots, walls2)
    )
    mine = got3.reshape(N, 5, 1, HALF)[:, 4].reshape(N, HALF)
    far_row = lax.ppermute(mine, "c", [(0, 1), (1, 0)])
    (solid_out,) = call(
        solid_kernel,
        [(2 * N, HALF)],
        [where, got3, Q_HALVES],
        scalars=1,
        out_specs=[hbm],
        scratch=[pltpu.VMEM((2 * N, HALF), F32), pltpu.SemaphoreType.DMA((2,))],
    )
    (fluid2,) = call(
        last_kernel,
        [(320, count)],
        [where, mine, far_row, Q_HALVES, slots, trace1, elem, patch, walls2, fluid2],
        specs=[smem] + [vmem] * 8 + [hbm],
        out_specs=[hbm],
        aliases={9: 0},
        scratch=[pltpu.VMEM((16, count), F32), pltpu.SemaphoreType.DMA],
    )
    return fluid2.reshape(fluid_state.shape), solid_out.reshape(solid_temp.shape)


def solution(mesh):
    fine = Mesh(mesh.devices.reshape(2, 2, 4, 8, 2), ALL)
    placed = (
        P(None, None, ALL),
        P(),
        P(None, SUB, "g"),
        P(ALL),
        P(ALL, None),
        P(ALL),
    )
    return jax.shard_map(
        on_device,
        mesh=fine,
        in_specs=placed,
        out_specs=(P(None, None, ALL), P(None, SUB, "g")),
        check_vma=False,
    )
```

```python
import functools

import jax
import jax.numpy as jnp
import ml_dtypes
import numpy as np
from jax import lax
from jax.experimental import pallas as pl
from jax.experimental.pallas import tpu as pltpu
from jax.sharding import Mesh, PartitionSpec as P

ALL = ("g", "yl", "x", "z", "c")
SUB = ("yl", "x", "z", "c")
SAME_CORE = ("g", "yl", "x", "z")
N = 256
HALF = 128
DT = 0.05
VISC = 0.05
GAIN = 0.3
F32 = jnp.float32
BF16 = jnp.bfloat16
NN = ((1,), (0,))
NT = ((1,), (1,))
TN = ((0,), (0,))


def sine_table(length):
    numbers = np.arange(length) + 1
    phases = numbers[:, None] * numbers[None, :] % (2 * (length + 1))
    return np.sqrt(2.0 / (length + 1)) * np.sin(np.pi * phases / (length + 1))


def rates(length):
    return 2.0 - 2.0 * np.cos(np.pi * (np.arange(length) + 1) / (length + 1))


SINE = sine_table(N)
RATES = rates(N)
MODE_ORDER = np.array([2 * q + k for k in range(2) for q in range(HALF)])


def surface_response():
    total = np.zeros((N, N))
    for c in range(N):
        total += SINE[0, c] ** 2 / (1.0 + 64.0 * (RATES[c] + RATES[:, None] + RATES[None, :]))
    return total


Q = SINE.astype(np.float32)
Q_HALVES = np.concatenate([Q[:, :HALF], Q[:, HALF:]], axis=0)
RESPONSE = surface_response()[MODE_ORDER].astype(np.float32)


def lobatto_derivative():
    points = np.array([-1.0, -1.0 / np.sqrt(5.0), 1.0 / np.sqrt(5.0), 1.0])
    weights = np.array(
        [1.0 / np.prod([points[j] - points[k] for k in range(4) if k != j]) for j in range(4)]
    )
    deriv = np.zeros((4, 4))
    for i in range(4):
        for j in range(4):
            if i != j:
                deriv[i, j] = weights[j] / weights[i] / (points[i] - points[j])
        deriv[i, i] = -np.sum(deriv[i])
    return deriv


def operator_parts():
    deriv, eye = lobatto_derivative(), np.eye(4)
    along = [
        np.kron(eye, np.kron(eye, deriv)),
        np.kron(eye, np.kron(deriv, eye)),
        np.kron(deriv, np.kron(eye, eye)),
    ]
    second = sum(d @ d for d in along)
    pick = np.zeros((4, 4, 4, 4))
    for i in range(4):
        for j in range(4):
            pick[i, j, i, j] = 1.0
    eye16 = np.eye(16)
    right, left = np.kron(eye16, pick[3, 3]), np.kron(eye16, pick[0, 0])
    right_from, left_from = np.kron(eye16, pick[3, 0]), np.kron(eye16, pick[0, 3])
    fixed = np.kron(np.eye(5), np.eye(64) - 0.15 * right - 0.15 * left)
    fixed = fixed + DT * VISC * np.kron(np.diag([0.0, 1.0, 1.0, 1.0, 1.0]), second)
    by_x = -DT * along[0] + 0.15 * right - 0.15 * left
    return [
        np.asarray(a, np.float32)
        for a in (
            fixed,
            by_x,
            -DT * along[1],
            -DT * along[2],
            np.kron(np.eye(5), 0.15 * right_from),
            -0.15 * right_from,
            np.kron(np.eye(5), 0.15 * left_from),
            0.15 * left_from,
        )
    ]


FIXED, BY_X, BY_Y, BY_Z, NEXT_FIXED, NEXT_X, PREV_FIXED, PREV_X = operator_parts()


def wall_tables():
    groups = []
    for fixed, tables in ((FIXED, (BY_X, BY_Y, BY_Z)), (NEXT_FIXED, (NEXT_X,)), (PREV_FIXED, (PREV_X,))):
        groups.append(fixed[256:272] - fixed[0:16])
        groups += [np.tile(t[:16], (1, 5)) for t in tables]
    return np.stack(groups).astype(np.float32)


WALL_TABLES = wall_tables()
RATE_LIST = RATES.astype(np.float32)
RATE_ROW = (1.0 + 64.0 * RATES)[None, :].astype(np.float32)
RATE_COLUMN = (64.0 * RATES)[:, None].astype(np.float32)
SURFACE_ROW = np.broadcast_to(Q[:1], (8, N)).copy()
FIELD_HOT = np.pad(np.kron(np.eye(5), np.ones((64, 1))), ((0, 0), (0, 3))).astype(ml_dtypes.bfloat16)
TILE_HOT = np.kron(np.ones((5, 1)), np.eye(64)).astype(ml_dtypes.bfloat16)
OPERATORS = np.stack([BY_X, BY_Y, BY_Z, NEXT_X, PREV_X])


def split(value):
    high = value.astype(BF16)
    return high, (value - high.astype(F32)).astype(BF16)


def dot(a, b, dims=NN):
    return lax.dot_general(a, b, (dims, ((), ())), preferred_element_type=F32)


def dot3(a, b, dims=NN):
    a = split(a) if not isinstance(a, tuple) else a
    b = split(b) if not isinstance(b, tuple) else b
    return dot(a[0], b[0], dims) + (dot(a[0], b[1], dims) + dot(a[1], b[0], dims))


def hot_dot(hot, b, dims=NN):
    high, low = split(b)
    return dot(hot, high, dims) + dot(hot, low, dims)


def dot_hot(a, hot, dims=NN):
    high, low = split(a)
    return dot(high, hot, dims) + dot(low, hot, dims)


def hot_of(condition):
    return jnp.where(condition, 1.0, 0.0).astype(BF16)


def iota(shape, dim):
    return lax.broadcasted_iota(jnp.int32, shape, dim)


def rows(ref, first, count, stride):
    return ref[pl.ds(first, count, stride) if stride > 1 else pl.ds(first, count), :]


def sine_rows(ref, first, count, stride):
    return jnp.concatenate([rows(ref, h * N + first, count, stride) for h in range(2)], axis=1)


def x_ordered(sine_ref):
    blocks = [sine_rows(sine_ref, 2 * k + i, 64, 4) for i in range(2) for k in range(2)]
    return split(jnp.concatenate(blocks, axis=0))


def mode_ordered(sine_ref):
    return jnp.concatenate([sine_rows(sine_ref, k, HALF, 2) for k in range(2)], axis=0)


def column_of(row):
    return jnp.broadcast_to(row.astype(F32), (8, row.shape[1])).T[:, 0:1].astype(jnp.int32)


def near_kernel(
    where_ref, jac_hbm, fluid_hbm, solid_hbm, sine_hbm, table_hbm, elem_hbm, owner_hbm, patch_hbm,
    out_ref, trace_ref, surface_ref, first_ref, last_ref, matrix_ref, far_table_ref,
    jac_ref, fluid_ref, solid_ref, sine_ref, table_ref, elem_ref, owner_ref, patch_ref, sems
):
    group = where_ref[0]
    count = fluid_ref.shape[1]
    copies = [
        pltpu.make_async_copy(jac_hbm, jac_ref, sems.at[0]),
        pltpu.make_async_copy(solid_hbm, solid_ref, sems.at[1]),
        pltpu.make_async_copy(sine_hbm, sine_ref, sems.at[2]),
        pltpu.make_async_copy(table_hbm, table_ref, sems.at[3]),
        pltpu.make_async_copy(elem_hbm, elem_ref, sems.at[4]),
        pltpu.make_async_copy(owner_hbm, owner_ref, sems.at[5]),
        pltpu.make_async_copy(patch_hbm, patch_ref, sems.at[6]),
    ]
    for i in range(5):
        at = pl.ds(64 * i, 64)
        copies.append(pltpu.make_async_copy(fluid_hbm.at[at, :], fluid_ref.at[at, :], sems.at[7 + i]))
    for copy in copies:
        copy.start()
    for copy in copies[:7]:
        copy.wait()

    near, far = [
        sine_ref[pl.ds(pl.multiple_of(half * N + group * HALF, HALF), HALF), :]
        for half in (group, 1 - group)
    ]
    far_table_ref[...] = far
    near = split(near)
    for i in range(2):
        modes = dot3(near, rows(solid_ref, i, N, 2), NT)
        for h in range(2):
            out_ref[pl.ds(2 * i + h, HALF, 5), :] = modes[:, h * HALF : (h + 1) * HALF]
    surface_ref[...] = solid_ref[0:2]

    field = iota((1, 320), 1) // 64
    coefficients = []
    for d in range(3):
        change = jac_ref[d, 4:5, :] - jac_ref[d, 0:1, :]
        row = jnp.zeros((1, 320), F32)
        for f in range(5):
            row = jnp.where(field == f, change[:, f : f + 1], row)
        coefficients.append(row)
    own = table_ref[0]
    for d in range(3):
        own = own + coefficients[d] * table_ref[1 + d]
    matrix_ref[0:16] = own
    matrix_ref[16:32] = table_ref[4] + coefficients[0] * table_ref[5]
    matrix_ref[32:48] = table_ref[6] + coefficients[0] * table_ref[7]

    owner, patch, elem = owner_ref[...], patch_ref[...], elem_ref[...]
    square = (HALF, HALF)
    same = (column_of(owner) == owner) & (iota(square, 0) < iota(square, 1))
    place = jnp.sum(jnp.where(same, 1.0, 0.0), axis=0, keepdims=True)
    elem_hot = hot_of(column_of(elem) == iota((HALF, count), 1))

    for copy in copies[7:]:
        copy.wait()
    lane = iota((1, 384), 1)
    gap = jnp.zeros((1, 64), F32)
    for block, at, out, element in (
        (fluid_ref[:, 0:HALF], (0, 1), first_ref, 0),
        (fluid_ref[:, count - HALF : count], (HALF - 1, HALF - 2), last_ref, count - 1),
    ):
        turned = block.T
        met = elem == element
        edge_owner = jnp.sum(jnp.where(met, owner + 1, 0).astype(F32), axis=1, keepdims=True)
        edge_patch = jnp.sum(jnp.where(met, patch, 0).astype(F32), axis=1, keepdims=True)
        out[0:1] = jnp.concatenate([turned[at[0] : at[0] + 1], gap], axis=1)
        out[1:2] = jnp.concatenate([turned[at[1] : at[1] + 1], gap], axis=1)
        out[2:3] = jnp.where(lane == 0, edge_owner, jnp.where(lane == 1, edge_patch, 0.0))
        out[3:8] = jnp.zeros((5, 384), F32)

    walls = dot3(matrix_ref[...], fluid_ref[...])
    wall0 = fluid_ref[256:272] - fluid_ref[0:16]
    lane = iota(wall0.shape, 1)
    following = pltpu.roll(walls[16:32], count - 1, 1)
    preceding = pltpu.roll(walls[32:48], 1, 1)
    later = walls[0:16] + jnp.where(lane == count - 1, 0.0, following)
    later = later + jnp.where(lane == 0, 0.0, preceding)
    values = dot_hot(jnp.concatenate([wall0, later - GAIN * wall0], axis=0), elem_hot, NT)
    trace_ref[...] = values[:16]
    ids = jnp.broadcast_to((patch + 1).astype(F32), (8, HALF))
    filler = jnp.zeros((24, HALF), F32)
    sent = jnp.concatenate([values, ids, filler], axis=0)
    none = jnp.zeros((64, HALF), F32)
    arranged = 0.0
    for i in range(2):
        hot = hot_of((iota(square, 0) == owner) & (place == float(i)))
        padded = jnp.concatenate([sent, none] if i == 0 else [none, sent], axis=0)
        arranged = arranged + hot_dot(hot, padded, NT)
    out_ref[pl.ds(4, HALF, 5), :] = arranged


def send_out(pairs, sems):
    copies = [pltpu.make_async_copy(a, b, sems.at[i]) for i, (a, b) in enumerate(pairs)]
    for copy in copies:
        copy.start()
    return copies


def far_kernel(far_ref, table_ref, near_ref, out_hbm, out_ref, sems):
    table = split(table_ref[...])
    out_ref[pl.ds(4, HALF, 5), :] = rows(near_ref, 4, HALF, 5)
    for i in range(2):
        modes = dot3(table, rows(far_ref, i, N, 2), NT)
        for h in range(2):
            part = modes[:, h * HALF : (h + 1) * HALF]
            out_ref[pl.ds(2 * i + h, HALF, 5), :] = rows(near_ref, 2 * i + h, HALF, 5) + part
    pieces = [pl.ds(160 * i, 160) for i in range(4)]
    for copy in send_out([(out_ref.at[at, :], out_hbm.at[at, :]) for at in pieces], sems):
        copy.wait()


def tables_kernel(
    where_ref, rate_ref, sine_ref, rate_row_ref, rate_col_ref, row_ref, order_ref,
    sine_out, x_out, modes_out, modes_t_out, split_out, decay_out, once_out, twice_out, rows_out
):
    del order_ref
    by_modes = mode_ordered(sine_ref)
    for out, table in (
        (sine_out, split(sine_rows(sine_ref, 0, N, 1))),
        (x_out, x_ordered(sine_ref)),
        (modes_out, split(by_modes)),
        (modes_t_out, split(by_modes.T)),
    ):
        out[0], out[1] = table
    for i in range(2):
        split_out[2 * i], split_out[2 * i + 1] = split(sine_rows(sine_ref, i, HALF, 2))
    decay = 1.0 / (rate_col_ref[...] + (rate_row_ref[...] + 64.0 * rate_ref[where_ref[2]]))
    decay_out[...] = decay
    sine = split(sine_rows(sine_ref, 0, N, 1))
    response = decay * sine_ref[pl.ds(0, N), 0:1]
    for k, out in enumerate((once_out, twice_out)):
        out[0], out[1] = split(dot3(response, sine, TN))
        rows_out[8 * k : 8 * k + 8] = dot3(row_ref[...], response)
        response = decay * response


def matrices_kernel(jac_ref, field_ref, tile_ref, fixed_ref, operators_ref, out_ref):
    field, tile = field_ref[...], tile_ref[...]

    def spread(d):
        return dot_hot(hot_dot(field, jac_ref[d]), field, NT)

    def tiled(d):
        return dot_hot(hot_dot(tile, operators_ref[d]), tile, NT)

    by_x = spread(0)
    own = by_x * tiled(0) + spread(1) * tiled(1) + spread(2) * tiled(2)
    out_ref[0:320] = fixed_ref[0] + own
    out_ref[320:640] = fixed_ref[1] + by_x * tiled(3)
    out_ref[640:960] = fixed_ref[2] + by_x * tiled(4)


def modes_kernel(
    where_ref, got_ref, surface_ref, sine_ref, split_ref, by_modes_ref, decay_ref, row_ref,
    matrix_ref, before_ref, after_ref, elem_ref, owner_ref, patch_ref, modes_ref, out_ref, *, count
):
    group = where_ref[0]
    sine = sine_ref[0], sine_ref[1]
    modes = 0.0
    for i in range(2):
        part = jnp.concatenate([rows(got_ref, 2 * i + h, HALF, 5) for h in range(2)], axis=1)
        by_z = dot3(sine, part, NT)
        modes = modes + dot3(by_z, (split_ref[2 * i], split_ref[2 * i + 1]))
    modes = decay_ref[...] * modes
    surface_row = dot3(row_ref[...], modes)[0:1]
    modes_ref[...] = decay_ref[...] * modes

    fluid = rows(got_ref, 4, HALF, 5)
    square = (HALF, HALF)
    lane = iota(square, 1)
    fluid_pair = split(fluid)
    sums = [[0.0, 0.0], [0.0, 0.0]]
    counts = [0.0, 0.0]
    count_lanes = 0.0
    for i in range(2):
        ids = fluid[:, i * 64 + 32 : i * 64 + 33].astype(jnp.int32) - 1
        count_lanes = count_lanes + jnp.sum(jnp.where(ids == lane, 1.0, 0.0), axis=0, keepdims=True)
        for f in range(2):
            pick = hot_of(iota(square, 0) == i * 64 + f * 16 + lane % 16)
            values = dot(fluid_pair[0], pick) + dot(fluid_pair[1], pick)
            for xl in range(2):
                mask = ids == xl * 8 + lane // 16
                sums[f][xl] = sums[f][xl] + jnp.sum(
                    jnp.where(mask, values, 0.0), axis=0, keepdims=True
                )
                if f == 0:
                    counts[xl] = counts[xl] + jnp.sum(
                        jnp.where(mask, 1.0, 0.0), axis=0, keepdims=True
                    )
    heat = [sums[0][xl] - counts[xl] * surface_ref[xl : xl + 1, :] for xl in range(2)]
    tail = jnp.where(lane < 16, count_lanes, 0.0)
    edge_rows = []
    for t, (part, ref, element) in enumerate(((2, before_ref, 0), (1, after_ref, count - 1))):
        met = elem_ref[...] == element
        owner, patch = [
            jnp.sum(jnp.where(met, value, 0).astype(F32), axis=1, keepdims=True).astype(jnp.int32)
            for value in (owner_ref[...] + 1, patch_ref[...])
        ]
        x_of_slot = patch // 8 * HALF + (owner - 1) % 2 * 64 + (owner - 1) // 2
        tail = jnp.where(lane == 40 + t, jnp.where(owner > 0, x_of_slot + 1, 0).astype(F32), tail)
        tables = matrix_ref[16 * part : 16 * part + 16]
        column = jnp.sum(tables * ref[0:1, 0:320], axis=1, keepdims=True)
        node, lane16 = iota((16, HALF), 0), iota((16, HALF), 1)
        used = (lane16 % 16 == node) & (lane16 // 16 == patch % 8)
        edge_rows.append(jnp.sum(jnp.where(used, column, 0.0), axis=0, keepdims=True))
    for k in range(2):
        by_modes = []
        for part in range(2):
            table = by_modes_ref[part, k * HALF : (k + 1) * HALF, :].astype(F32)
            own = jnp.where(group == 0, table[:, :HALF], table[:, HALF:])
            by_modes.append(own.astype(BF16))
        by_modes = tuple(by_modes)
        for xl in range(2):
            column = dot3(by_modes, jnp.broadcast_to(sums[1][xl], (8, HALF)), NT)[:, 0:1]
            tail = jnp.where(lane == 16 + 2 * k + xl, column, tail)
        for t in range(2):
            column = dot3(by_modes, jnp.broadcast_to(edge_rows[t], (8, HALF)), NT)[:, 0:1]
            tail = jnp.where(lane == 32 + 2 * t + k, column, tail)
    shared = [surface_row[:, :HALF], surface_row[:, HALF:], heat[0], heat[1]]
    for r in range(4):
        out_ref[pl.ds(r, HALF, 5), :] = jnp.broadcast_to(shared[r], square)
    out_ref[pl.ds(4, HALF, 5), :] = tail


def solve_kernel(
    where_ref, got_ref, other_ref, modes_ref, response_ref, sine_ref, pair_ref, x_ref, by_modes_ref,
    from_modes_ref, split_ref, once_ref, twice_ref, rows_ref, row_ref,
    surface_hbm, out_hbm, heat_ref, surface_ref, out_ref, sem, sems
):
    core, me = where_ref[1], where_ref[2]
    first = jnp.full((HALF, HALF), core, jnp.int32) == 0
    ordered = []
    for r in range(5):
        mine, theirs = rows(got_ref, r, HALF, 5), rows(other_ref, r, HALF, 5)
        ordered.append((jnp.where(first, mine, theirs), jnp.where(first, theirs, mine)))

    modes = split(modes_ref[...])
    sine = pair_ref[0], pair_ref[1]
    back = [
        dot3(dot3((split_ref[2 * xl], split_ref[2 * xl + 1]), modes, NT), sine) for xl in range(2)
    ]
    final_row = dot3(row_ref[...], modes)[0:1]

    def block(g, r):
        return jnp.concatenate([ordered[r][k][g * 64 : (g + 1) * 64] for k in range(2)], axis=0)

    halves = [
        tuple(by_modes_ref[part, :, g * HALF : (g + 1) * HALF] for part in range(2))
        for g in range(2)
    ]
    by_x = x_ref[0], x_ref[1]
    heat_modes = 0.0
    for xl in range(2):
        by_y = 0.0
        for g in range(2):
            by_y = by_y + dot3(halves[g], block(g, 2 + xl), NT)
        at = slice(xl * HALF, (xl + 1) * HALF)
        heat_modes = heat_modes + dot3(by_y, (by_x[0][at], by_x[1][at]))
    heat_ref[...] = heat_modes
    given = jnp.concatenate(
        [jnp.concatenate([ordered[h][k] for h in range(2)], axis=1) for k in range(2)], axis=0
    )
    surface = dot3((from_modes_ref[0], from_modes_ref[1]), given + response_ref[...] * heat_modes)
    surface = dot3(surface, by_x, NT)
    surface_ref[...] = surface
    copy = pltpu.make_async_copy(surface_ref, surface_hbm, sem)
    copy.start()
    square = (HALF, HALF)
    tails = [block(g, 4) for g in range(2)]
    tail_pairs = [tail.astype(BF16) for tail in tails]
    expand = [hot_of(iota(square, 1) == xl * 8 + iota(square, 0) // 16) for xl in range(2)]
    count = jnp.concatenate(
        [
            jnp.concatenate([dot(expand[xl], tail_pairs[g], NT) for xl in range(2)], axis=1)
            for g in range(2)
        ],
        axis=0,
    )
    own_sine = jnp.broadcast_to(sine_rows(sine_ref, me, 1, 1), (8, N))
    reduced = dot3(own_sine, count * surface)
    tail_sum = tails[0] + tails[1]
    lane8 = iota((8, HALF), 1)
    later = jnp.concatenate(
        [hot_dot(hot_of(lane8 == 16 + 2 * core + xl), tail_sum, NT) for xl in range(2)], axis=1
    )
    wide = iota((HALF, N), 1)
    for k in range(2):
        tail = ordered[4][k]
        for t in range(2):
            value = jnp.where(first[:, 0:1], tail[:, 32 + 2 * t : 33 + 2 * t], tail[:, 33 + 2 * t : 34 + 2 * t])
            met = tail[:, 40 + t : 41 + t].astype(jnp.int32) - 1 == wide
            later = later + jnp.sum(jnp.where(met, value, 0.0), axis=0, keepdims=True)
    heat1 = dot3(later - 0.7 * reduced, by_x)[0:1]
    heat0 = heat_ref[pl.ds(core * HALF + me // 2, 1), :]
    final_row = final_row + heat0 * rows_ref[8:9] + heat1 * rows_ref[0:1]
    for xl in range(2):
        table = sine_rows(sine_ref, xl, HALF, 2)
        part = back[xl] + dot3(table * heat0, (twice_ref[0], twice_ref[1]))
        part = part + dot3(table * heat1, (once_ref[0], once_ref[1]))
        for h in range(2):
            out_ref[pl.ds(2 * xl + h, HALF, 5), :] = part[:, h * HALF : (h + 1) * HALF]
    for k in range(2):
        out_ref[pl.ds(4 + 5 * k, 64, 10), :] = jnp.broadcast_to(
            final_row[:, k * HALF : (k + 1) * HALF], (64, HALF)
        )
    pieces = [(160 * i, 640 * g + 160 * i) for i in range(4) for g in range(2)]
    for sending in send_out(
        [(out_ref.at[pl.ds(a, 160), :], out_hbm.at[pl.ds(b, 160), :]) for a, b in pieces], sems
    ):
        sending.wait()
    copy.wait()


def met_values(surface, owner, patch):
    x_of_slot = patch // 8 * HALF + owner % 2 * 64 + owner // 2
    x_hot = hot_of(iota((N, HALF), 0) == x_of_slot)
    met = dot_hot(surface, x_hot)
    return jnp.where(iota((HALF, HALF), 0) // 16 == patch % 8, met, 0.0)


def folded(met):
    fold = hot_of(iota((16, HALF), 0) == iota((16, HALF), 1) % 16)
    return hot_dot(fold, met)


def stepped(extended, matrix_ref):
    fluid = split(extended)
    width = extended.shape[1]
    own, following, preceding = [
        dot3(matrix_ref[pl.ds(320 * i, 320), :], fluid) for i in range(3)
    ]
    return own + pltpu.roll(following, width - 1, 1) + pltpu.roll(preceding, 1, 1)


def step_kernel(where_ref, fluid_ref, matrix_ref, before_ref, after_ref, out_ref):
    count = fluid_ref.shape[1]
    me = where_ref[2]
    lane = iota((320, HALF), 1)
    following, preceding = after_ref[...].T[0:320], before_ref[...].T[0:320]
    halo = jnp.zeros((320, HALF), F32)
    for at, column in (
        (0, following[:, 0:1]),
        (1, following[:, 1:2]),
        (HALF - 1, preceding[:, 0:1]),
        (HALF - 2, preceding[:, 1:2]),
    ):
        halo = jnp.where(lane == at, column, halo)
    result = stepped(jnp.concatenate([fluid_ref[...], halo], axis=1), matrix_ref)
    edge = result[:, count:]
    beyond = ((lane == 0) & (me == 255)) | ((lane == HALF - 1) & (me == 0))
    out_ref[:, :count] = result[:, :count]
    out_ref[:, count:] = jnp.where(beyond, 0.0, edge)


def second_kernel(
    where_ref, fluid_ref, surface_ref, trace_ref, matrix_ref, before_ref, after_ref, elem_ref,
    owner_ref, patch_ref, sine_ref, out_ref, later_ref, slots_ref, walls_ref
):
    group, me = where_ref[0], where_ref[2]
    width = fluid_ref.shape[1]
    count = width - HALF
    own_surface = surface_ref[pl.ds(pl.multiple_of(group * HALF, HALF), HALF), :]
    elem_hot = hot_of(column_of(elem_ref[...]) == iota((HALF, count), 1))
    met = folded(met_values(own_surface, owner_ref[...], patch_ref[...]))
    source = GAIN * dot_hot(met - trace_ref[...], elem_hot)
    square = (16, HALF)
    edge = jnp.zeros(square, F32)
    for ref, at, device in ((after_ref, 0, me + 1), (before_ref, HALF - 1, me - 1)):
        owner = ref[2:3, 0:1].astype(jnp.int32) - 1
        patch = ref[2:3, 1:2].astype(jnp.int32)
        side = jnp.clip(device, 0, 255) // HALF
        near = surface_ref[pl.ds(pl.multiple_of(side * HALF, HALF), HALF), :]
        lanes = jnp.zeros((1, HALF), jnp.int32)
        value = folded(met_values(near, owner + lanes, patch + lanes))
        column = ref[...].T
        value = GAIN * (value - (column[256:272, 0:1] - column[0:16, 0:1]))
        used = (iota(square, 1) == at) & (owner >= 0)
        edge = jnp.where(used, value, edge)
    slot_hot = hot_of(iota((N, HALF), 0) == 2 * owner_ref[...] + patch_ref[...] // 8)
    slots_ref[...] = dot_hot(sine_rows(sine_ref, 0, N, 1), slot_hot)
    walls = fluid_ref[256:272] + jnp.concatenate([source, edge], axis=1)
    later_ref[...] = dot_hot(walls[:, :count] - fluid_ref[0:16, :count], elem_hot, NT)
    extended = jnp.concatenate([fluid_ref[0:256], walls, fluid_ref[272:320]], axis=0)
    result = stepped(extended, matrix_ref)[:, :count]
    out_ref[...] = result
    walls_ref[...] = result[256:272]


def solid_half(h, where_ref, got_ref, sine_ref, solid_hbm, solid_ref, sem):
    by_y = split(sine_ref[pl.ds(pl.multiple_of(where_ref[0] * N, N), N), :])
    for xl in range(2):
        part = rows(got_ref, 2 * xl + h, N, 5)
        solid_ref[pl.ds(xl, HALF, 2), :] = dot3(part, by_y, TN)
    copy = pltpu.make_async_copy(solid_ref, solid_hbm.at[pl.ds(h * N, N), :], sem)
    copy.start()
    return copy


def solid_kernel(where_ref, got_ref, sine_ref, solid_hbm, solid_ref, sem):
    solid_half(0, where_ref, got_ref, sine_ref, solid_hbm, solid_ref, sem).wait()


def last_kernel(
    where_ref, got_ref, mine_ref, other_ref, sine_ref, slots_ref, later_ref, elem_ref, patch_ref,
    walls_ref, fluid_hbm, half_hbm, out_hbm, solid_hbm, out_ref, solid_ref, sem, solid_sem
):
    group, core = where_ref[0], where_ref[1]
    solid = solid_half(1, where_ref, got_ref, sine_ref, solid_hbm, solid_ref, solid_sem)
    first = jnp.full((N, HALF), core, jnp.int32) == 0
    mine, other = mine_ref[...], other_ref[...]
    given = jnp.concatenate([jnp.where(first, mine, other), jnp.where(first, other, mine)], axis=1)
    own_rows = sine_rows(sine_ref, pl.multiple_of(group * HALF, HALF), HALF, 1)
    met = dot3(own_rows, dot3(given, slots_ref[...]))
    met = folded(jnp.where(iota((HALF, HALF), 0) // 16 == patch_ref[...] % 8, met, 0.0))
    elem_hot = hot_of(column_of(elem_ref[...]) == iota((HALF, walls_ref.shape[1]), 1))
    out_ref[...] = walls_ref[...] + GAIN * dot_hot(met - later_ref[...], elem_hot)
    copy = pltpu.make_async_copy(out_ref, out_hbm.at[pl.ds(256, 16), :], sem)
    copy.start()
    solid.wait()
    copy.wait()


def call(kernel, outs, args, scalars=0, scratch=(), aliases=None, specs=None, out_specs=None, cost=None, limit=40):
    whole = pl.BlockSpec(memory_space=pltpu.VMEM)
    given = [pl.BlockSpec(memory_space=pltpu.SMEM)] * scalars + [whole] * (len(args) - scalars)
    return pl.pallas_call(
        kernel,
        out_shape=[
            jax.ShapeDtypeStruct(*(out if isinstance(out[0], tuple) else (out, F32))) for out in outs
        ],
        in_specs=specs or given,
        out_specs=out_specs or [whole] * len(outs),
        scratch_shapes=list(scratch),
        input_output_aliases=aliases or {},
        cost_estimate=pl.CostEstimate(flops=int(cost or 1e8), bytes_accessed=1 << 20, transcendentals=0),
        compiler_params=pltpu.CompilerParams(vmem_limit_bytes=limit << 20),
    )(*args)


def exchange(payload, axes):
    chunks = payload.reshape(payload.shape[0], 1, HALF)
    return lax.all_to_all(chunks, axes, split_axis=0, concat_axis=0, tiled=True).reshape(payload.shape)


def on_device(fluid_state, flux_jacobian, solid_temp, iface_elem, iface_owner, iface_patch):
    me = lax.axis_index(ALL)
    where = jnp.stack([me // HALF, me % 2, me]).astype(jnp.int32)
    fluid0 = fluid_state.reshape(320, -1)
    count = fluid0.shape[1]
    solid = solid_temp.reshape(2 * N, HALF)
    elem, owner, patch = iface_elem[None, :], iface_owner.reshape(1, HALF), iface_patch[None, :]
    smem = pl.BlockSpec(memory_space=pltpu.SMEM)
    vmem = pl.BlockSpec(memory_space=pltpu.VMEM)
    hbm = pl.BlockSpec(memory_space=pltpu.HBM)

    far = lax.ppermute(solid, "g", [(0, 1), (1, 0)])
    near, trace0, surface0, first, last, wall_matrix, far_table = call(
        near_kernel,
        [(5 * HALF, HALF), (16, HALF), (2, HALF), (8, 384), (8, 384), (48, 320), (HALF, HALF)],
        [where, flux_jacobian, fluid0, solid, Q_HALVES, WALL_TABLES, elem, owner, patch],
        specs=[smem] + [hbm] * 8,
        limit=52,
        scratch=[
            pltpu.VMEM(flux_jacobian.shape, F32),
            pltpu.VMEM(fluid0.shape, F32),
            pltpu.VMEM(solid.shape, F32),
            pltpu.VMEM(Q_HALVES.shape, F32),
            pltpu.VMEM(WALL_TABLES.shape, F32),
            pltpu.VMEM((1, HALF), jnp.int32),
            pltpu.VMEM((1, HALF), jnp.int32),
            pltpu.VMEM((1, HALF), jnp.int32),
            pltpu.SemaphoreType.DMA((12,)),
        ],
    )
    before = lax.ppermute(last, ALL, [(i, i + 1) for i in range(255)])
    after = lax.ppermute(first, ALL, [(i + 1, i) for i in range(255)])
    (pay1,) = call(
        far_kernel,
        [(5 * HALF, HALF)],
        [far, far_table, near],
        out_specs=[hbm],
        scratch=[pltpu.VMEM((5 * HALF, HALF), F32), pltpu.SemaphoreType.DMA((4,))],
    )
    got1 = exchange(pay1, SUB)
    tables = call(
        tables_kernel,
        [((2, N, N), BF16)] * 4
        + [((4, HALF, N), BF16), (N, N), ((2, N, N), BF16), ((2, N, N), BF16), (16, N)],
        [where, RATE_LIST, Q_HALVES, RATE_ROW, RATE_COLUMN, SURFACE_ROW, surface0],
        scalars=2,
    )
    sine_pair, x_pair, modes_pair, modes_t_pair, split_pair, decay, once, twice, heat_rows = tables
    jacobian = jnp.pad(flux_jacobian, ((0, 0), (0, 3), (0, 3)))
    (matrix,) = call(
        matrices_kernel,
        [(960, 320)],
        [jacobian, FIELD_HOT, TILE_HOT, np.stack([FIXED, NEXT_FIXED, PREV_FIXED]), OPERATORS],
    )
    (fluid1,) = call(
        step_kernel,
        [(320, count + HALF)],
        [where, fluid0, matrix, before, after],
        scalars=1,
        cost=2e9,
    )
    modes, pay2 = call(
        functools.partial(modes_kernel, count=count),
        [(N, N), (5 * HALF, HALF)],
        [where, got1, surface0, sine_pair, split_pair, modes_pair, decay, SURFACE_ROW,
         wall_matrix, before, after, elem, owner, patch],
        scalars=1,
    )
    got2 = exchange(pay2, SAME_CORE)
    other = lax.ppermute(got2, "c", [(0, 1), (1, 0)])
    surface1, pay3 = call(
        solve_kernel,
        [(N, N), (5 * N, HALF)],
        [where, got2, other, modes, RESPONSE, Q_HALVES, sine_pair, x_pair, modes_pair, modes_t_pair,
         split_pair, once, twice, heat_rows, SURFACE_ROW],
        scalars=1,
        out_specs=[hbm, hbm],
        scratch=[
            pltpu.VMEM((N, N), F32),
            pltpu.VMEM((N, N), F32),
            pltpu.VMEM((5 * HALF, HALF), F32),
            pltpu.SemaphoreType.DMA,
            pltpu.SemaphoreType.DMA((8,)),
        ],
    )
    got3 = exchange(pay3, ALL)
    fluid2, trace1, slots, walls2 = call(
        second_kernel,
        [(320, count), (16, HALF), (N, HALF), (16, count)],
        [where, fluid1, surface1, trace0, matrix, before, after, elem, owner, patch, Q_HALVES],
        scalars=1,
        cost=2e9,
    )
    got3, fluid2, trace1, slots, walls2 = lax.optimization_barrier(
        (got3, fluid2, trace1, slots, walls2)
    )
    mine = got3.reshape(N, 5, 1, HALF)[:, 4].reshape(N, HALF)
    far_row = lax.ppermute(mine, "c", [(0, 1), (1, 0)])
    (solid_out,) = call(
        solid_kernel,
        [(2 * N, HALF)],
        [where, got3, Q_HALVES],
        scalars=1,
        out_specs=[hbm],
        scratch=[pltpu.VMEM((N, HALF), F32), pltpu.SemaphoreType.DMA],
    )
    fluid2, solid_out = call(
        last_kernel,
        [(320, count), (2 * N, HALF)],
        [where, got3, mine, far_row, Q_HALVES, slots, trace1, elem, patch, walls2, fluid2, solid_out],
        specs=[smem] + [vmem] * 9 + [hbm] * 2,
        out_specs=[hbm] * 2,
        aliases={10: 0, 11: 1},
        scratch=[
            pltpu.VMEM((16, count), F32),
            pltpu.VMEM((N, HALF), F32),
            pltpu.SemaphoreType.DMA,
            pltpu.SemaphoreType.DMA,
        ],
    )
    return fluid2.reshape(fluid_state.shape), solid_out.reshape(solid_temp.shape)


def solution(mesh):
    fine = Mesh(mesh.devices.reshape(2, 2, 4, 8, 2), ALL)
    placed = (
        P(None, None, ALL),
        P(),
        P(None, SUB, "g"),
        P(ALL),
        P(ALL, None),
        P(ALL),
    )
    return jax.shard_map(
        on_device,
        mesh=fine,
        in_specs=placed,
        out_specs=(P(None, None, ALL), P(None, SUB, "g")),
        check_vma=False,
    )
```

```python
import functools

import jax
import jax.numpy as jnp
import ml_dtypes
import numpy as np
from jax import lax
from jax.experimental import pallas as pl
from jax.experimental.pallas import tpu as pltpu
from jax.sharding import Mesh, PartitionSpec as P

ALL = ("g", "yl", "x", "z", "c")
SUB = ("yl", "x", "z", "c")
SAME_CORE = ("g", "yl", "x", "z")
N = 256
HALF = 128
DT = 0.05
VISC = 0.05
GAIN = 0.3
F32 = jnp.float32
BF16 = jnp.bfloat16
NN = ((1,), (0,))
NT = ((1,), (1,))
TN = ((0,), (0,))


def sine_table(length):
    numbers = np.arange(length) + 1
    phases = numbers[:, None] * numbers[None, :] % (2 * (length + 1))
    return np.sqrt(2.0 / (length + 1)) * np.sin(np.pi * phases / (length + 1))


def rates(length):
    return 2.0 - 2.0 * np.cos(np.pi * (np.arange(length) + 1) / (length + 1))


SINE = sine_table(N)
RATES = rates(N)
MODE_ORDER = np.array([2 * q + k for k in range(2) for q in range(HALF)])


def surface_response():
    total = np.zeros((N, N))
    for c in range(N):
        total += SINE[0, c] ** 2 / (1.0 + 64.0 * (RATES[c] + RATES[:, None] + RATES[None, :]))
    return total


Q = SINE.astype(np.float32)
Q_HALVES = np.concatenate([Q[:, :HALF], Q[:, HALF:]], axis=0)
RESPONSE = surface_response()[MODE_ORDER].astype(np.float32)


def lobatto_derivative():
    points = np.array([-1.0, -1.0 / np.sqrt(5.0), 1.0 / np.sqrt(5.0), 1.0])
    weights = np.array(
        [1.0 / np.prod([points[j] - points[k] for k in range(4) if k != j]) for j in range(4)]
    )
    deriv = np.zeros((4, 4))
    for i in range(4):
        for j in range(4):
            if i != j:
                deriv[i, j] = weights[j] / weights[i] / (points[i] - points[j])
        deriv[i, i] = -np.sum(deriv[i])
    return deriv


def operator_parts():
    deriv, eye = lobatto_derivative(), np.eye(4)
    along = [
        np.kron(eye, np.kron(eye, deriv)),
        np.kron(eye, np.kron(deriv, eye)),
        np.kron(deriv, np.kron(eye, eye)),
    ]
    second = sum(d @ d for d in along)
    pick = np.zeros((4, 4, 4, 4))
    for i in range(4):
        for j in range(4):
            pick[i, j, i, j] = 1.0
    eye16 = np.eye(16)
    right, left = np.kron(eye16, pick[3, 3]), np.kron(eye16, pick[0, 0])
    right_from, left_from = np.kron(eye16, pick[3, 0]), np.kron(eye16, pick[0, 3])
    fixed = np.kron(np.eye(5), np.eye(64) - 0.15 * right - 0.15 * left)
    fixed = fixed + DT * VISC * np.kron(np.diag([0.0, 1.0, 1.0, 1.0, 1.0]), second)
    by_x = -DT * along[0] + 0.15 * right - 0.15 * left
    return [
        np.asarray(a, np.float32)
        for a in (
            fixed,
            by_x,
            -DT * along[1],
            -DT * along[2],
            np.kron(np.eye(5), 0.15 * right_from),
            -0.15 * right_from,
            np.kron(np.eye(5), 0.15 * left_from),
            0.15 * left_from,
        )
    ]


FIXED, BY_X, BY_Y, BY_Z, NEXT_FIXED, NEXT_X, PREV_FIXED, PREV_X = operator_parts()


def wall_tables():
    groups = []
    for fixed, tables in ((FIXED, (BY_X, BY_Y, BY_Z)), (NEXT_FIXED, (NEXT_X,)), (PREV_FIXED, (PREV_X,))):
        groups.append(fixed[256:272] - fixed[0:16])
        groups += [np.tile(t[:16], (1, 5)) for t in tables]
    return np.stack(groups).astype(np.float32)


WALL_TABLES = wall_tables()
RATE_LIST = RATES.astype(np.float32)
RATE_ROW = (1.0 + 64.0 * RATES)[None, :].astype(np.float32)
RATE_COLUMN = (64.0 * RATES)[:, None].astype(np.float32)
SURFACE_ROW = np.broadcast_to(Q[:1], (8, N)).copy()
FIELD_HOT = np.pad(np.kron(np.eye(5), np.ones((64, 1))), ((0, 0), (0, 3))).astype(ml_dtypes.bfloat16)
TILE_HOT = np.kron(np.ones((5, 1)), np.eye(64)).astype(ml_dtypes.bfloat16)
OPERATORS = np.stack([BY_X, BY_Y, BY_Z, NEXT_X, PREV_X])


def split(value):
    high = value.astype(BF16)
    return high, (value - high.astype(F32)).astype(BF16)


def dot(a, b, dims=NN):
    return lax.dot_general(a, b, (dims, ((), ())), preferred_element_type=F32)


def dot3(a, b, dims=NN):
    a = split(a) if not isinstance(a, tuple) else a
    b = split(b) if not isinstance(b, tuple) else b
    a = jnp.concatenate([a[0], a[1], a[0]], axis=dims[0][0])
    b = jnp.concatenate([b[0], b[0], b[1]], axis=dims[1][0])
    return dot(a, b, dims)


def hot_dot(hot, b, dims=NN):
    high, low = split(b)
    return dot(hot, high, dims) + dot(hot, low, dims)


def dot_hot(a, hot, dims=NN):
    high, low = split(a)
    return dot(high, hot, dims) + dot(low, hot, dims)


def hot_of(condition):
    return jnp.where(condition, 1.0, 0.0).astype(BF16)


def iota(shape, dim):
    return lax.broadcasted_iota(jnp.int32, shape, dim)


def rows(ref, first, count, stride):
    return ref[pl.ds(first, count, stride) if stride > 1 else pl.ds(first, count), :]


def sine_rows(ref, first, count, stride):
    return jnp.concatenate([rows(ref, h * N + first, count, stride) for h in range(2)], axis=1)


def x_ordered(sine_ref):
    blocks = [sine_rows(sine_ref, 2 * k + i, 64, 4) for i in range(2) for k in range(2)]
    return split(jnp.concatenate(blocks, axis=0))


def mode_ordered(sine_ref):
    return jnp.concatenate([sine_rows(sine_ref, k, HALF, 2) for k in range(2)], axis=0)


def column_of(row):
    return jnp.broadcast_to(row.astype(F32), (8, row.shape[1])).T[:, 0:1].astype(jnp.int32)


def near_kernel(
    where_ref, jac_hbm, fluid_hbm, solid_hbm, sine_hbm, table_hbm, elem_hbm, owner_hbm, patch_hbm,
    out_ref, trace_ref, surface_ref, first_ref, last_ref, matrix_ref, far_table_ref,
    jac_ref, fluid_ref, solid_ref, sine_ref, table_ref, elem_ref, owner_ref, patch_ref, sems
):
    group = where_ref[0]
    count = fluid_ref.shape[1]
    copies = [
        pltpu.make_async_copy(jac_hbm, jac_ref, sems.at[0]),
        pltpu.make_async_copy(solid_hbm, solid_ref, sems.at[1]),
        pltpu.make_async_copy(sine_hbm, sine_ref, sems.at[2]),
        pltpu.make_async_copy(table_hbm, table_ref, sems.at[3]),
        pltpu.make_async_copy(elem_hbm, elem_ref, sems.at[4]),
        pltpu.make_async_copy(owner_hbm, owner_ref, sems.at[5]),
        pltpu.make_async_copy(patch_hbm, patch_ref, sems.at[6]),
    ]
    for i in range(5):
        at = pl.ds(64 * i, 64)
        copies.append(pltpu.make_async_copy(fluid_hbm.at[at, :], fluid_ref.at[at, :], sems.at[7 + i]))
    for copy in copies:
        copy.start()
    for copy in copies[:7]:
        copy.wait()

    near, far = [
        sine_ref[pl.ds(pl.multiple_of(half * N + group * HALF, HALF), HALF), :]
        for half in (group, 1 - group)
    ]
    far_table_ref[...] = far
    near = split(near)
    for i in range(2):
        modes = dot3(near, rows(solid_ref, i, N, 2), NT)
        for h in range(2):
            out_ref[pl.ds(2 * i + h, HALF, 5), :] = modes[:, h * HALF : (h + 1) * HALF]
    surface_ref[...] = solid_ref[0:2]

    field = iota((1, 320), 1) // 64
    coefficients = []
    for d in range(3):
        change = jac_ref[d, 4:5, :] - jac_ref[d, 0:1, :]
        row = jnp.zeros((1, 320), F32)
        for f in range(5):
            row = jnp.where(field == f, change[:, f : f + 1], row)
        coefficients.append(row)
    own = table_ref[0]
    for d in range(3):
        own = own + coefficients[d] * table_ref[1 + d]
    matrix_ref[0:16] = own
    matrix_ref[16:32] = table_ref[4] + coefficients[0] * table_ref[5]
    matrix_ref[32:48] = table_ref[6] + coefficients[0] * table_ref[7]

    owner, patch, elem = owner_ref[...], patch_ref[...], elem_ref[...]
    square = (HALF, HALF)
    same = (column_of(owner) == owner) & (iota(square, 0) < iota(square, 1))
    place = jnp.sum(jnp.where(same, 1.0, 0.0), axis=0, keepdims=True)
    elem_hot = hot_of(column_of(elem) == iota((HALF, count), 1))

    for copy in copies[7:]:
        copy.wait()
    lane = iota((1, 384), 1)
    gap = jnp.zeros((1, 64), F32)
    for block, at, out, element in (
        (fluid_ref[:, 0:HALF], (0, 1), first_ref, 0),
        (fluid_ref[:, count - HALF : count], (HALF - 1, HALF - 2), last_ref, count - 1),
    ):
        turned = block.T
        met = elem == element
        edge_owner = jnp.sum(jnp.where(met, owner + 1, 0).astype(F32), axis=1, keepdims=True)
        edge_patch = jnp.sum(jnp.where(met, patch, 0).astype(F32), axis=1, keepdims=True)
        out[0:1] = jnp.concatenate([turned[at[0] : at[0] + 1], gap], axis=1)
        out[1:2] = jnp.concatenate([turned[at[1] : at[1] + 1], gap], axis=1)
        out[2:3] = jnp.where(lane == 0, edge_owner, jnp.where(lane == 1, edge_patch, 0.0))
        out[3:8] = jnp.zeros((5, 384), F32)

    walls = dot3(matrix_ref[...], fluid_ref[...])
    wall0 = fluid_ref[256:272] - fluid_ref[0:16]
    lane = iota(wall0.shape, 1)
    following = pltpu.roll(walls[16:32], count - 1, 1)
    preceding = pltpu.roll(walls[32:48], 1, 1)
    later = walls[0:16] + jnp.where(lane == count - 1, 0.0, following)
    later = later + jnp.where(lane == 0, 0.0, preceding)
    values = dot_hot(jnp.concatenate([wall0, later - GAIN * wall0], axis=0), elem_hot, NT)
    trace_ref[...] = values[:16]
    ids = jnp.broadcast_to((patch + 1).astype(F32), (8, HALF))
    filler = jnp.zeros((24, HALF), F32)
    sent = jnp.concatenate([values, ids, filler], axis=0)
    none = jnp.zeros((64, HALF), F32)
    arranged = 0.0
    for i in range(2):
        hot = hot_of((iota(square, 0) == owner) & (place == float(i)))
        padded = jnp.concatenate([sent, none] if i == 0 else [none, sent], axis=0)
        arranged = arranged + hot_dot(hot, padded, NT)
    out_ref[pl.ds(4, HALF, 5), :] = arranged


def send_out(pairs, sems):
    copies = [pltpu.make_async_copy(a, b, sems.at[i]) for i, (a, b) in enumerate(pairs)]
    for copy in copies:
        copy.start()
    return copies


def far_kernel(far_ref, table_ref, near_ref, out_hbm, out_ref, sems):
    table = split(table_ref[...])
    out_ref[pl.ds(4, HALF, 5), :] = rows(near_ref, 4, HALF, 5)
    for i in range(2):
        modes = dot3(table, rows(far_ref, i, N, 2), NT)
        for h in range(2):
            part = modes[:, h * HALF : (h + 1) * HALF]
            out_ref[pl.ds(2 * i + h, HALF, 5), :] = rows(near_ref, 2 * i + h, HALF, 5) + part
    pieces = [pl.ds(160 * i, 160) for i in range(4)]
    for copy in send_out([(out_ref.at[at, :], out_hbm.at[at, :]) for at in pieces], sems):
        copy.wait()


def tables_kernel(
    where_ref, rate_ref, sine_ref, rate_row_ref, rate_col_ref, order_ref,
    sine_out, x_out, modes_out, modes_t_out, split_out, decay_out
):
    del order_ref
    by_modes = mode_ordered(sine_ref)
    for out, table in (
        (sine_out, split(sine_rows(sine_ref, 0, N, 1))),
        (x_out, x_ordered(sine_ref)),
        (modes_out, split(by_modes)),
        (modes_t_out, split(by_modes.T)),
    ):
        out[0], out[1] = table
    for i in range(2):
        split_out[2 * i], split_out[2 * i + 1] = split(sine_rows(sine_ref, i, HALF, 2))
    decay_out[...] = 1.0 / (rate_col_ref[...] + (rate_row_ref[...] + 64.0 * rate_ref[where_ref[2]]))


def matrices_kernel(jac_ref, field_ref, tile_ref, fixed_ref, operators_ref, out_ref):
    field, tile = field_ref[...], tile_ref[...]

    def spread(d):
        return dot_hot(hot_dot(field, jac_ref[d]), field, NT)

    def tiled(d):
        return dot_hot(hot_dot(tile, operators_ref[d]), tile, NT)

    by_x = spread(0)
    own = by_x * tiled(0) + spread(1) * tiled(1) + spread(2) * tiled(2)
    out_ref[0:320] = fixed_ref[0] + own
    out_ref[320:640] = fixed_ref[1] + by_x * tiled(3)
    out_ref[640:960] = fixed_ref[2] + by_x * tiled(4)


def modes_kernel(
    where_ref, got_ref, surface_ref, sine_ref, split_ref, by_modes_ref, decay_ref, row_ref,
    matrix_ref, before_ref, after_ref, elem_ref, owner_ref, patch_ref, modes_ref, out_ref, *, count
):
    group = where_ref[0]
    sine = sine_ref[0], sine_ref[1]
    modes = 0.0
    for i in range(2):
        part = jnp.concatenate([rows(got_ref, 2 * i + h, HALF, 5) for h in range(2)], axis=1)
        by_z = dot3(sine, part, NT)
        modes = modes + dot3(by_z, (split_ref[2 * i], split_ref[2 * i + 1]))
    modes_ref[...] = modes
    surface_row = dot3(row_ref[...], decay_ref[...] * modes)[0:1]

    fluid = rows(got_ref, 4, HALF, 5)
    square = (HALF, HALF)
    lane = iota(square, 1)
    fluid_pair = split(fluid)
    sums = [[0.0, 0.0], [0.0, 0.0]]
    counts = [0.0, 0.0]
    count_lanes = 0.0
    for i in range(2):
        ids = fluid[:, i * 64 + 32 : i * 64 + 33].astype(jnp.int32) - 1
        count_lanes = count_lanes + jnp.sum(jnp.where(ids == lane, 1.0, 0.0), axis=0, keepdims=True)
        for f in range(2):
            pick = hot_of(iota(square, 0) == i * 64 + f * 16 + lane % 16)
            values = dot(fluid_pair[0], pick) + dot(fluid_pair[1], pick)
            for xl in range(2):
                mask = ids == xl * 8 + lane // 16
                sums[f][xl] = sums[f][xl] + jnp.sum(
                    jnp.where(mask, values, 0.0), axis=0, keepdims=True
                )
                if f == 0:
                    counts[xl] = counts[xl] + jnp.sum(
                        jnp.where(mask, 1.0, 0.0), axis=0, keepdims=True
                    )
    heat = [sums[0][xl] - counts[xl] * surface_ref[xl : xl + 1, :] for xl in range(2)]
    tail = jnp.where(lane < 16, count_lanes, 0.0)
    edge_rows = []
    for t, (part, ref, element) in enumerate(((2, before_ref, 0), (1, after_ref, count - 1))):
        met = elem_ref[...] == element
        owner, patch = [
            jnp.sum(jnp.where(met, value, 0).astype(F32), axis=1, keepdims=True).astype(jnp.int32)
            for value in (owner_ref[...] + 1, patch_ref[...])
        ]
        x_of_slot = patch // 8 * HALF + (owner - 1) % 2 * 64 + (owner - 1) // 2
        tail = jnp.where(lane == 40 + t, jnp.where(owner > 0, x_of_slot + 1, 0).astype(F32), tail)
        tables = matrix_ref[16 * part : 16 * part + 16]
        column = jnp.sum(tables * ref[0:1, 0:320], axis=1, keepdims=True)
        node, lane16 = iota((16, HALF), 0), iota((16, HALF), 1)
        used = (lane16 % 16 == node) & (lane16 // 16 == patch % 8)
        edge_rows.append(jnp.sum(jnp.where(used, column, 0.0), axis=0, keepdims=True))
    for k in range(2):
        by_modes = []
        for part in range(2):
            table = by_modes_ref[part, k * HALF : (k + 1) * HALF, :].astype(F32)
            own = jnp.where(group == 0, table[:, :HALF], table[:, HALF:])
            by_modes.append(own.astype(BF16))
        by_modes = tuple(by_modes)
        for xl in range(2):
            column = dot3(by_modes, jnp.broadcast_to(sums[1][xl], (8, HALF)), NT)[:, 0:1]
            tail = jnp.where(lane == 16 + 2 * k + xl, column, tail)
        for t in range(2):
            column = dot3(by_modes, jnp.broadcast_to(edge_rows[t], (8, HALF)), NT)[:, 0:1]
            tail = jnp.where(lane == 32 + 2 * t + k, column, tail)
    shared = [surface_row[:, :HALF], surface_row[:, HALF:], heat[0], heat[1]]
    for r in range(4):
        out_ref[pl.ds(r, HALF, 5), :] = jnp.broadcast_to(shared[r], square)
    out_ref[pl.ds(4, HALF, 5), :] = tail


def solve_kernel(
    where_ref, got_ref, other_ref, modes_ref, response_ref, sine_ref, pair_ref, x_ref, by_modes_ref,
    from_modes_ref, split_ref, decay_ref, row_ref,
    surface_hbm, out_hbm, heat_ref, surface_ref, out_ref, sem, sems
):
    core, me = where_ref[1], where_ref[2]
    first = jnp.full((HALF, HALF), core, jnp.int32) == 0
    ordered = []
    for r in range(5):
        mine, theirs = rows(got_ref, r, HALF, 5), rows(other_ref, r, HALF, 5)
        ordered.append((jnp.where(first, mine, theirs), jnp.where(first, theirs, mine)))

    def block(g, r):
        return jnp.concatenate([ordered[r][k][g * 64 : (g + 1) * 64] for k in range(2)], axis=0)

    halves = [
        tuple(by_modes_ref[part, :, g * HALF : (g + 1) * HALF] for part in range(2))
        for g in range(2)
    ]
    by_x = x_ref[0], x_ref[1]
    heat_modes = 0.0
    for xl in range(2):
        by_y = 0.0
        for g in range(2):
            by_y = by_y + dot3(halves[g], block(g, 2 + xl), NT)
        at = slice(xl * HALF, (xl + 1) * HALF)
        heat_modes = heat_modes + dot3(by_y, (by_x[0][at], by_x[1][at]))
    heat_ref[...] = heat_modes
    given = jnp.concatenate(
        [jnp.concatenate([ordered[h][k] for h in range(2)], axis=1) for k in range(2)], axis=0
    )
    surface = dot3((from_modes_ref[0], from_modes_ref[1]), given + response_ref[...] * heat_modes)
    surface = dot3(surface, by_x, NT)
    surface_ref[...] = surface
    copy = pltpu.make_async_copy(surface_ref, surface_hbm, sem)
    copy.start()
    square = (HALF, HALF)
    tails = [block(g, 4) for g in range(2)]
    tail_pairs = [tail.astype(BF16) for tail in tails]
    expand = [hot_of(iota(square, 1) == xl * 8 + iota(square, 0) // 16) for xl in range(2)]
    count = jnp.concatenate(
        [
            jnp.concatenate([dot(expand[xl], tail_pairs[g], NT) for xl in range(2)], axis=1)
            for g in range(2)
        ],
        axis=0,
    )
    own_sine = jnp.broadcast_to(sine_rows(sine_ref, me, 1, 1), (8, N))
    reduced = dot3(own_sine, count * surface)
    tail_sum = tails[0] + tails[1]
    lane8 = iota((8, HALF), 1)
    later = jnp.concatenate(
        [hot_dot(hot_of(lane8 == 16 + 2 * core + xl), tail_sum, NT) for xl in range(2)], axis=1
    )
    wide = iota((HALF, N), 1)
    for k in range(2):
        tail = ordered[4][k]
        for t in range(2):
            value = jnp.where(first[:, 0:1], tail[:, 32 + 2 * t : 33 + 2 * t], tail[:, 33 + 2 * t : 34 + 2 * t])
            met = tail[:, 40 + t : 41 + t].astype(jnp.int32) - 1 == wide
            later = later + jnp.sum(jnp.where(met, value, 0.0), axis=0, keepdims=True)
    heat1 = dot3(later - 0.7 * reduced, by_x)[0:1]
    heat0 = heat_ref[pl.ds(core * HALF + me // 2, 1), :]
    decay = decay_ref[...]
    column = sine_ref[pl.ds(0, N), 0:1]
    final = decay * (decay * (modes_ref[...] + column * heat0) + column * heat1)
    final_row = dot3(row_ref[...], final)[0:1]
    final = split(final)
    sine = pair_ref[0], pair_ref[1]
    for xl in range(2):
        part = dot3(dot3((split_ref[2 * xl], split_ref[2 * xl + 1]), final, NT), sine)
        for h in range(2):
            out_ref[pl.ds(2 * xl + h, HALF, 5), :] = part[:, h * HALF : (h + 1) * HALF]
    for k in range(2):
        out_ref[pl.ds(4 + 5 * k, 64, 10), :] = jnp.broadcast_to(
            final_row[:, k * HALF : (k + 1) * HALF], (64, HALF)
        )
    pieces = [(160 * i, 640 * g + 160 * i) for i in range(4) for g in range(2)]
    for sending in send_out(
        [(out_ref.at[pl.ds(a, 160), :], out_hbm.at[pl.ds(b, 160), :]) for a, b in pieces], sems
    ):
        sending.wait()
    copy.wait()


def met_values(surface, owner, patch):
    x_of_slot = patch // 8 * HALF + owner % 2 * 64 + owner // 2
    x_hot = hot_of(iota((N, HALF), 0) == x_of_slot)
    met = dot_hot(surface, x_hot)
    return jnp.where(iota((HALF, HALF), 0) // 16 == patch % 8, met, 0.0)


def folded(met):
    fold = hot_of(iota((16, HALF), 0) == iota((16, HALF), 1) % 16)
    return hot_dot(fold, met)


def stepped(extended, matrix_ref):
    fluid = split(extended)
    width = extended.shape[1]
    own, following, preceding = [
        dot3(matrix_ref[pl.ds(320 * i, 320), :], fluid) for i in range(3)
    ]
    return own + pltpu.roll(following, width - 1, 1) + pltpu.roll(preceding, 1, 1)


def step_kernel(where_ref, fluid_ref, matrix_ref, before_ref, after_ref, out_ref):
    count = fluid_ref.shape[1]
    me = where_ref[2]
    lane = iota((320, HALF), 1)
    following, preceding = after_ref[...].T[0:320], before_ref[...].T[0:320]
    halo = jnp.zeros((320, HALF), F32)
    for at, column in (
        (0, following[:, 0:1]),
        (1, following[:, 1:2]),
        (HALF - 1, preceding[:, 0:1]),
        (HALF - 2, preceding[:, 1:2]),
    ):
        halo = jnp.where(lane == at, column, halo)
    result = stepped(jnp.concatenate([fluid_ref[...], halo], axis=1), matrix_ref)
    edge = result[:, count:]
    beyond = ((lane == 0) & (me == 255)) | ((lane == HALF - 1) & (me == 0))
    out_ref[:, :count] = result[:, :count]
    out_ref[:, count:] = jnp.where(beyond, 0.0, edge)


def second_kernel(
    where_ref, fluid_ref, surface_ref, trace_ref, matrix_ref, before_ref, after_ref, elem_ref,
    owner_ref, patch_ref, sine_ref, out_ref, later_ref, slots_ref, walls_ref
):
    group, me = where_ref[0], where_ref[2]
    width = fluid_ref.shape[1]
    count = width - HALF
    own_surface = surface_ref[pl.ds(pl.multiple_of(group * HALF, HALF), HALF), :]
    elem_hot = hot_of(column_of(elem_ref[...]) == iota((HALF, count), 1))
    met = folded(met_values(own_surface, owner_ref[...], patch_ref[...]))
    source = GAIN * dot_hot(met - trace_ref[...], elem_hot)
    square = (16, HALF)
    edge = jnp.zeros(square, F32)
    for ref, at, device in ((after_ref, 0, me + 1), (before_ref, HALF - 1, me - 1)):
        owner = ref[2:3, 0:1].astype(jnp.int32) - 1
        patch = ref[2:3, 1:2].astype(jnp.int32)
        side = jnp.clip(device, 0, 255) // HALF
        near = surface_ref[pl.ds(pl.multiple_of(side * HALF, HALF), HALF), :]
        lanes = jnp.zeros((1, HALF), jnp.int32)
        value = folded(met_values(near, owner + lanes, patch + lanes))
        column = ref[...].T
        value = GAIN * (value - (column[256:272, 0:1] - column[0:16, 0:1]))
        used = (iota(square, 1) == at) & (owner >= 0)
        edge = jnp.where(used, value, edge)
    slot_hot = hot_of(iota((N, HALF), 0) == 2 * owner_ref[...] + patch_ref[...] // 8)
    slots_ref[...] = dot_hot(sine_rows(sine_ref, 0, N, 1), slot_hot)
    walls = fluid_ref[256:272] + jnp.concatenate([source, edge], axis=1)
    later_ref[...] = dot_hot(walls[:, :count] - fluid_ref[0:16, :count], elem_hot, NT)
    extended = jnp.concatenate([fluid_ref[0:256], walls, fluid_ref[272:320]], axis=0)
    result = stepped(extended, matrix_ref)[:, :count]
    out_ref[...] = result
    walls_ref[...] = result[256:272]


def solid_half(h, where_ref, got_ref, sine_ref, solid_hbm, solid_ref, sem):
    by_y = split(sine_ref[pl.ds(pl.multiple_of(where_ref[0] * N, N), N), :])
    for xl in range(2):
        part = rows(got_ref, 2 * xl + h, N, 5)
        solid_ref[pl.ds(xl, HALF, 2), :] = dot3(part, by_y, TN)
    copy = pltpu.make_async_copy(solid_ref, solid_hbm.at[pl.ds(h * N, N), :], sem)
    copy.start()
    return copy


def solid_kernel(where_ref, got_ref, sine_ref, solid_hbm, solid_ref, sem):
    solid_half(0, where_ref, got_ref, sine_ref, solid_hbm, solid_ref, sem).wait()


def last_kernel(
    where_ref, got_ref, mine_ref, other_ref, sine_ref, slots_ref, later_ref, elem_ref, patch_ref,
    walls_ref, fluid_hbm, half_hbm, out_hbm, solid_hbm, out_ref, solid_ref, sem, solid_sem
):
    group, core = where_ref[0], where_ref[1]
    solid = solid_half(1, where_ref, got_ref, sine_ref, solid_hbm, solid_ref, solid_sem)
    first = jnp.full((N, HALF), core, jnp.int32) == 0
    mine, other = mine_ref[...], other_ref[...]
    given = jnp.concatenate([jnp.where(first, mine, other), jnp.where(first, other, mine)], axis=1)
    own_rows = sine_rows(sine_ref, pl.multiple_of(group * HALF, HALF), HALF, 1)
    met = dot3(own_rows, dot3(given, slots_ref[...]))
    met = folded(jnp.where(iota((HALF, HALF), 0) // 16 == patch_ref[...] % 8, met, 0.0))
    elem_hot = hot_of(column_of(elem_ref[...]) == iota((HALF, walls_ref.shape[1]), 1))
    out_ref[...] = walls_ref[...] + GAIN * dot_hot(met - later_ref[...], elem_hot)
    copy = pltpu.make_async_copy(out_ref, out_hbm.at[pl.ds(256, 16), :], sem)
    copy.start()
    solid.wait()
    copy.wait()


def call(kernel, outs, args, scalars=0, scratch=(), aliases=None, specs=None, out_specs=None, cost=None, limit=40):
    whole = pl.BlockSpec(memory_space=pltpu.VMEM)
    given = [pl.BlockSpec(memory_space=pltpu.SMEM)] * scalars + [whole] * (len(args) - scalars)
    return pl.pallas_call(
        kernel,
        out_shape=[
            jax.ShapeDtypeStruct(*(out if isinstance(out[0], tuple) else (out, F32))) for out in outs
        ],
        in_specs=specs or given,
        out_specs=out_specs or [whole] * len(outs),
        scratch_shapes=list(scratch),
        input_output_aliases=aliases or {},
        cost_estimate=pl.CostEstimate(flops=int(cost or 1e8), bytes_accessed=1 << 20, transcendentals=0),
        compiler_params=pltpu.CompilerParams(vmem_limit_bytes=limit << 20),
    )(*args)


def exchange(payload, axes):
    chunks = payload.reshape(payload.shape[0], 1, HALF)
    return lax.all_to_all(chunks, axes, split_axis=0, concat_axis=0, tiled=True).reshape(payload.shape)


def on_device(fluid_state, flux_jacobian, solid_temp, iface_elem, iface_owner, iface_patch):
    me = lax.axis_index(ALL)
    where = jnp.stack([me // HALF, me % 2, me]).astype(jnp.int32)
    fluid0 = fluid_state.reshape(320, -1)
    count = fluid0.shape[1]
    solid = solid_temp.reshape(2 * N, HALF)
    elem, owner, patch = iface_elem[None, :], iface_owner.reshape(1, HALF), iface_patch[None, :]
    smem = pl.BlockSpec(memory_space=pltpu.SMEM)
    vmem = pl.BlockSpec(memory_space=pltpu.VMEM)
    hbm = pl.BlockSpec(memory_space=pltpu.HBM)

    far = lax.ppermute(solid, "g", [(0, 1), (1, 0)])
    near, trace0, surface0, first, last, wall_matrix, far_table = call(
        near_kernel,
        [(5 * HALF, HALF), (16, HALF), (2, HALF), (8, 384), (8, 384), (48, 320), (HALF, HALF)],
        [where, flux_jacobian, fluid0, solid, Q_HALVES, WALL_TABLES, elem, owner, patch],
        specs=[smem] + [hbm] * 8,
        limit=52,
        scratch=[
            pltpu.VMEM(flux_jacobian.shape, F32),
            pltpu.VMEM(fluid0.shape, F32),
            pltpu.VMEM(solid.shape, F32),
            pltpu.VMEM(Q_HALVES.shape, F32),
            pltpu.VMEM(WALL_TABLES.shape, F32),
            pltpu.VMEM((1, HALF), jnp.int32),
            pltpu.VMEM((1, HALF), jnp.int32),
            pltpu.VMEM((1, HALF), jnp.int32),
            pltpu.SemaphoreType.DMA((12,)),
        ],
    )
    before = lax.ppermute(last, ALL, [(i, i + 1) for i in range(255)])
    after = lax.ppermute(first, ALL, [(i + 1, i) for i in range(255)])
    (pay1,) = call(
        far_kernel,
        [(5 * HALF, HALF)],
        [far, far_table, near],
        out_specs=[hbm],
        scratch=[pltpu.VMEM((5 * HALF, HALF), F32), pltpu.SemaphoreType.DMA((4,))],
    )
    got1 = exchange(pay1, SUB)
    tables = call(
        tables_kernel,
        [((2, N, N), BF16)] * 4
        + [((4, HALF, N), BF16), (N, N)],
        [where, RATE_LIST, Q_HALVES, RATE_ROW, RATE_COLUMN, surface0],
        scalars=2,
    )
    sine_pair, x_pair, modes_pair, modes_t_pair, split_pair, decay = tables
    jacobian = jnp.pad(flux_jacobian, ((0, 0), (0, 3), (0, 3)))
    (matrix,) = call(
        matrices_kernel,
        [(960, 320)],
        [jacobian, FIELD_HOT, TILE_HOT, np.stack([FIXED, NEXT_FIXED, PREV_FIXED]), OPERATORS],
    )
    (fluid1,) = call(
        step_kernel,
        [(320, count + HALF)],
        [where, fluid0, matrix, before, after],
        scalars=1,
        cost=2e9,
    )
    modes, pay2 = call(
        functools.partial(modes_kernel, count=count),
        [(N, N), (5 * HALF, HALF)],
        [where, got1, surface0, sine_pair, split_pair, modes_pair, decay, SURFACE_ROW,
         wall_matrix, before, after, elem, owner, patch],
        scalars=1,
    )
    got2 = exchange(pay2, SAME_CORE)
    other = lax.ppermute(got2, "c", [(0, 1), (1, 0)])
    surface1, pay3 = call(
        solve_kernel,
        [(N, N), (5 * N, HALF)],
        [where, got2, other, modes, RESPONSE, Q_HALVES, sine_pair, x_pair, modes_pair, modes_t_pair,
         split_pair, decay, SURFACE_ROW],
        scalars=1,
        out_specs=[hbm, hbm],
        scratch=[
            pltpu.VMEM((N, N), F32),
            pltpu.VMEM((N, N), F32),
            pltpu.VMEM((5 * HALF, HALF), F32),
            pltpu.SemaphoreType.DMA,
            pltpu.SemaphoreType.DMA((8,)),
        ],
    )
    got3 = exchange(pay3, ALL)
    fluid2, trace1, slots, walls2 = call(
        second_kernel,
        [(320, count), (16, HALF), (N, HALF), (16, count)],
        [where, fluid1, surface1, trace0, matrix, before, after, elem, owner, patch, Q_HALVES],
        scalars=1,
        cost=2e9,
    )
    got3, fluid2, trace1, slots, walls2 = lax.optimization_barrier(
        (got3, fluid2, trace1, slots, walls2)
    )
    mine = got3.reshape(N, 5, 1, HALF)[:, 4].reshape(N, HALF)
    far_row = lax.ppermute(mine, "c", [(0, 1), (1, 0)])
    (solid_out,) = call(
        solid_kernel,
        [(2 * N, HALF)],
        [where, got3, Q_HALVES],
        scalars=1,
        out_specs=[hbm],
        scratch=[pltpu.VMEM((N, HALF), F32), pltpu.SemaphoreType.DMA],
    )
    fluid2, solid_out = call(
        last_kernel,
        [(320, count), (2 * N, HALF)],
        [where, got3, mine, far_row, Q_HALVES, slots, trace1, elem, patch, walls2, fluid2, solid_out],
        specs=[smem] + [vmem] * 9 + [hbm] * 2,
        out_specs=[hbm] * 2,
        aliases={10: 0, 11: 1},
        scratch=[
            pltpu.VMEM((16, count), F32),
            pltpu.VMEM((N, HALF), F32),
            pltpu.SemaphoreType.DMA,
            pltpu.SemaphoreType.DMA,
        ],
    )
    return fluid2.reshape(fluid_state.shape), solid_out.reshape(solid_temp.shape)


def solution(mesh):
    fine = Mesh(mesh.devices.reshape(2, 2, 4, 8, 2), ALL)
    placed = (
        P(None, None, ALL),
        P(),
        P(None, SUB, "g"),
        P(ALL),
        P(ALL, None),
        P(ALL),
    )
    return jax.shard_map(
        on_device,
        mesh=fine,
        in_specs=placed,
        out_specs=(P(None, None, ALL), P(None, SUB, "g")),
        check_vma=False,
    )
```

```python
import functools

import jax
import jax.numpy as jnp
import ml_dtypes
import numpy as np
from jax import lax
from jax.experimental import pallas as pl
from jax.experimental.pallas import tpu as pltpu
from jax.sharding import Mesh, PartitionSpec as P

ALL = ("g", "yl", "x", "z", "c")
SUB = ("yl", "x", "z", "c")
SAME_CORE = ("g", "yl", "x", "z")
N = 256
HALF = 128
DT = 0.05
VISC = 0.05
GAIN = 0.3
SURFACE_ROWS = 20480
F32 = jnp.float32
BF16 = jnp.bfloat16
NN = ((1,), (0,))
NT = ((1,), (1,))
TN = ((0,), (0,))


def sine_table(length):
    numbers = np.arange(length) + 1
    phases = numbers[:, None] * numbers[None, :] % (2 * (length + 1))
    return np.sqrt(2.0 / (length + 1)) * np.sin(np.pi * phases / (length + 1))


def rates(length):
    return 2.0 - 2.0 * np.cos(np.pi * (np.arange(length) + 1) / (length + 1))


SINE = sine_table(N)
RATES = rates(N)
MODE_ORDER = np.array([2 * q + k for k in range(2) for q in range(HALF)])


def surface_response():
    total = np.zeros((N, N))
    for c in range(N):
        total += SINE[0, c] ** 2 / (1.0 + 64.0 * (RATES[c] + RATES[:, None] + RATES[None, :]))
    return total


Q = SINE.astype(np.float32)
Q_HALVES = np.concatenate([Q[:, :HALF], Q[:, HALF:]], axis=0)
RESPONSE = surface_response()[MODE_ORDER].astype(np.float32)


def lobatto_derivative():
    points = np.array([-1.0, -1.0 / np.sqrt(5.0), 1.0 / np.sqrt(5.0), 1.0])
    weights = np.array(
        [1.0 / np.prod([points[j] - points[k] for k in range(4) if k != j]) for j in range(4)]
    )
    deriv = np.zeros((4, 4))
    for i in range(4):
        for j in range(4):
            if i != j:
                deriv[i, j] = weights[j] / weights[i] / (points[i] - points[j])
        deriv[i, i] = -np.sum(deriv[i])
    return deriv


def operator_parts():
    deriv, eye = lobatto_derivative(), np.eye(4)
    along = [
        np.kron(eye, np.kron(eye, deriv)),
        np.kron(eye, np.kron(deriv, eye)),
        np.kron(deriv, np.kron(eye, eye)),
    ]
    second = sum(d @ d for d in along)
    pick = np.zeros((4, 4, 4, 4))
    for i in range(4):
        for j in range(4):
            pick[i, j, i, j] = 1.0
    eye16 = np.eye(16)
    right, left = np.kron(eye16, pick[3, 3]), np.kron(eye16, pick[0, 0])
    right_from, left_from = np.kron(eye16, pick[3, 0]), np.kron(eye16, pick[0, 3])
    fixed = np.kron(np.eye(5), np.eye(64) - 0.15 * right - 0.15 * left)
    fixed = fixed + DT * VISC * np.kron(np.diag([0.0, 1.0, 1.0, 1.0, 1.0]), second)
    by_x = -DT * along[0] + 0.15 * right - 0.15 * left
    return [
        np.asarray(a, np.float32)
        for a in (
            fixed,
            by_x,
            -DT * along[1],
            -DT * along[2],
            np.kron(np.eye(5), 0.15 * right_from),
            -0.15 * right_from,
            np.kron(np.eye(5), 0.15 * left_from),
            0.15 * left_from,
        )
    ]


FIXED, BY_X, BY_Y, BY_Z, NEXT_FIXED, NEXT_X, PREV_FIXED, PREV_X = operator_parts()


def wall_tables():
    groups = []
    for fixed, tables in ((FIXED, (BY_X, BY_Y, BY_Z)), (NEXT_FIXED, (NEXT_X,)), (PREV_FIXED, (PREV_X,))):
        groups.append(fixed[256:272] - fixed[0:16])
        groups += [np.tile(t[:16], (1, 5)) for t in tables]
    return np.stack(groups).astype(np.float32)


WALL_TABLES = wall_tables()
RATE_LIST = RATES.astype(np.float32)
RATE_ROW = (1.0 + 64.0 * RATES)[None, :].astype(np.float32)
RATE_COLUMN = (64.0 * RATES)[:, None].astype(np.float32)
SURFACE_ROW = np.broadcast_to(Q[:1], (8, N)).copy()
FIELD_HOT = np.pad(np.kron(np.eye(5), np.ones((64, 1))), ((0, 0), (0, 3))).astype(ml_dtypes.bfloat16)
TILE_HOT = np.kron(np.ones((5, 1)), np.eye(64)).astype(ml_dtypes.bfloat16)
OPERATORS = np.stack([BY_X, BY_Y, BY_Z, NEXT_X, PREV_X])


def split(value):
    high = value.astype(BF16)
    return high, (value - high.astype(F32)).astype(BF16)


def dot(a, b, dims=NN):
    return lax.dot_general(a, b, (dims, ((), ())), preferred_element_type=F32)


def dot3(a, b, dims=NN):
    a = split(a) if not isinstance(a, tuple) else a
    b = split(b) if not isinstance(b, tuple) else b
    a = jnp.concatenate([a[0], a[1], a[0]], axis=dims[0][0])
    b = jnp.concatenate([b[0], b[0], b[1]], axis=dims[1][0])
    return dot(a, b, dims)


def hot_dot(hot, b, dims=NN):
    high, low = split(b)
    return dot(hot, high, dims) + dot(hot, low, dims)


def dot_hot(a, hot, dims=NN):
    high, low = split(a)
    return dot(high, hot, dims) + dot(low, hot, dims)


def hot_of(condition):
    return jnp.where(condition, 1.0, 0.0).astype(BF16)


def iota(shape, dim):
    return lax.broadcasted_iota(jnp.int32, shape, dim)


def rows(ref, first, count, stride):
    return ref[pl.ds(first, count, stride) if stride > 1 else pl.ds(first, count), :]


def sine_rows(ref, first, count, stride):
    return jnp.concatenate([rows(ref, h * N + first, count, stride) for h in range(2)], axis=1)


def x_ordered(sine_ref):
    blocks = [sine_rows(sine_ref, 2 * k + i, 64, 4) for i in range(2) for k in range(2)]
    return split(jnp.concatenate(blocks, axis=0))


def mode_ordered(sine_ref):
    return jnp.concatenate([sine_rows(sine_ref, k, HALF, 2) for k in range(2)], axis=0)


def column_of(row):
    return jnp.broadcast_to(row.astype(F32), (8, row.shape[1])).T[:, 0:1].astype(jnp.int32)


def near_kernel(
    where_ref, jac_hbm, fluid_hbm, solid_hbm, sine_hbm, table_hbm, elem_hbm, owner_hbm, patch_hbm,
    out_ref, trace_ref, surface_ref, first_ref, last_ref, matrix_ref, far_table_ref,
    jac_ref, fluid_ref, solid_ref, sine_ref, table_ref, elem_ref, owner_ref, patch_ref, sems
):
    group = where_ref[0]
    count = fluid_ref.shape[1]
    copies = [
        pltpu.make_async_copy(jac_hbm, jac_ref, sems.at[0]),
        pltpu.make_async_copy(solid_hbm, solid_ref, sems.at[1]),
        pltpu.make_async_copy(sine_hbm, sine_ref, sems.at[2]),
        pltpu.make_async_copy(table_hbm, table_ref, sems.at[3]),
        pltpu.make_async_copy(elem_hbm, elem_ref, sems.at[4]),
        pltpu.make_async_copy(owner_hbm, owner_ref, sems.at[5]),
        pltpu.make_async_copy(patch_hbm, patch_ref, sems.at[6]),
    ]
    for i in range(5):
        at = pl.ds(64 * i, 64)
        copies.append(pltpu.make_async_copy(fluid_hbm.at[at, :], fluid_ref.at[at, :], sems.at[7 + i]))
    for copy in copies:
        copy.start()
    for copy in copies[:7]:
        copy.wait()

    near, far = [
        sine_ref[pl.ds(pl.multiple_of(half * N + group * HALF, HALF), HALF), :]
        for half in (group, 1 - group)
    ]
    far_table_ref[...] = far
    near = split(near)
    for i in range(2):
        modes = dot3(near, rows(solid_ref, i, N, 2), NT)
        for h in range(2):
            out_ref[pl.ds(2 * i + h, HALF, 5), :] = modes[:, h * HALF : (h + 1) * HALF]
    surface_ref[...] = solid_ref[0:2]

    field = iota((1, 320), 1) // 64
    coefficients = []
    for d in range(3):
        change = jac_ref[d, 4:5, :] - jac_ref[d, 0:1, :]
        row = jnp.zeros((1, 320), F32)
        for f in range(5):
            row = jnp.where(field == f, change[:, f : f + 1], row)
        coefficients.append(row)
    own = table_ref[0]
    for d in range(3):
        own = own + coefficients[d] * table_ref[1 + d]
    matrix_ref[0:16] = own
    matrix_ref[16:32] = table_ref[4] + coefficients[0] * table_ref[5]
    matrix_ref[32:48] = table_ref[6] + coefficients[0] * table_ref[7]

    owner, patch, elem = owner_ref[...], patch_ref[...], elem_ref[...]
    square = (HALF, HALF)
    same = (column_of(owner) == owner) & (iota(square, 0) < iota(square, 1))
    place = jnp.sum(jnp.where(same, 1.0, 0.0), axis=0, keepdims=True)
    elem_hot = hot_of(column_of(elem) == iota((HALF, count), 1))

    for copy in copies[7:]:
        copy.wait()
    lane = iota((1, 384), 1)
    gap = jnp.zeros((1, 64), F32)
    for block, at, out, element in (
        (fluid_ref[:, 0:HALF], (0, 1), first_ref, 0),
        (fluid_ref[:, count - HALF : count], (HALF - 1, HALF - 2), last_ref, count - 1),
    ):
        turned = block.T
        met = elem == element
        edge_owner = jnp.sum(jnp.where(met, owner + 1, 0).astype(F32), axis=1, keepdims=True)
        edge_patch = jnp.sum(jnp.where(met, patch, 0).astype(F32), axis=1, keepdims=True)
        out[0:1] = jnp.concatenate([turned[at[0] : at[0] + 1], gap], axis=1)
        out[1:2] = jnp.concatenate([turned[at[1] : at[1] + 1], gap], axis=1)
        out[2:3] = jnp.where(lane == 0, edge_owner, jnp.where(lane == 1, edge_patch, 0.0))
        out[3:8] = jnp.zeros((5, 384), F32)

    walls = dot3(matrix_ref[...], fluid_ref[...])
    wall0 = fluid_ref[256:272] - fluid_ref[0:16]
    lane = iota(wall0.shape, 1)
    following = pltpu.roll(walls[16:32], count - 1, 1)
    preceding = pltpu.roll(walls[32:48], 1, 1)
    later = walls[0:16] + jnp.where(lane == count - 1, 0.0, following)
    later = later + jnp.where(lane == 0, 0.0, preceding)
    values = dot_hot(jnp.concatenate([wall0, later - GAIN * wall0], axis=0), elem_hot, NT)
    trace_ref[...] = values[:16]
    ids = jnp.broadcast_to((patch + 1).astype(F32), (8, HALF))
    filler = jnp.zeros((24, HALF), F32)
    sent = jnp.concatenate([values, ids, filler], axis=0)
    none = jnp.zeros((64, HALF), F32)
    arranged = 0.0
    for i in range(2):
        hot = hot_of((iota(square, 0) == owner) & (place == float(i)))
        padded = jnp.concatenate([sent, none] if i == 0 else [none, sent], axis=0)
        arranged = arranged + hot_dot(hot, padded, NT)
    out_ref[pl.ds(4, HALF, 5), :] = arranged


def send_out(pairs, sems):
    copies = [pltpu.make_async_copy(a, b, sems.at[i]) for i, (a, b) in enumerate(pairs)]
    for copy in copies:
        copy.start()
    return copies


def far_kernel(far_ref, table_ref, near_ref, out_hbm, out_ref, sems):
    table = split(table_ref[...])
    out_ref[pl.ds(4, HALF, 5), :] = rows(near_ref, 4, HALF, 5)
    for i in range(2):
        modes = dot3(table, rows(far_ref, i, N, 2), NT)
        for h in range(2):
            part = modes[:, h * HALF : (h + 1) * HALF]
            out_ref[pl.ds(2 * i + h, HALF, 5), :] = rows(near_ref, 2 * i + h, HALF, 5) + part
    pieces = [pl.ds(160 * i, 160) for i in range(4)]
    for copy in send_out([(out_ref.at[at, :], out_hbm.at[at, :]) for at in pieces], sems):
        copy.wait()


def tables_kernel(
    where_ref, rate_ref, sine_ref, rate_row_ref, rate_col_ref, order_ref,
    sine_out, x_out, modes_out, modes_t_out, split_out, decay_out
):
    del order_ref
    by_modes = mode_ordered(sine_ref)
    for out, table in (
        (sine_out, split(sine_rows(sine_ref, 0, N, 1))),
        (x_out, x_ordered(sine_ref)),
        (modes_out, split(by_modes)),
        (modes_t_out, split(by_modes.T)),
    ):
        out[0], out[1] = table
    for i in range(2):
        split_out[2 * i], split_out[2 * i + 1] = split(sine_rows(sine_ref, i, HALF, 2))
    decay_out[...] = 1.0 / (rate_col_ref[...] + (rate_row_ref[...] + 64.0 * rate_ref[where_ref[2]]))


def matrices_kernel(jac_ref, field_ref, tile_ref, fixed_ref, operators_ref, out_ref):
    field, tile = field_ref[...], tile_ref[...]

    def spread(d):
        return dot_hot(hot_dot(field, jac_ref[d]), field, NT)

    def tiled(d):
        return dot_hot(hot_dot(tile, operators_ref[d]), tile, NT)

    by_x = spread(0)
    own = by_x * tiled(0) + spread(1) * tiled(1) + spread(2) * tiled(2)
    out_ref[0:320] = fixed_ref[0] + own
    out_ref[320:640] = fixed_ref[1] + by_x * tiled(3)
    out_ref[640:960] = fixed_ref[2] + by_x * tiled(4)


def modes_kernel(
    where_ref, got_ref, surface_ref, sine_ref, split_ref, by_modes_ref, decay_ref, row_ref,
    matrix_ref, before_ref, after_ref, elem_ref, owner_ref, patch_ref, modes_ref, out_ref, *, count
):
    group = where_ref[0]
    sine = sine_ref[0], sine_ref[1]
    modes = 0.0
    for i in range(2):
        part = jnp.concatenate([rows(got_ref, 2 * i + h, HALF, 5) for h in range(2)], axis=1)
        by_z = dot3(sine, part, NT)
        modes = modes + dot3(by_z, (split_ref[2 * i], split_ref[2 * i + 1]))
    modes_ref[...] = modes
    surface_row = dot3(row_ref[...], decay_ref[...] * modes)[0:1]

    fluid = rows(got_ref, 4, HALF, 5)
    square = (HALF, HALF)
    lane = iota(square, 1)
    fluid_pair = split(fluid)
    sums = [[0.0, 0.0], [0.0, 0.0]]
    counts = [0.0, 0.0]
    count_lanes = 0.0
    for i in range(2):
        ids = fluid[:, i * 64 + 32 : i * 64 + 33].astype(jnp.int32) - 1
        count_lanes = count_lanes + jnp.sum(jnp.where(ids == lane, 1.0, 0.0), axis=0, keepdims=True)
        for f in range(2):
            pick = hot_of(iota(square, 0) == i * 64 + f * 16 + lane % 16)
            values = dot(fluid_pair[0], pick) + dot(fluid_pair[1], pick)
            for xl in range(2):
                mask = ids == xl * 8 + lane // 16
                sums[f][xl] = sums[f][xl] + jnp.sum(
                    jnp.where(mask, values, 0.0), axis=0, keepdims=True
                )
                if f == 0:
                    counts[xl] = counts[xl] + jnp.sum(
                        jnp.where(mask, 1.0, 0.0), axis=0, keepdims=True
                    )
    heat = [sums[0][xl] - counts[xl] * surface_ref[xl : xl + 1, :] for xl in range(2)]
    tail = jnp.where(lane < 16, count_lanes, 0.0)
    edge_rows = []
    for t, (part, ref, element) in enumerate(((2, before_ref, 0), (1, after_ref, count - 1))):
        met = elem_ref[...] == element
        owner, patch = [
            jnp.sum(jnp.where(met, value, 0).astype(F32), axis=1, keepdims=True).astype(jnp.int32)
            for value in (owner_ref[...] + 1, patch_ref[...])
        ]
        x_of_slot = patch // 8 * HALF + (owner - 1) % 2 * 64 + (owner - 1) // 2
        tail = jnp.where(lane == 40 + t, jnp.where(owner > 0, x_of_slot + 1, 0).astype(F32), tail)
        tables = matrix_ref[16 * part : 16 * part + 16]
        column = jnp.sum(tables * ref[0:1, 0:320], axis=1, keepdims=True)
        node, lane16 = iota((16, HALF), 0), iota((16, HALF), 1)
        used = (lane16 % 16 == node) & (lane16 // 16 == patch % 8)
        edge_rows.append(jnp.sum(jnp.where(used, column, 0.0), axis=0, keepdims=True))
    for k in range(2):
        by_modes = []
        for part in range(2):
            table = by_modes_ref[part, k * HALF : (k + 1) * HALF, :].astype(F32)
            own = jnp.where(group == 0, table[:, :HALF], table[:, HALF:])
            by_modes.append(own.astype(BF16))
        by_modes = tuple(by_modes)
        for xl in range(2):
            column = dot3(by_modes, jnp.broadcast_to(sums[1][xl], (8, HALF)), NT)[:, 0:1]
            tail = jnp.where(lane == 16 + 2 * k + xl, column, tail)
        for t in range(2):
            column = dot3(by_modes, jnp.broadcast_to(edge_rows[t], (8, HALF)), NT)[:, 0:1]
            tail = jnp.where(lane == 32 + 2 * t + k, column, tail)
    shared = [surface_row[:, :HALF], surface_row[:, HALF:], heat[0], heat[1]]
    for r in range(4):
        out_ref[pl.ds(r, HALF, 5), :] = jnp.broadcast_to(shared[r], square)
    out_ref[pl.ds(4, HALF, 5), :] = tail


def solve_kernel(
    where_ref, got_ref, other_ref, modes_ref, response_ref, sine_ref, pair_ref, x_ref, by_modes_ref,
    from_modes_ref, split_ref, decay_ref, row_ref,
    surface_hbm, out_hbm, heat_ref, surface_ref, out_ref, sem, sems
):
    core, me = where_ref[1], where_ref[2]
    first = jnp.full((HALF, HALF), core, jnp.int32) == 0
    ordered = []
    for r in range(5):
        mine, theirs = rows(got_ref, r, HALF, 5), rows(other_ref, r, HALF, 5)
        ordered.append((jnp.where(first, mine, theirs), jnp.where(first, theirs, mine)))

    def block(g, r):
        return jnp.concatenate([ordered[r][k][g * 64 : (g + 1) * 64] for k in range(2)], axis=0)

    halves = [
        tuple(by_modes_ref[part, :, g * HALF : (g + 1) * HALF] for part in range(2))
        for g in range(2)
    ]
    by_x = x_ref[0], x_ref[1]
    heat_modes = 0.0
    for xl in range(2):
        by_y = 0.0
        for g in range(2):
            by_y = by_y + dot3(halves[g], block(g, 2 + xl), NT)
        at = slice(xl * HALF, (xl + 1) * HALF)
        heat_modes = heat_modes + dot3(by_y, (by_x[0][at], by_x[1][at]))
    heat_ref[...] = heat_modes
    given = jnp.concatenate(
        [jnp.concatenate([ordered[h][k] for h in range(2)], axis=1) for k in range(2)], axis=0
    )
    surface = dot3((from_modes_ref[0], from_modes_ref[1]), given + response_ref[...] * heat_modes)
    surface = dot3(surface, by_x, NT)
    surface_ref[...] = surface
    copy = pltpu.make_async_copy(surface_ref, surface_hbm.at[pl.ds(0, N), :], sem)
    copy.start()
    square = (HALF, HALF)
    tails = [block(g, 4) for g in range(2)]
    tail_pairs = [tail.astype(BF16) for tail in tails]
    expand = [hot_of(iota(square, 1) == xl * 8 + iota(square, 0) // 16) for xl in range(2)]
    count = jnp.concatenate(
        [
            jnp.concatenate([dot(expand[xl], tail_pairs[g], NT) for xl in range(2)], axis=1)
            for g in range(2)
        ],
        axis=0,
    )
    own_sine = jnp.broadcast_to(sine_rows(sine_ref, me, 1, 1), (8, N))
    reduced = dot3(own_sine, count * surface)
    tail_sum = tails[0] + tails[1]
    lane8 = iota((8, HALF), 1)
    later = jnp.concatenate(
        [hot_dot(hot_of(lane8 == 16 + 2 * core + xl), tail_sum, NT) for xl in range(2)], axis=1
    )
    wide = iota((HALF, N), 1)
    for k in range(2):
        tail = ordered[4][k]
        for t in range(2):
            value = jnp.where(first[:, 0:1], tail[:, 32 + 2 * t : 33 + 2 * t], tail[:, 33 + 2 * t : 34 + 2 * t])
            met = tail[:, 40 + t : 41 + t].astype(jnp.int32) - 1 == wide
            later = later + jnp.sum(jnp.where(met, value, 0.0), axis=0, keepdims=True)
    heat1 = dot3(later - 0.7 * reduced, by_x)[0:1]
    heat0 = heat_ref[pl.ds(core * HALF + me // 2, 1), :]
    decay = decay_ref[...]
    column = sine_ref[pl.ds(0, N), 0:1]
    final = decay * (decay * (modes_ref[...] + column * heat0) + column * heat1)
    final_row = dot3(row_ref[...], final)[0:1]
    final = split(final)
    sine = pair_ref[0], pair_ref[1]
    for xl in range(2):
        part = dot3(dot3((split_ref[2 * xl], split_ref[2 * xl + 1]), final, NT), sine)
        for h in range(2):
            out_ref[pl.ds(2 * xl + h, HALF, 5), :] = part[:, h * HALF : (h + 1) * HALF]
    for k in range(2):
        out_ref[pl.ds(4 + 5 * k, 64, 10), :] = jnp.broadcast_to(
            final_row[:, k * HALF : (k + 1) * HALF], (64, HALF)
        )
    pieces = [(160 * i, 640 * g + 160 * i) for i in range(4) for g in range(2)]
    for sending in send_out(
        [(out_ref.at[pl.ds(a, 160), :], out_hbm.at[pl.ds(b, 160), :]) for a, b in pieces], sems
    ):
        sending.wait()
    copy.wait()


def met_values(surface, owner, patch):
    x_of_slot = patch // 8 * HALF + owner % 2 * 64 + owner // 2
    x_hot = hot_of(iota((N, HALF), 0) == x_of_slot)
    met = dot_hot(surface, x_hot)
    return jnp.where(iota((HALF, HALF), 0) // 16 == patch % 8, met, 0.0)


def folded(met):
    fold = hot_of(iota((16, HALF), 0) == iota((16, HALF), 1) % 16)
    return hot_dot(fold, met)


def stepped(extended, matrix_ref):
    fluid = split(extended)
    width = extended.shape[1]
    own, following, preceding = [
        dot3(matrix_ref[pl.ds(320 * i, 320), :], fluid) for i in range(3)
    ]
    return own + pltpu.roll(following, width - 1, 1) + pltpu.roll(preceding, 1, 1)


def step_kernel(where_ref, fluid_ref, matrix_ref, before_ref, after_ref, out_ref):
    count = fluid_ref.shape[1]
    me = where_ref[2]
    lane = iota((320, HALF), 1)
    following, preceding = after_ref[...].T[0:320], before_ref[...].T[0:320]
    halo = jnp.zeros((320, HALF), F32)
    for at, column in (
        (0, following[:, 0:1]),
        (1, following[:, 1:2]),
        (HALF - 1, preceding[:, 0:1]),
        (HALF - 2, preceding[:, 1:2]),
    ):
        halo = jnp.where(lane == at, column, halo)
    result = stepped(jnp.concatenate([fluid_ref[...], halo], axis=1), matrix_ref)
    edge = result[:, count:]
    beyond = ((lane == 0) & (me == 255)) | ((lane == HALF - 1) & (me == 0))
    out_ref[:, :count] = result[:, :count]
    out_ref[:, count:] = jnp.where(beyond, 0.0, edge)


def second_kernel(
    where_ref, surface_hbm, fluid_ref, trace_ref, matrix_ref, before_ref, after_ref, elem_ref,
    owner_ref, patch_ref, sine_ref, out_ref, later_ref, slots_ref, walls_ref, surface_ref, sem
):
    copy = pltpu.make_async_copy(surface_hbm.at[pl.ds(0, N), :], surface_ref, sem)
    copy.start()
    copy.wait()
    group, me = where_ref[0], where_ref[2]
    width = fluid_ref.shape[1]
    count = width - HALF
    own_surface = surface_ref[pl.ds(pl.multiple_of(group * HALF, HALF), HALF), :]
    elem_hot = hot_of(column_of(elem_ref[...]) == iota((HALF, count), 1))
    met = folded(met_values(own_surface, owner_ref[...], patch_ref[...]))
    source = GAIN * dot_hot(met - trace_ref[...], elem_hot)
    square = (16, HALF)
    edge = jnp.zeros(square, F32)
    for ref, at, device in ((after_ref, 0, me + 1), (before_ref, HALF - 1, me - 1)):
        owner = ref[2:3, 0:1].astype(jnp.int32) - 1
        patch = ref[2:3, 1:2].astype(jnp.int32)
        side = jnp.clip(device, 0, 255) // HALF
        near = surface_ref[pl.ds(pl.multiple_of(side * HALF, HALF), HALF), :]
        lanes = jnp.zeros((1, HALF), jnp.int32)
        value = folded(met_values(near, owner + lanes, patch + lanes))
        column = ref[...].T
        value = GAIN * (value - (column[256:272, 0:1] - column[0:16, 0:1]))
        used = (iota(square, 1) == at) & (owner >= 0)
        edge = jnp.where(used, value, edge)
    slot_hot = hot_of(iota((N, HALF), 0) == 2 * owner_ref[...] + patch_ref[...] // 8)
    slots_ref[...] = dot_hot(sine_rows(sine_ref, 0, N, 1), slot_hot)
    walls = fluid_ref[256:272] + jnp.concatenate([source, edge], axis=1)
    later_ref[...] = dot_hot(walls[:, :count] - fluid_ref[0:16, :count], elem_hot, NT)
    extended = jnp.concatenate([fluid_ref[0:256], walls, fluid_ref[272:320]], axis=0)
    result = stepped(extended, matrix_ref)[:, :count]
    out_ref[...] = result
    walls_ref[...] = result[256:272]


def solid_kernel(where_ref, got_ref, sine_ref, solid_ref):
    by_y = split(sine_ref[pl.ds(pl.multiple_of(where_ref[0] * N, N), N), :])
    for xl in range(2):
        for h in range(2):
            part = rows(got_ref, 2 * xl + h, N, 5)
            solid_ref[pl.ds(h * N + xl, HALF, 2), :] = dot3(part, by_y, TN)


def last_kernel(
    where_ref, solid_ref, mine_ref, other_ref, sine_ref, slots_ref, later_ref, elem_ref, patch_ref,
    walls_ref, fluid_hbm, out_hbm, solid_hbm, out_ref, sem, solid_sems
):
    group, core = where_ref[0], where_ref[1]
    pieces = [pl.ds(HALF * i, HALF) for i in range(4)]
    solid = send_out([(solid_ref.at[at, :], solid_hbm.at[at, :]) for at in pieces], solid_sems)
    first = jnp.full((N, HALF), core, jnp.int32) == 0
    mine, other = mine_ref[...], other_ref[...]
    given = jnp.concatenate([jnp.where(first, mine, other), jnp.where(first, other, mine)], axis=1)
    own_rows = sine_rows(sine_ref, pl.multiple_of(group * HALF, HALF), HALF, 1)
    met = dot3(own_rows, dot3(given, slots_ref[...]))
    met = folded(jnp.where(iota((HALF, HALF), 0) // 16 == patch_ref[...] % 8, met, 0.0))
    elem_hot = hot_of(column_of(elem_ref[...]) == iota((HALF, walls_ref.shape[1]), 1))
    out_ref[...] = walls_ref[...] + GAIN * dot_hot(met - later_ref[...], elem_hot)
    copy = pltpu.make_async_copy(out_ref, out_hbm.at[pl.ds(256, 16), :], sem)
    copy.start()
    for sending in solid:
        sending.wait()
    copy.wait()


def call(kernel, outs, args, scalars=0, scratch=(), aliases=None, specs=None, out_specs=None, cost=None, limit=40):
    whole = pl.BlockSpec(memory_space=pltpu.VMEM)
    given = [pl.BlockSpec(memory_space=pltpu.SMEM)] * scalars + [whole] * (len(args) - scalars)
    return pl.pallas_call(
        kernel,
        out_shape=[
            jax.ShapeDtypeStruct(*(out if isinstance(out[0], tuple) else (out, F32))) for out in outs
        ],
        in_specs=specs or given,
        out_specs=out_specs or [whole] * len(outs),
        scratch_shapes=list(scratch),
        input_output_aliases=aliases or {},
        cost_estimate=pl.CostEstimate(flops=int(cost or 1e8), bytes_accessed=1 << 20, transcendentals=0),
        compiler_params=pltpu.CompilerParams(vmem_limit_bytes=limit << 20),
    )(*args)


def exchange(payload, axes):
    chunks = payload.reshape(payload.shape[0], 1, HALF)
    return lax.all_to_all(chunks, axes, split_axis=0, concat_axis=0, tiled=True).reshape(payload.shape)


def on_device(fluid_state, flux_jacobian, solid_temp, iface_elem, iface_owner, iface_patch):
    me = lax.axis_index(ALL)
    where = jnp.stack([me // HALF, me % 2, me]).astype(jnp.int32)
    fluid0 = fluid_state.reshape(320, -1)
    count = fluid0.shape[1]
    solid = solid_temp.reshape(2 * N, HALF)
    elem, owner, patch = iface_elem[None, :], iface_owner.reshape(1, HALF), iface_patch[None, :]
    smem = pl.BlockSpec(memory_space=pltpu.SMEM)
    vmem = pl.BlockSpec(memory_space=pltpu.VMEM)
    hbm = pl.BlockSpec(memory_space=pltpu.HBM)

    far = lax.ppermute(solid, "g", [(0, 1), (1, 0)])
    near, trace0, surface0, first, last, wall_matrix, far_table = call(
        near_kernel,
        [(5 * HALF, HALF), (16, HALF), (2, HALF), (8, 384), (8, 384), (48, 320), (HALF, HALF)],
        [where, flux_jacobian, fluid0, solid, Q_HALVES, WALL_TABLES, elem, owner, patch],
        specs=[smem] + [hbm] * 8,
        limit=52,
        scratch=[
            pltpu.VMEM(flux_jacobian.shape, F32),
            pltpu.VMEM(fluid0.shape, F32),
            pltpu.VMEM(solid.shape, F32),
            pltpu.VMEM(Q_HALVES.shape, F32),
            pltpu.VMEM(WALL_TABLES.shape, F32),
            pltpu.VMEM((1, HALF), jnp.int32),
            pltpu.VMEM((1, HALF), jnp.int32),
            pltpu.VMEM((1, HALF), jnp.int32),
            pltpu.SemaphoreType.DMA((12,)),
        ],
    )
    before = lax.ppermute(last, ALL, [(i, i + 1) for i in range(255)])
    after = lax.ppermute(first, ALL, [(i + 1, i) for i in range(255)])
    (pay1,) = call(
        far_kernel,
        [(5 * HALF, HALF)],
        [far, far_table, near],
        out_specs=[hbm],
        scratch=[pltpu.VMEM((5 * HALF, HALF), F32), pltpu.SemaphoreType.DMA((4,))],
    )
    got1 = exchange(pay1, SUB)
    tables = call(
        tables_kernel,
        [((2, N, N), BF16)] * 4
        + [((4, HALF, N), BF16), (N, N)],
        [where, RATE_LIST, Q_HALVES, RATE_ROW, RATE_COLUMN, surface0],
        scalars=2,
    )
    sine_pair, x_pair, modes_pair, modes_t_pair, split_pair, decay = tables
    jacobian = jnp.pad(flux_jacobian, ((0, 0), (0, 3), (0, 3)))
    (matrix,) = call(
        matrices_kernel,
        [(960, 320)],
        [jacobian, FIELD_HOT, TILE_HOT, np.stack([FIXED, NEXT_FIXED, PREV_FIXED]), OPERATORS],
    )
    (fluid1,) = call(
        step_kernel,
        [(320, count + HALF)],
        [where, fluid0, matrix, before, after],
        scalars=1,
        cost=2e9,
    )
    modes, pay2 = call(
        functools.partial(modes_kernel, count=count),
        [(N, N), (5 * HALF, HALF)],
        [where, got1, surface0, sine_pair, split_pair, modes_pair, decay, SURFACE_ROW,
         wall_matrix, before, after, elem, owner, patch],
        scalars=1,
    )
    got2 = exchange(pay2, SAME_CORE)
    other = lax.ppermute(got2, "c", [(0, 1), (1, 0)])
    surface1, pay3 = call(
        solve_kernel,
        [(SURFACE_ROWS, N), (5 * N, HALF)],
        [where, got2, other, modes, RESPONSE, Q_HALVES, sine_pair, x_pair, modes_pair, modes_t_pair,
         split_pair, decay, SURFACE_ROW],
        scalars=1,
        out_specs=[hbm, hbm],
        scratch=[
            pltpu.VMEM((N, N), F32),
            pltpu.VMEM((N, N), F32),
            pltpu.VMEM((5 * HALF, HALF), F32),
            pltpu.SemaphoreType.DMA,
            pltpu.SemaphoreType.DMA((8,)),
        ],
    )
    got3 = exchange(pay3, ALL)
    fluid2, trace1, slots, walls2 = call(
        second_kernel,
        [(320, count), (16, HALF), (N, HALF), (16, count)],
        [where, surface1, fluid1, trace0, matrix, before, after, elem, owner, patch, Q_HALVES],
        specs=[smem, hbm] + [vmem] * 9,
        scratch=[pltpu.VMEM((N, N), F32), pltpu.SemaphoreType.DMA],
        cost=2e9,
    )
    got3, fluid2, trace1, slots, walls2 = lax.optimization_barrier(
        (got3, fluid2, trace1, slots, walls2)
    )
    mine = got3.reshape(N, 5, 1, HALF)[:, 4].reshape(N, HALF)
    far_row = lax.ppermute(mine, "c", [(0, 1), (1, 0)])
    (solid_new,) = call(solid_kernel, [(2 * N, HALF)], [where, got3, Q_HALVES], scalars=1)
    fluid2, solid_out = call(
        last_kernel,
        [(320, count), (2 * N, HALF)],
        [where, solid_new, mine, far_row, Q_HALVES, slots, trace1, elem, patch, walls2, fluid2],
        specs=[smem] + [vmem] * 9 + [hbm],
        out_specs=[hbm] * 2,
        aliases={10: 0},
        scratch=[
            pltpu.VMEM((16, count), F32),
            pltpu.SemaphoreType.DMA,
            pltpu.SemaphoreType.DMA((4,)),
        ],
    )
    return fluid2.reshape(fluid_state.shape), solid_out.reshape(solid_temp.shape)


def solution(mesh):
    fine = Mesh(mesh.devices.reshape(2, 2, 4, 8, 2), ALL)
    placed = (
        P(None, None, ALL),
        P(),
        P(None, SUB, "g"),
        P(ALL),
        P(ALL, None),
        P(ALL),
    )
    return jax.shard_map(
        on_device,
        mesh=fine,
        in_specs=placed,
        out_specs=(P(None, None, ALL), P(None, SUB, "g")),
        check_vma=False,
    )
```

```python
import functools

import jax
import jax.numpy as jnp
import ml_dtypes
import numpy as np
from jax import lax
from jax.experimental import pallas as pl
from jax.experimental.pallas import tpu as pltpu
from jax.sharding import Mesh, PartitionSpec as P

ALL = ("g", "yl", "x", "z", "c")
SUB = ("yl", "x", "z", "c")
SAME_CORE = ("g", "yl", "x", "z")
N = 256
HALF = 128
DT = 0.05
VISC = 0.05
GAIN = 0.3
SURFACE_ROWS = 20480
F32 = jnp.float32
BF16 = jnp.bfloat16
NN = ((1,), (0,))
NT = ((1,), (1,))
TN = ((0,), (0,))


def sine_table(length):
    numbers = np.arange(length) + 1
    phases = numbers[:, None] * numbers[None, :] % (2 * (length + 1))
    return np.sqrt(2.0 / (length + 1)) * np.sin(np.pi * phases / (length + 1))


def rates(length):
    return 2.0 - 2.0 * np.cos(np.pi * (np.arange(length) + 1) / (length + 1))


SINE = sine_table(N)
RATES = rates(N)
MODE_ORDER = np.array([2 * q + k for k in range(2) for q in range(HALF)])


def surface_response():
    total = np.zeros((N, N))
    for c in range(N):
        total += SINE[0, c] ** 2 / (1.0 + 64.0 * (RATES[c] + RATES[:, None] + RATES[None, :]))
    return total


Q = SINE.astype(np.float32)
Q_HALVES = np.concatenate([Q[:, :HALF], Q[:, HALF:]], axis=0)
RESPONSE = surface_response()[MODE_ORDER].astype(np.float32)


def lobatto_derivative():
    points = np.array([-1.0, -1.0 / np.sqrt(5.0), 1.0 / np.sqrt(5.0), 1.0])
    weights = np.array(
        [1.0 / np.prod([points[j] - points[k] for k in range(4) if k != j]) for j in range(4)]
    )
    deriv = np.zeros((4, 4))
    for i in range(4):
        for j in range(4):
            if i != j:
                deriv[i, j] = weights[j] / weights[i] / (points[i] - points[j])
        deriv[i, i] = -np.sum(deriv[i])
    return deriv


def operator_parts():
    deriv, eye = lobatto_derivative(), np.eye(4)
    along = [
        np.kron(eye, np.kron(eye, deriv)),
        np.kron(eye, np.kron(deriv, eye)),
        np.kron(deriv, np.kron(eye, eye)),
    ]
    second = sum(d @ d for d in along)
    pick = np.zeros((4, 4, 4, 4))
    for i in range(4):
        for j in range(4):
            pick[i, j, i, j] = 1.0
    eye16 = np.eye(16)
    right, left = np.kron(eye16, pick[3, 3]), np.kron(eye16, pick[0, 0])
    right_from, left_from = np.kron(eye16, pick[3, 0]), np.kron(eye16, pick[0, 3])
    fixed = np.kron(np.eye(5), np.eye(64) - 0.15 * right - 0.15 * left)
    fixed = fixed + DT * VISC * np.kron(np.diag([0.0, 1.0, 1.0, 1.0, 1.0]), second)
    by_x = -DT * along[0] + 0.15 * right - 0.15 * left
    return [
        np.asarray(a, np.float32)
        for a in (
            fixed,
            by_x,
            -DT * along[1],
            -DT * along[2],
            np.kron(np.eye(5), 0.15 * right_from),
            -0.15 * right_from,
            np.kron(np.eye(5), 0.15 * left_from),
            0.15 * left_from,
        )
    ]


FIXED, BY_X, BY_Y, BY_Z, NEXT_FIXED, NEXT_X, PREV_FIXED, PREV_X = operator_parts()


def wall_tables():
    groups = []
    for fixed, tables in ((FIXED, (BY_X, BY_Y, BY_Z)), (NEXT_FIXED, (NEXT_X,)), (PREV_FIXED, (PREV_X,))):
        groups.append(fixed[256:272] - fixed[0:16])
        groups += [np.tile(t[:16], (1, 5)) for t in tables]
    return np.stack(groups).astype(np.float32)


WALL_TABLES = wall_tables()
RATE_LIST = RATES.astype(np.float32)
RATE_ROW = (1.0 + 64.0 * RATES)[None, :].astype(np.float32)
RATE_COLUMN = (64.0 * RATES)[:, None].astype(np.float32)
SURFACE_ROW = np.broadcast_to(Q[:1], (8, N)).copy()
FIELD_HOT = np.pad(np.kron(np.eye(5), np.ones((64, 1))), ((0, 0), (0, 3))).astype(ml_dtypes.bfloat16)
TILE_HOT = np.kron(np.ones((5, 1)), np.eye(64)).astype(ml_dtypes.bfloat16)
OPERATORS = np.stack([BY_X, BY_Y, BY_Z, NEXT_X, PREV_X])


def split(value):
    high = value.astype(BF16)
    return high, (value - high.astype(F32)).astype(BF16)


def dot(a, b, dims=NN):
    return lax.dot_general(a, b, (dims, ((), ())), preferred_element_type=F32)


def dot3(a, b, dims=NN):
    a = split(a) if not isinstance(a, tuple) else a
    b = split(b) if not isinstance(b, tuple) else b
    a = jnp.concatenate([a[0], a[1], a[0]], axis=dims[0][0])
    b = jnp.concatenate([b[0], b[0], b[1]], axis=dims[1][0])
    return dot(a, b, dims)


def hot_dot(hot, b, dims=NN):
    high, low = split(b)
    return dot(hot, high, dims) + dot(hot, low, dims)


def dot_hot(a, hot, dims=NN):
    high, low = split(a)
    return dot(high, hot, dims) + dot(low, hot, dims)


def hot_of(condition):
    return jnp.where(condition, 1.0, 0.0).astype(BF16)


def iota(shape, dim):
    return lax.broadcasted_iota(jnp.int32, shape, dim)


def rows(ref, first, count, stride):
    return ref[pl.ds(first, count, stride) if stride > 1 else pl.ds(first, count), :]


def sine_rows(ref, first, count, stride):
    return jnp.concatenate([rows(ref, h * N + first, count, stride) for h in range(2)], axis=1)


def x_ordered(sine_ref):
    blocks = [sine_rows(sine_ref, 2 * k + i, 64, 4) for i in range(2) for k in range(2)]
    return split(jnp.concatenate(blocks, axis=0))


def mode_ordered(sine_ref):
    return jnp.concatenate([sine_rows(sine_ref, k, HALF, 2) for k in range(2)], axis=0)


def column_of(row):
    return jnp.broadcast_to(row.astype(F32), (8, row.shape[1])).T[:, 0:1].astype(jnp.int32)


def near_kernel(
    where_ref, jac_hbm, fluid_hbm, solid_hbm, sine_hbm, table_hbm, elem_hbm, owner_hbm, patch_hbm,
    out_ref, trace_ref, surface_ref, first_ref, last_ref, matrix_ref, far_table_ref,
    jac_ref, fluid_ref, solid_ref, sine_ref, table_ref, elem_ref, owner_ref, patch_ref, sems
):
    group = where_ref[0]
    count = fluid_ref.shape[1]
    copies = [
        pltpu.make_async_copy(jac_hbm, jac_ref, sems.at[0]),
        pltpu.make_async_copy(solid_hbm, solid_ref, sems.at[1]),
        pltpu.make_async_copy(sine_hbm, sine_ref, sems.at[2]),
        pltpu.make_async_copy(table_hbm, table_ref, sems.at[3]),
        pltpu.make_async_copy(elem_hbm, elem_ref, sems.at[4]),
        pltpu.make_async_copy(owner_hbm, owner_ref, sems.at[5]),
        pltpu.make_async_copy(patch_hbm, patch_ref, sems.at[6]),
    ]
    for i in range(5):
        at = pl.ds(64 * i, 64)
        copies.append(pltpu.make_async_copy(fluid_hbm.at[at, :], fluid_ref.at[at, :], sems.at[7 + i]))
    for copy in copies:
        copy.start()
    for copy in copies[:7]:
        copy.wait()

    near, far = [
        sine_ref[pl.ds(pl.multiple_of(half * N + group * HALF, HALF), HALF), :]
        for half in (group, 1 - group)
    ]
    far_table_ref[...] = far
    near = split(near)
    for i in range(2):
        modes = dot3(near, rows(solid_ref, i, N, 2), NT)
        for h in range(2):
            out_ref[pl.ds(2 * i + h, HALF, 5), :] = modes[:, h * HALF : (h + 1) * HALF]
    surface_ref[...] = solid_ref[0:2]

    field = iota((1, 320), 1) // 64
    coefficients = []
    for d in range(3):
        change = jac_ref[d, 4:5, :] - jac_ref[d, 0:1, :]
        row = jnp.zeros((1, 320), F32)
        for f in range(5):
            row = jnp.where(field == f, change[:, f : f + 1], row)
        coefficients.append(row)
    own = table_ref[0]
    for d in range(3):
        own = own + coefficients[d] * table_ref[1 + d]
    matrix_ref[0:16] = own
    matrix_ref[16:32] = table_ref[4] + coefficients[0] * table_ref[5]
    matrix_ref[32:48] = table_ref[6] + coefficients[0] * table_ref[7]

    owner, patch, elem = owner_ref[...], patch_ref[...], elem_ref[...]
    square = (HALF, HALF)
    same = (column_of(owner) == owner) & (iota(square, 0) < iota(square, 1))
    place = jnp.sum(jnp.where(same, 1.0, 0.0), axis=0, keepdims=True)
    elem_hot = hot_of(column_of(elem) == iota((HALF, count), 1))

    for copy in copies[7:]:
        copy.wait()
    lane = iota((1, 384), 1)
    gap = jnp.zeros((1, 64), F32)
    for block, at, out, element in (
        (fluid_ref[:, 0:HALF], (0, 1), first_ref, 0),
        (fluid_ref[:, count - HALF : count], (HALF - 1, HALF - 2), last_ref, count - 1),
    ):
        turned = block.T
        met = elem == element
        edge_owner = jnp.sum(jnp.where(met, owner + 1, 0).astype(F32), axis=1, keepdims=True)
        edge_patch = jnp.sum(jnp.where(met, patch, 0).astype(F32), axis=1, keepdims=True)
        out[0:1] = jnp.concatenate([turned[at[0] : at[0] + 1], gap], axis=1)
        out[1:2] = jnp.concatenate([turned[at[1] : at[1] + 1], gap], axis=1)
        out[2:3] = jnp.where(lane == 0, edge_owner, jnp.where(lane == 1, edge_patch, 0.0))
        out[3:8] = jnp.zeros((5, 384), F32)

    walls = dot3(matrix_ref[...], fluid_ref[...])
    wall0 = fluid_ref[256:272] - fluid_ref[0:16]
    lane = iota(wall0.shape, 1)
    following = pltpu.roll(walls[16:32], count - 1, 1)
    preceding = pltpu.roll(walls[32:48], 1, 1)
    later = walls[0:16] + jnp.where(lane == count - 1, 0.0, following)
    later = later + jnp.where(lane == 0, 0.0, preceding)
    values = dot_hot(jnp.concatenate([wall0, later - GAIN * wall0], axis=0), elem_hot, NT)
    trace_ref[...] = values[:16]
    ids = jnp.broadcast_to((patch + 1).astype(F32), (8, HALF))
    filler = jnp.zeros((24, HALF), F32)
    sent = jnp.concatenate([values, ids, filler], axis=0)
    none = jnp.zeros((64, HALF), F32)
    arranged = 0.0
    for i in range(2):
        hot = hot_of((iota(square, 0) == owner) & (place == float(i)))
        padded = jnp.concatenate([sent, none] if i == 0 else [none, sent], axis=0)
        arranged = arranged + hot_dot(hot, padded, NT)
    out_ref[pl.ds(4, HALF, 5), :] = arranged


def send_out(pairs, sems):
    copies = [pltpu.make_async_copy(a, b, sems.at[i]) for i, (a, b) in enumerate(pairs)]
    for copy in copies:
        copy.start()
    return copies


def far_kernel(far_ref, table_ref, near_ref, out_hbm, out_ref, sems):
    table = split(table_ref[...])
    out_ref[pl.ds(4, HALF, 5), :] = rows(near_ref, 4, HALF, 5)
    for i in range(2):
        modes = dot3(table, rows(far_ref, i, N, 2), NT)
        for h in range(2):
            part = modes[:, h * HALF : (h + 1) * HALF]
            out_ref[pl.ds(2 * i + h, HALF, 5), :] = rows(near_ref, 2 * i + h, HALF, 5) + part
    pieces = [pl.ds(160 * i, 160) for i in range(4)]
    for copy in send_out([(out_ref.at[at, :], out_hbm.at[at, :]) for at in pieces], sems):
        copy.wait()


def tables_kernel(
    where_ref, rate_ref, sine_ref, rate_row_ref, rate_col_ref, order_ref,
    sine_out, x_out, modes_out, modes_t_out, split_out, decay_out
):
    del order_ref
    by_modes = mode_ordered(sine_ref)
    for out, table in (
        (sine_out, split(sine_rows(sine_ref, 0, N, 1))),
        (x_out, x_ordered(sine_ref)),
        (modes_out, split(by_modes)),
        (modes_t_out, split(by_modes.T)),
    ):
        out[0], out[1] = table
    columns = [sine_rows(sine_ref, i, HALF, 2) for i in range(2)]
    split_out[0], split_out[1] = split(jnp.concatenate(columns, axis=0))
    decay_out[...] = 1.0 / (rate_col_ref[...] + (rate_row_ref[...] + 64.0 * rate_ref[where_ref[2]]))


def matrices_kernel(jac_ref, field_ref, tile_ref, fixed_ref, operators_ref, out_ref):
    field, tile = field_ref[...], tile_ref[...]

    def spread(d):
        return dot_hot(hot_dot(field, jac_ref[d]), field, NT)

    def tiled(d):
        return dot_hot(hot_dot(tile, operators_ref[d]), tile, NT)

    by_x = spread(0)
    own = by_x * tiled(0) + spread(1) * tiled(1) + spread(2) * tiled(2)
    out_ref[0:320] = fixed_ref[0] + own
    out_ref[320:640] = fixed_ref[1] + by_x * tiled(3)
    out_ref[640:960] = fixed_ref[2] + by_x * tiled(4)


def modes_kernel(
    where_ref, got_ref, surface_ref, sine_ref, split_ref, by_modes_ref, decay_ref, row_ref,
    matrix_ref, before_ref, after_ref, elem_ref, owner_ref, patch_ref, modes_ref, out_ref, *, count
):
    group = where_ref[0]
    sine = sine_ref[0], sine_ref[1]
    parts = [
        jnp.concatenate([rows(got_ref, 2 * i + h, HALF, 5) for h in range(2)], axis=1)
        for i in range(2)
    ]
    by_z = dot3(sine, jnp.concatenate(parts, axis=0), NT)
    modes = dot3(by_z, (split_ref[0], split_ref[1]))
    modes_ref[...] = modes
    surface_row = dot3(row_ref[...], decay_ref[...] * modes)[0:1]

    fluid = rows(got_ref, 4, HALF, 5)
    square = (HALF, HALF)
    lane = iota(square, 1)
    fluid_pair = split(fluid)
    sums = [[0.0, 0.0], [0.0, 0.0]]
    counts = [0.0, 0.0]
    count_lanes = 0.0
    for i in range(2):
        ids = fluid[:, i * 64 + 32 : i * 64 + 33].astype(jnp.int32) - 1
        count_lanes = count_lanes + jnp.sum(jnp.where(ids == lane, 1.0, 0.0), axis=0, keepdims=True)
        for f in range(2):
            pick = hot_of(iota(square, 0) == i * 64 + f * 16 + lane % 16)
            values = dot(fluid_pair[0], pick) + dot(fluid_pair[1], pick)
            for xl in range(2):
                mask = ids == xl * 8 + lane // 16
                sums[f][xl] = sums[f][xl] + jnp.sum(
                    jnp.where(mask, values, 0.0), axis=0, keepdims=True
                )
                if f == 0:
                    counts[xl] = counts[xl] + jnp.sum(
                        jnp.where(mask, 1.0, 0.0), axis=0, keepdims=True
                    )
    heat = [sums[0][xl] - counts[xl] * surface_ref[xl : xl + 1, :] for xl in range(2)]
    tail = jnp.where(lane < 16, count_lanes, 0.0)
    edge_rows = []
    for t, (part, ref, element) in enumerate(((2, before_ref, 0), (1, after_ref, count - 1))):
        met = elem_ref[...] == element
        owner, patch = [
            jnp.sum(jnp.where(met, value, 0).astype(F32), axis=1, keepdims=True).astype(jnp.int32)
            for value in (owner_ref[...] + 1, patch_ref[...])
        ]
        x_of_slot = patch // 8 * HALF + (owner - 1) % 2 * 64 + (owner - 1) // 2
        tail = jnp.where(lane == 40 + t, jnp.where(owner > 0, x_of_slot + 1, 0).astype(F32), tail)
        tables = matrix_ref[16 * part : 16 * part + 16]
        column = jnp.sum(tables * ref[0:1, 0:320], axis=1, keepdims=True)
        node, lane16 = iota((16, HALF), 0), iota((16, HALF), 1)
        used = (lane16 % 16 == node) & (lane16 // 16 == patch % 8)
        edge_rows.append(jnp.sum(jnp.where(used, column, 0.0), axis=0, keepdims=True))
    for k in range(2):
        by_modes = []
        for part in range(2):
            table = by_modes_ref[part, k * HALF : (k + 1) * HALF, :].astype(F32)
            own = jnp.where(group == 0, table[:, :HALF], table[:, HALF:])
            by_modes.append(own.astype(BF16))
        by_modes = tuple(by_modes)
        for xl in range(2):
            column = dot3(by_modes, jnp.broadcast_to(sums[1][xl], (8, HALF)), NT)[:, 0:1]
            tail = jnp.where(lane == 16 + 2 * k + xl, column, tail)
        for t in range(2):
            column = dot3(by_modes, jnp.broadcast_to(edge_rows[t], (8, HALF)), NT)[:, 0:1]
            tail = jnp.where(lane == 32 + 2 * t + k, column, tail)
    shared = [surface_row[:, :HALF], surface_row[:, HALF:], heat[0], heat[1]]
    for r in range(4):
        out_ref[pl.ds(r, HALF, 5), :] = jnp.broadcast_to(shared[r], square)
    out_ref[pl.ds(4, HALF, 5), :] = tail


def solve_kernel(
    where_ref, got_ref, other_ref, modes_ref, response_ref, sine_ref, pair_ref, x_ref, by_modes_ref,
    from_modes_ref, split_ref, decay_ref, row_ref,
    surface_hbm, out_hbm, heat_ref, surface_ref, out_ref, sem, sems
):
    core, me = where_ref[1], where_ref[2]
    first = jnp.full((HALF, HALF), core, jnp.int32) == 0
    ordered = []
    for r in range(5):
        mine, theirs = rows(got_ref, r, HALF, 5), rows(other_ref, r, HALF, 5)
        ordered.append((jnp.where(first, mine, theirs), jnp.where(first, theirs, mine)))

    def block(g, r):
        return jnp.concatenate([ordered[r][k][g * 64 : (g + 1) * 64] for k in range(2)], axis=0)

    by_x = x_ref[0], x_ref[1]
    heat = jnp.concatenate(
        [jnp.concatenate([block(g, 2 + xl) for g in range(2)], axis=1) for xl in range(2)], axis=0
    )
    heat_modes = dot3(dot3((by_modes_ref[0], by_modes_ref[1]), heat, NT), by_x)
    heat_ref[...] = heat_modes
    given = jnp.concatenate(
        [jnp.concatenate([ordered[h][k] for h in range(2)], axis=1) for k in range(2)], axis=0
    )
    surface = dot3((from_modes_ref[0], from_modes_ref[1]), given + response_ref[...] * heat_modes)
    surface = dot3(surface, by_x, NT)
    surface_ref[...] = surface
    copy = pltpu.make_async_copy(surface_ref, surface_hbm.at[pl.ds(0, N), :], sem)
    copy.start()
    square = (HALF, HALF)
    tails = [block(g, 4) for g in range(2)]
    tail_pairs = [tail.astype(BF16) for tail in tails]
    expand = [hot_of(iota(square, 1) == xl * 8 + iota(square, 0) // 16) for xl in range(2)]
    count = jnp.concatenate(
        [
            jnp.concatenate([dot(expand[xl], tail_pairs[g], NT) for xl in range(2)], axis=1)
            for g in range(2)
        ],
        axis=0,
    )
    own_sine = jnp.broadcast_to(sine_rows(sine_ref, me, 1, 1), (8, N))
    reduced = dot3(own_sine, count * surface)
    tail_sum = tails[0] + tails[1]
    lane8 = iota((8, HALF), 1)
    later = jnp.concatenate(
        [hot_dot(hot_of(lane8 == 16 + 2 * core + xl), tail_sum, NT) for xl in range(2)], axis=1
    )
    wide = iota((HALF, N), 1)
    for k in range(2):
        tail = ordered[4][k]
        for t in range(2):
            value = jnp.where(first[:, 0:1], tail[:, 32 + 2 * t : 33 + 2 * t], tail[:, 33 + 2 * t : 34 + 2 * t])
            met = tail[:, 40 + t : 41 + t].astype(jnp.int32) - 1 == wide
            later = later + jnp.sum(jnp.where(met, value, 0.0), axis=0, keepdims=True)
    heat1 = dot3(later - 0.7 * reduced, by_x)[0:1]
    heat0 = heat_ref[pl.ds(core * HALF + me // 2, 1), :]
    decay = decay_ref[...]
    column = sine_ref[pl.ds(0, N), 0:1]
    final = decay * (decay * (modes_ref[...] + column * heat0) + column * heat1)
    final_row = dot3(row_ref[...], final)[0:1]
    final = split(final)
    sine = pair_ref[0], pair_ref[1]
    back = dot3(dot3((split_ref[0], split_ref[1]), final, NT), sine)
    for xl in range(2):
        for h in range(2):
            part = back[xl * HALF : (xl + 1) * HALF, h * HALF : (h + 1) * HALF]
            out_ref[pl.ds(2 * xl + h, HALF, 5), :] = part
    for k in range(2):
        out_ref[pl.ds(4 + 5 * k, 64, 10), :] = jnp.broadcast_to(
            final_row[:, k * HALF : (k + 1) * HALF], (64, HALF)
        )
    pieces = [(160 * i, 640 * g + 160 * i) for i in range(4) for g in range(2)]
    for sending in send_out(
        [(out_ref.at[pl.ds(a, 160), :], out_hbm.at[pl.ds(b, 160), :]) for a, b in pieces], sems
    ):
        sending.wait()
    copy.wait()


def met_values(surface, owner, patch):
    x_of_slot = patch // 8 * HALF + owner % 2 * 64 + owner // 2
    x_hot = hot_of(iota((N, HALF), 0) == x_of_slot)
    met = dot_hot(surface, x_hot)
    return jnp.where(iota((HALF, HALF), 0) // 16 == patch % 8, met, 0.0)


def folded(met):
    fold = hot_of(iota((16, HALF), 0) == iota((16, HALF), 1) % 16)
    return hot_dot(fold, met)


def stepped(extended, matrix_ref):
    fluid = split(extended)
    width = extended.shape[1]
    own, following, preceding = [
        dot3(matrix_ref[pl.ds(320 * i, 320), :], fluid) for i in range(3)
    ]
    return own + pltpu.roll(following, width - 1, 1) + pltpu.roll(preceding, 1, 1)


def step_kernel(where_ref, fluid_ref, matrix_ref, before_ref, after_ref, out_ref):
    count = fluid_ref.shape[1]
    me = where_ref[2]
    lane = iota((320, HALF), 1)
    following, preceding = after_ref[...].T[0:320], before_ref[...].T[0:320]
    halo = jnp.zeros((320, HALF), F32)
    for at, column in (
        (0, following[:, 0:1]),
        (1, following[:, 1:2]),
        (HALF - 1, preceding[:, 0:1]),
        (HALF - 2, preceding[:, 1:2]),
    ):
        halo = jnp.where(lane == at, column, halo)
    result = stepped(jnp.concatenate([fluid_ref[...], halo], axis=1), matrix_ref)
    edge = result[:, count:]
    beyond = ((lane == 0) & (me == 255)) | ((lane == HALF - 1) & (me == 0))
    out_ref[:, :count] = result[:, :count]
    out_ref[:, count:] = jnp.where(beyond, 0.0, edge)


def second_kernel(
    where_ref, surface_hbm, fluid_ref, trace_ref, matrix_ref, before_ref, after_ref, elem_ref,
    owner_ref, patch_ref, sine_ref, out_ref, later_ref, slots_ref, walls_ref, surface_ref, sem
):
    copy = pltpu.make_async_copy(surface_hbm.at[pl.ds(0, N), :], surface_ref, sem)
    copy.start()
    copy.wait()
    group, me = where_ref[0], where_ref[2]
    width = fluid_ref.shape[1]
    count = width - HALF
    own_surface = surface_ref[pl.ds(pl.multiple_of(group * HALF, HALF), HALF), :]
    elem_hot = hot_of(column_of(elem_ref[...]) == iota((HALF, count), 1))
    met = folded(met_values(own_surface, owner_ref[...], patch_ref[...]))
    source = GAIN * dot_hot(met - trace_ref[...], elem_hot)
    square = (16, HALF)
    edge = jnp.zeros(square, F32)
    for ref, at, device in ((after_ref, 0, me + 1), (before_ref, HALF - 1, me - 1)):
        owner = ref[2:3, 0:1].astype(jnp.int32) - 1
        patch = ref[2:3, 1:2].astype(jnp.int32)
        side = jnp.clip(device, 0, 255) // HALF
        near = surface_ref[pl.ds(pl.multiple_of(side * HALF, HALF), HALF), :]
        lanes = jnp.zeros((1, HALF), jnp.int32)
        value = folded(met_values(near, owner + lanes, patch + lanes))
        column = ref[...].T
        value = GAIN * (value - (column[256:272, 0:1] - column[0:16, 0:1]))
        used = (iota(square, 1) == at) & (owner >= 0)
        edge = jnp.where(used, value, edge)
    slot_hot = hot_of(iota((N, HALF), 0) == 2 * owner_ref[...] + patch_ref[...] // 8)
    slots_ref[...] = dot_hot(sine_rows(sine_ref, 0, N, 1), slot_hot)
    walls = fluid_ref[256:272] + jnp.concatenate([source, edge], axis=1)
    later_ref[...] = dot_hot(walls[:, :count] - fluid_ref[0:16, :count], elem_hot, NT)
    extended = jnp.concatenate([fluid_ref[0:256], walls, fluid_ref[272:320]], axis=0)
    result = stepped(extended, matrix_ref)[:, :count]
    out_ref[...] = result
    walls_ref[...] = result[256:272]


def solid_kernel(where_ref, got_ref, sine_ref, solid_ref):
    by_y = split(sine_ref[pl.ds(pl.multiple_of(where_ref[0] * N, N), N), :])
    parts = jnp.concatenate([rows(got_ref, i, N, 5) for i in range(4)], axis=1)
    solid = dot3(parts, by_y, TN)
    for xl in range(2):
        for h in range(2):
            at = (2 * xl + h) * HALF
            solid_ref[pl.ds(h * N + xl, HALF, 2), :] = solid[at : at + HALF]


def last_kernel(
    where_ref, solid_ref, mine_ref, other_ref, sine_ref, slots_ref, later_ref, elem_ref, patch_ref,
    walls_ref, fluid_hbm, out_hbm, solid_hbm, out_ref, sem, solid_sems
):
    group, core = where_ref[0], where_ref[1]
    pieces = [pl.ds(HALF * i, HALF) for i in range(4)]
    solid = send_out([(solid_ref.at[at, :], solid_hbm.at[at, :]) for at in pieces], solid_sems)
    first = jnp.full((N, HALF), core, jnp.int32) == 0
    mine, other = mine_ref[...], other_ref[...]
    given = jnp.concatenate([jnp.where(first, mine, other), jnp.where(first, other, mine)], axis=1)
    own_rows = sine_rows(sine_ref, pl.multiple_of(group * HALF, HALF), HALF, 1)
    met = dot3(own_rows, dot3(given, slots_ref[...]))
    met = folded(jnp.where(iota((HALF, HALF), 0) // 16 == patch_ref[...] % 8, met, 0.0))
    elem_hot = hot_of(column_of(elem_ref[...]) == iota((HALF, walls_ref.shape[1]), 1))
    out_ref[...] = walls_ref[...] + GAIN * dot_hot(met - later_ref[...], elem_hot)
    copy = pltpu.make_async_copy(out_ref, out_hbm.at[pl.ds(256, 16), :], sem)
    copy.start()
    for sending in solid:
        sending.wait()
    copy.wait()


def call(kernel, outs, args, scalars=0, scratch=(), aliases=None, specs=None, out_specs=None, cost=None, limit=40):
    whole = pl.BlockSpec(memory_space=pltpu.VMEM)
    given = [pl.BlockSpec(memory_space=pltpu.SMEM)] * scalars + [whole] * (len(args) - scalars)
    return pl.pallas_call(
        kernel,
        out_shape=[
            jax.ShapeDtypeStruct(*(out if isinstance(out[0], tuple) else (out, F32))) for out in outs
        ],
        in_specs=specs or given,
        out_specs=out_specs or [whole] * len(outs),
        scratch_shapes=list(scratch),
        input_output_aliases=aliases or {},
        cost_estimate=pl.CostEstimate(flops=int(cost or 1e8), bytes_accessed=1 << 20, transcendentals=0),
        compiler_params=pltpu.CompilerParams(vmem_limit_bytes=limit << 20),
    )(*args)


def exchange(payload, axes):
    chunks = payload.reshape(payload.shape[0], 1, HALF)
    return lax.all_to_all(chunks, axes, split_axis=0, concat_axis=0, tiled=True).reshape(payload.shape)


def on_device(fluid_state, flux_jacobian, solid_temp, iface_elem, iface_owner, iface_patch):
    me = lax.axis_index(ALL)
    where = jnp.stack([me // HALF, me % 2, me]).astype(jnp.int32)
    fluid0 = fluid_state.reshape(320, -1)
    count = fluid0.shape[1]
    solid = solid_temp.reshape(2 * N, HALF)
    elem, owner, patch = iface_elem[None, :], iface_owner.reshape(1, HALF), iface_patch[None, :]
    smem = pl.BlockSpec(memory_space=pltpu.SMEM)
    vmem = pl.BlockSpec(memory_space=pltpu.VMEM)
    hbm = pl.BlockSpec(memory_space=pltpu.HBM)

    far = lax.ppermute(solid, "g", [(0, 1), (1, 0)])
    near, trace0, surface0, first, last, wall_matrix, far_table = call(
        near_kernel,
        [(5 * HALF, HALF), (16, HALF), (2, HALF), (8, 384), (8, 384), (48, 320), (HALF, HALF)],
        [where, flux_jacobian, fluid0, solid, Q_HALVES, WALL_TABLES, elem, owner, patch],
        specs=[smem] + [hbm] * 8,
        limit=52,
        scratch=[
            pltpu.VMEM(flux_jacobian.shape, F32),
            pltpu.VMEM(fluid0.shape, F32),
            pltpu.VMEM(solid.shape, F32),
            pltpu.VMEM(Q_HALVES.shape, F32),
            pltpu.VMEM(WALL_TABLES.shape, F32),
            pltpu.VMEM((1, HALF), jnp.int32),
            pltpu.VMEM((1, HALF), jnp.int32),
            pltpu.VMEM((1, HALF), jnp.int32),
            pltpu.SemaphoreType.DMA((12,)),
        ],
    )
    before = lax.ppermute(last, ALL, [(i, i + 1) for i in range(255)])
    after = lax.ppermute(first, ALL, [(i + 1, i) for i in range(255)])
    (pay1,) = call(
        far_kernel,
        [(5 * HALF, HALF)],
        [far, far_table, near],
        out_specs=[hbm],
        scratch=[pltpu.VMEM((5 * HALF, HALF), F32), pltpu.SemaphoreType.DMA((4,))],
    )
    got1 = exchange(pay1, SUB)
    tables = call(
        tables_kernel,
        [((2, N, N), BF16)] * 4
        + [((2, N, N), BF16), (N, N)],
        [where, RATE_LIST, Q_HALVES, RATE_ROW, RATE_COLUMN, surface0],
        scalars=2,
    )
    sine_pair, x_pair, modes_pair, modes_t_pair, split_pair, decay = tables
    jacobian = jnp.pad(flux_jacobian, ((0, 0), (0, 3), (0, 3)))
    (matrix,) = call(
        matrices_kernel,
        [(960, 320)],
        [jacobian, FIELD_HOT, TILE_HOT, np.stack([FIXED, NEXT_FIXED, PREV_FIXED]), OPERATORS],
    )
    (fluid1,) = call(
        step_kernel,
        [(320, count + HALF)],
        [where, fluid0, matrix, before, after],
        scalars=1,
        cost=2e9,
    )
    modes, pay2 = call(
        functools.partial(modes_kernel, count=count),
        [(N, N), (5 * HALF, HALF)],
        [where, got1, surface0, sine_pair, split_pair, modes_pair, decay, SURFACE_ROW,
         wall_matrix, before, after, elem, owner, patch],
        scalars=1,
    )
    got2 = exchange(pay2, SAME_CORE)
    other = lax.ppermute(got2, "c", [(0, 1), (1, 0)])
    surface1, pay3 = call(
        solve_kernel,
        [(SURFACE_ROWS, N), (5 * N, HALF)],
        [where, got2, other, modes, RESPONSE, Q_HALVES, sine_pair, x_pair, modes_pair, modes_t_pair,
         split_pair, decay, SURFACE_ROW],
        scalars=1,
        out_specs=[hbm, hbm],
        scratch=[
            pltpu.VMEM((N, N), F32),
            pltpu.VMEM((N, N), F32),
            pltpu.VMEM((5 * HALF, HALF), F32),
            pltpu.SemaphoreType.DMA,
            pltpu.SemaphoreType.DMA((8,)),
        ],
    )
    got3 = exchange(pay3, ALL)
    fluid2, trace1, slots, walls2 = call(
        second_kernel,
        [(320, count), (16, HALF), (N, HALF), (16, count)],
        [where, surface1, fluid1, trace0, matrix, before, after, elem, owner, patch, Q_HALVES],
        specs=[smem, hbm] + [vmem] * 9,
        scratch=[pltpu.VMEM((N, N), F32), pltpu.SemaphoreType.DMA],
        cost=2e9,
    )
    got3, fluid2, trace1, slots, walls2 = lax.optimization_barrier(
        (got3, fluid2, trace1, slots, walls2)
    )
    mine = got3.reshape(N, 5, 1, HALF)[:, 4].reshape(N, HALF)
    far_row = lax.ppermute(mine, "c", [(0, 1), (1, 0)])
    (solid_new,) = call(solid_kernel, [(2 * N, HALF)], [where, got3, Q_HALVES], scalars=1)
    fluid2, solid_out = call(
        last_kernel,
        [(320, count), (2 * N, HALF)],
        [where, solid_new, mine, far_row, Q_HALVES, slots, trace1, elem, patch, walls2, fluid2],
        specs=[smem] + [vmem] * 9 + [hbm],
        out_specs=[hbm] * 2,
        aliases={10: 0},
        scratch=[
            pltpu.VMEM((16, count), F32),
            pltpu.SemaphoreType.DMA,
            pltpu.SemaphoreType.DMA((4,)),
        ],
    )
    return fluid2.reshape(fluid_state.shape), solid_out.reshape(solid_temp.shape)


def solution(mesh):
    fine = Mesh(mesh.devices.reshape(2, 2, 4, 8, 2), ALL)
    placed = (
        P(None, None, ALL),
        P(),
        P(None, SUB, "g"),
        P(ALL),
        P(ALL, None),
        P(ALL),
    )
    return jax.shard_map(
        on_device,
        mesh=fine,
        in_specs=placed,
        out_specs=(P(None, None, ALL), P(None, SUB, "g")),
        check_vma=False,
    )
```
